32 devices in a mesh: seq: 16 (over z, x, core), head: 2 (over y).
Axes of the slice: x: 2, y: 2, z: 4, core: 2. Of those that a mesh axis runs over, the one named last changes fastest.
Arguments:
- queries: bfloat16 [3072, 4096], P('seq', 'head'), may hold values from -12.5 to 12.5
- keys: bfloat16 [3072, 1024], P('seq', 'head'), may hold values from -10.5 to 10.5
- values: bfloat16 [3072, 1024], P('seq', 'head'), may hold values from -6 to 6
- d_out: bfloat16 [3072, 4096], P('seq', 'head'), may hold values from -6 to 6
- w_out: bfloat16 [4096, 4096], P('head'), may hold values from -0.09375 to 0.09375
- doc_starts: int32 [4], replicated, may hold values from 0 to 3056, as said below
Outputs:
- query_grad: bfloat16 [3072, 4096], P('seq', 'head')
- key_grad: bfloat16 [3072, 1024], P('seq', 'head')
- value_grad: bfloat16 [3072, 1024], P('seq', 'head')
The draws below stay inside these ranges and needn't reach their ends.
Inputs may be any that keep to these rules, and one draw needn't show every extreme that they name: doc_starts[0] is 0, the entries rise strictly, every entry is a multiple of 16, and the last entry is 3056, so the last document has 16 positions; a document runs from its start to the next start or to the end of the sequence.
All inputs are finite; a program needn't handle non-finite values.
Results may differ from the reference program's by a relative error of at most 0.0163.
Values may be sent and summed in bfloat16 or wider, within the bound.
No kernel may reach another device: no remote copies, remote signals or barrier semaphores. Data moves between devices by JAX's collectives and lax.ppermute only.
A program may use at most 192 MiB of HBM per device.

```python
import math
import jax
import jax.numpy as jnp
from jax import lax

D = 4096
QH = 32
KVH = 8
DH = 128
NDOC = 4
TOKENS = 3072


def row_scales(key, row_count):
    return jnp.exp(jax.random.uniform(key, (row_count, 1), jnp.float32, math.log(0.4), math.log(2.5)))


def base_block(key, shape):
    return jnp.clip(jax.random.normal(key, shape, jnp.float32), -4.0, 4.0)


def draw_queries(key, part):
    base = base_block(jax.random.fold_in(key, 11), (TOKENS, QH * DH)) * row_scales(jax.random.fold_in(key, 12), TOKENS)
    return base.astype(jnp.bfloat16)


def draw_keys(key, part):
    base = base_block(jax.random.fold_in(key, 21), (TOKENS, KVH * DH)) * row_scales(jax.random.fold_in(key, 22), TOKENS)
    return base.astype(jnp.bfloat16)


def draw_doc_starts(key, part):
    slot_count = TOKENS // 16
    shuffled = jax.random.permutation(jax.random.fold_in(key, 41), slot_count - 2) + 1
    cut_points = jnp.sort(shuffled[:NDOC - 2]) * 16
    final_start = jnp.full((1,), (slot_count - 1) * 16, jnp.int32)
    return jnp.concatenate([jnp.zeros((1,), jnp.int32), cut_points.astype(jnp.int32), final_start])


def level_of(stream_key, shape, shards, low, high):
    def one(position, blocks):
        steps = jax.random.uniform(jax.random.fold_in(jax.random.fold_in(stream_key, 6), position), (blocks,), jnp.float32, low / len(shards), high / len(shards))
        return jnp.repeat(jnp.exp(steps), shape[position] // blocks).reshape((-1,) + (1,) * (len(shape) - position - 1))

    level = one(*shards[0])
    for cut in shards[1:]:
        level = level * one(*cut)
    return level


def centred(stream_key, dims, scale, bound, pieces=(), kind=jnp.bfloat16):
    values = jax.random.normal(stream_key, dims, jnp.float32) * scale
    if len(pieces) > 0:
        values = level_of(stream_key, dims, pieces, -0.22, 0.18) * values
    return jnp.clip(values, min=-bound, max=bound).astype(kind)


def setup_inputs(seed: int = 0) -> dict:
    key_of = jax.random.split(jax.random.key(seed), 7)
    return {
        "queries": draw_queries(jax.random.fold_in(key_of[6], 71), 0),
        "keys": draw_keys(jax.random.fold_in(key_of[6], 71), 0),
        "values": centred(key_of[2], (TOKENS, KVH * DH), 1.0, 6.0, ((0, 16), (1, 2))),
        "d_out": centred(key_of[3], (TOKENS, D), 1.0, 6.0, ((0, 16), (1, 2))),
        "w_out": centred(key_of[4], (QH * DH, D), D ** -0.5, 0.09375, ((0, 2),)),
        "doc_starts": draw_doc_starts(jax.random.fold_in(key_of[6], 71), 0),
    }


NEG_FILL = -1e+30

def doc_index(doc_starts, places):
    return lax.optimization_barrier(jnp.sum((places[:, None] >= doc_starts[None, :]).astype(jnp.int32), axis=1))

def rounded(values_in):
    return lax.optimization_barrier(values_in.astype(jnp.bfloat16)).astype(jnp.float32)

def reference(queries, keys, values, d_out, w_out, doc_starts):
    seq_length = queries.shape[0]
    per_group = QH // KVH
    scaling = 1.0 / math.sqrt(DH)
    attn_grad = lax.dot_general(d_out, w_out, (((1,), (1,)), ((), ())), preferred_element_type=jnp.float32).astype(jnp.bfloat16)
    places = jnp.arange(seq_length, dtype=jnp.int32)
    doc_of = doc_index(doc_starts, places)
    block_rows = math.gcd(seq_length, 512)
    query_parts = []
    key_parts = []
    value_parts = []
    for group_id in range(KVH):
        key_one = keys[:, group_id * DH:(group_id + 1) * DH].astype(jnp.float32)
        value_one = values[:, group_id * DH:(group_id + 1) * DH].astype(jnp.float32)
        first_col = group_id * per_group * DH
        last_col = (group_id + 1) * per_group * DH
        query_grp = queries[:, first_col:last_col].astype(jnp.float32).reshape(seq_length, per_group, DH)
        grad_grp = attn_grad[:, first_col:last_col].astype(jnp.float32).reshape(seq_length, per_group, DH)

        def one_block(carried, block_no):
            key_acc, value_acc = carried
            offset = block_no * block_rows
            row_ids = offset + jnp.arange(block_rows, dtype=jnp.int32)
            q_blk = lax.dynamic_slice_in_dim(query_grp, offset, block_rows, 0)
            g_blk = lax.dynamic_slice_in_dim(grad_grp, offset, block_rows, 0)
            row_docs = lax.dynamic_slice_in_dim(doc_of, offset, block_rows, 0)
            allowed = ((places[None, :] <= row_ids[:, None]) & (doc_of[None, :] == row_docs[:, None]))[None]
            scores = jnp.einsum('shd,kd->hsk', q_blk, key_one) * scaling
            masked = jnp.where(allowed, scores, NEG_FILL)
            highest = lax.optimization_barrier(jnp.max(masked, axis=-1, keepdims=True))
            summed = lax.optimization_barrier(jnp.sum(jnp.where(allowed, jnp.exp(masked - highest), 0.0), axis=-1, keepdims=True))
            log_total = highest + jnp.log(summed)
            prob_full = jnp.where(allowed, jnp.exp(scores - log_total), 0.0)
            grad_dots = jnp.einsum('shd,kd->hsk', g_blk, value_one)
            row_delta = lax.optimization_barrier(jnp.sum(prob_full * grad_dots, axis=-1, keepdims=True))
            dscores = rounded(prob_full * (grad_dots - row_delta) * scaling)
            prob_half = rounded(prob_full)
            query_out = jnp.einsum('hsk,kd->shd', dscores, key_one)
            key_acc = key_acc + jnp.einsum('hsk,shd->kd', dscores, q_blk)
            value_acc = value_acc + jnp.einsum('hsk,shd->kd', prob_half, g_blk)
            return ((key_acc, value_acc), query_out)
        empty_acc = jnp.zeros((seq_length, DH), jnp.float32)
        finals, query_out = lax.scan(one_block, (empty_acc, empty_acc), jnp.arange(seq_length // block_rows, dtype=jnp.int32))
        query_parts.append(query_out.reshape(seq_length, per_group * DH))
        key_parts.append(finals[0])
        value_parts.append(finals[1])
    query_grad = jnp.concatenate(query_parts, axis=1).astype(jnp.bfloat16)
    key_grad = jnp.concatenate(key_parts, axis=1).astype(jnp.bfloat16)
    value_grad = jnp.concatenate(value_parts, axis=1).astype(jnp.bfloat16)
    return (query_grad, key_grad, value_grad)
```

```python
import functools
import math

import jax
import jax.numpy as jnp
from jax import lax
from jax.experimental import pallas as pl
from jax.experimental.pallas import tpu as pltpu
from jax.sharding import PartitionSpec as P

DH = 128
LOG2E = 1.4426950408889634
NEG = -1e30
VMEM_LIMIT = 56 * 1024 * 1024

NT = (((1,), (1,)), ((), ()))
NN = (((1,), (0,)), ((), ()))


def dot(a, b, dims):
    return lax.dot_general(a, b, dims, preferred_element_type=jnp.float32)


def params():
    return pltpu.CompilerParams(vmem_limit_bytes=VMEM_LIMIT)


def whole(memory_space=pltpu.VMEM):
    return pl.BlockSpec(memory_space=memory_space)


def cost(flops, nbytes, exps=0):
    return pl.CostEstimate(flops=int(flops), bytes_accessed=int(nbytes), transcendentals=int(exps))


def row_starts(scal, docs, pos):
    low = jnp.zeros_like(pos)
    for n in range(docs):
        low = jnp.where(pos >= scal[2 + n], scal[2 + n], low)
    return low


def doc_start_at(scal, docs, pos):
    low = jnp.int32(0)
    for n in range(docs):
        low = jnp.where(pos >= scal[2 + n], scal[2 + n], low)
    return low


def tile_bias(scal, docs, q0, k0, tile):
    qpos = q0 + lax.broadcasted_iota(jnp.int32, (1, tile), 1)
    kpos = k0 + lax.broadcasted_iota(jnp.int32, (tile, 1), 0)
    low = row_starts(scal, docs, qpos)
    return jnp.where((kpos <= qpos) & (kpos >= low), 0.0, NEG).astype(jnp.float32)


def needed(scal, docs, q0, k0, tile):
    return (k0 <= q0 + tile - 1) & (k0 + tile - 1 >= doc_start_at(scal, docs, q0))


def stats_kernel(docs, tile, heads, first, scal, q_ref, kv_ref, *refs):
    if first:
        m_ref, l_ref, o_ref, vt_ref = refs
        m_ref[...] = jnp.full_like(m_ref, NEG)
        l_ref[...] = jnp.zeros_like(l_ref)
        o_ref[...] = jnp.zeros_like(o_ref)
    else:
        m_in, l_in, o_in, m_ref, l_ref, o_ref, vt_ref = refs
        m_ref[...] = m_in[...]
        l_ref[...] = l_in[...]
        o_ref[...] = o_in[...]
    chunk = q_ref.shape[0]
    tiles = chunk // tile
    factor = LOG2E / math.sqrt(DH)
    vt_ref[...] = kv_ref[:, DH:].T

    def step(i, _):
        qt = i // tiles
        kt = i % tiles
        qo = pl.multiple_of(qt * tile, tile)
        ko = pl.multiple_of(kt * tile, tile)
        q0 = scal[0] + qo
        k0 = scal[1] + ko

        @pl.when(needed(scal, docs, q0, k0, tile))
        def _():
            bias = tile_bias(scal, docs, q0, k0, tile)
            k = kv_ref[pl.ds(ko, tile), :DH]
            vt = vt_ref[:, pl.ds(ko, tile)]
            for h in range(heads):
                q = q_ref[pl.ds(qo, tile), h * DH : (h + 1) * DH]
                s = dot(k, q, NT) * factor + bias
                m_old = m_ref[h : h + 1, pl.ds(qo, tile)]
                m_new = jnp.maximum(m_old, jnp.max(s, axis=0, keepdims=True))
                p = jnp.exp2(s - m_new)
                alpha = jnp.exp2(m_old - m_new)
                m_ref[h : h + 1, pl.ds(qo, tile)] = m_new
                l_ref[h : h + 1, pl.ds(qo, tile)] = alpha * l_ref[
                    h : h + 1, pl.ds(qo, tile)
                ] + jnp.sum(p, axis=0, keepdims=True)
                o_ref[h * DH : (h + 1) * DH, pl.ds(qo, tile)] = alpha * o_ref[
                    h * DH : (h + 1) * DH, pl.ds(qo, tile)
                ] + dot(vt, p.astype(jnp.bfloat16), NN)

        return 0

    lax.fori_loop(0, tiles * tiles, step, 0)


def stats(scal, docs, tile, q, kv, state):
    chunk, width = q.shape
    heads = width // DH
    shapes = (
        jax.ShapeDtypeStruct((heads, chunk), jnp.float32),
        jax.ShapeDtypeStruct((heads, chunk), jnp.float32),
        jax.ShapeDtypeStruct((width, chunk), jnp.float32),
    )
    first = state is None
    extra = () if first else state
    return pl.pallas_call(
        functools.partial(stats_kernel, docs, tile, heads, first),
        out_shape=shapes,
        in_specs=[whole(pltpu.SMEM)] + [whole()] * (2 + len(extra)),
        out_specs=(whole(),) * 3,
        scratch_shapes=[pltpu.VMEM((DH, chunk), jnp.bfloat16)],
        compiler_params=params(),
        cost_estimate=cost(4 * chunk * chunk * width, 12 * chunk * width, chunk * chunk * heads),
        name="row_stats",
    )(scal, q, kv, *extra)


def finish_kernel(heads, g_ref, m_ref, l_ref, o_ref, log_ref, delta_ref):
    log_ref[...] = m_ref[...] + jnp.log2(l_ref[...])
    for h in range(heads):
        gt = g_ref[:, h * DH : (h + 1) * DH].T.astype(jnp.float32)
        part = jnp.sum(gt * o_ref[h * DH : (h + 1) * DH, :], axis=0, keepdims=True)
        delta_ref[h : h + 1, :] = part / l_ref[h : h + 1, :]


def finish(g, m, l, o):
    heads, chunk = m.shape
    shape = jax.ShapeDtypeStruct((heads, chunk), jnp.float32)
    return pl.pallas_call(
        functools.partial(finish_kernel, heads),
        out_shape=(shape, shape),
        in_specs=[whole()] * 4,
        out_specs=(whole(),) * 2,
        compiler_params=params(),
        cost_estimate=cost(2 * chunk * heads * DH, 6 * chunk * heads * DH),
        name="row_delta",
    )(g, m, l, o)


def grads_kernel(docs, tile, heads, first, scal, q_ref, g_ref, kv_ref, log_ref, delta_ref, *refs):
    if first:
        dq_ref, dk_ref = refs
        dq_ref[...] = jnp.zeros_like(dq_ref)
    else:
        dq_in, dq_ref, dk_ref = refs
        dq_ref[...] = dq_in[...]
    dk_ref[...] = jnp.zeros_like(dk_ref)
    chunk = q_ref.shape[0]
    tiles = chunk // tile
    scaling = 1.0 / math.sqrt(DH)
    factor = LOG2E * scaling

    def step(i, _):
        qt = i // tiles
        kt = i % tiles
        qo = pl.multiple_of(qt * tile, tile)
        ko = pl.multiple_of(kt * tile, tile)
        q0 = scal[0] + qo
        k0 = scal[1] + ko

        @pl.when(needed(scal, docs, q0, k0, tile))
        def _():
            bias = tile_bias(scal, docs, q0, k0, tile)
            k = kv_ref[pl.ds(ko, tile), :DH]
            v = kv_ref[pl.ds(ko, tile), DH:]
            dk = jnp.zeros((tile, DH), jnp.float32)
            dv = jnp.zeros((tile, DH), jnp.float32)
            for h in range(heads):
                cols = slice(h * DH, (h + 1) * DH)
                q = q_ref[pl.ds(qo, tile), cols]
                g = g_ref[pl.ds(qo, tile), cols]
                s = dot(k, q, NT) * factor + bias
                p = jnp.exp2(s - log_ref[h : h + 1, pl.ds(qo, tile)])
                dp = dot(v, g, NT)
                ds = (p * (dp - delta_ref[h : h + 1, pl.ds(qo, tile)])).astype(jnp.bfloat16)
                dv += dot(p.astype(jnp.bfloat16), g, NN)
                dk += dot(ds, q, NN)
                dq_ref[pl.ds(qo, tile), cols] += dot(ds.T, k, NN) * scaling
            dk_ref[pl.ds(ko, tile), :DH] += dk * scaling
            dk_ref[pl.ds(ko, tile), DH:] += dv

        return 0

    lax.fori_loop(0, tiles * tiles, step, 0)


def grads(scal, docs, tile, q, g, kv, log_total, delta, dq):
    chunk, width = q.shape
    heads = width // DH
    shapes = (
        jax.ShapeDtypeStruct((chunk, width), jnp.float32),
        jax.ShapeDtypeStruct((chunk, 2 * DH), jnp.float32),
    )
    first = dq is None
    extra = () if first else (dq,)
    return pl.pallas_call(
        functools.partial(grads_kernel, docs, tile, heads, first),
        out_shape=shapes,
        in_specs=[whole(pltpu.SMEM)] + [whole()] * (5 + len(extra)),
        out_specs=(whole(),) * 2,
        compiler_params=params(),
        cost_estimate=cost(10 * chunk * chunk * width, 12 * chunk * width, chunk * chunk * heads),
        name="pair_grads",
    )(scal, q, g, kv, log_total, delta, *extra)


def project_kernel(with_part, half, d_ref, w_ref, *refs):
    total = dot(d_ref[...], w_ref[...], NT)
    if with_part:
        part_ref, out_ref = refs
        total = total + part_ref[...]
    else:
        (out_ref,) = refs
    out_ref[...] = total.astype(out_ref.dtype)


def project(half, d, w, part, first_block, count, blocks, dtype):
    rows, depth = d.shape
    wide = w.shape[0] // blocks
    extra = () if part is None else (part,)

    def kernel(idx, *refs):
        project_kernel(part is not None, half, *refs)

    grid_spec = pltpu.PrefetchScalarGridSpec(
        num_scalar_prefetch=1,
        grid=(count,),
        in_specs=[
            pl.BlockSpec((rows, depth), lambda i, idx: (0, 0)),
            pl.BlockSpec((wide, depth), lambda i, idx: (idx[1 + i], idx[0])),
        ]
        + [pl.BlockSpec((rows, wide), lambda i, idx: (0, idx[1 + i]))] * len(extra),
        out_specs=pl.BlockSpec((rows, wide), lambda i, idx: (0, idx[1 + i] if count > 1 else 0)),
    )
    return pl.pallas_call(
        kernel,
        out_shape=jax.ShapeDtypeStruct((rows, wide * count), dtype),
        grid_spec=grid_spec,
        compiler_params=params(),
        cost_estimate=cost(2 * rows * depth * wide * count, 2 * depth * wide * count),
        name="project",
    )(jnp.concatenate([half[None], first_block]), d, w, *extra)


def solution(mesh):
    n_seq = mesh.shape["seq"]
    n_head = mesh.shape["head"]

    def shards(queries, keys, values, d_out, w_out, doc_starts):
        rows = queries.shape[0]
        groups = keys.shape[1] // DH
        heads = queries.shape[1] // keys.shape[1]
        width = heads * DH
        docs = doc_starts.shape[0]
        team = groups
        layers = n_seq // team
        chunk = team * rows
        tile = 256 if chunk % 256 == 0 else rows
        me = lax.axis_index("seq")
        mine = me % team
        layer = me // team
        head = lax.axis_index("head")

        def swap(m, x):
            return lax.ppermute(x, "seq", [(i, i ^ m) for i in range(n_seq)])

        def shift(d, x):
            pairs = [(i, i + d * team) for i in range(n_seq) if 0 <= i + d * team < n_seq]
            return lax.ppermute(x, "seq", pairs)

        def ordered(parts, axis):
            if team == 1:
                return parts[0]
            size = parts[0].shape[axis]
            shape = list(parts[0].shape)
            shape[axis] *= team
            out = jnp.zeros(shape, parts[0].dtype)
            for m, x in enumerate(parts):
                out = lax.dynamic_update_slice_in_dim(out, x, (mine ^ m) * size, axis)
            return out

        def columns(x, m, size):
            return lax.dynamic_slice_in_dim(x, (mine ^ m) * size, size, 1)

        def scalars(d):
            return jnp.concatenate(
                [jnp.stack([layer * chunk, (layer - d) * chunk]), doc_starts]
            ).astype(jnp.int32)

        order = list(range(1, team)) + [0]
        if n_head == 2:
            d_far = lax.ppermute(d_out, "head", [(0, 1), (1, 0)])
        kv_parts = [
            jnp.concatenate([columns(keys, m, DH), columns(values, m, DH)], axis=1)
            for m in range(team)
        ]
        kv_parts = [x if m == 0 else swap(m, x) for m, x in enumerate(kv_parts)]
        kv = ordered(kv_parts, 0)
        q_parts = [columns(queries, m, width) for m in range(team)]
        q_parts = [x if m == 0 else swap(m, x) for m, x in enumerate(q_parts)]
        q = ordered(q_parts, 0)

        blocks = [(mine ^ m) for m in range(team)]
        if n_head == 2:
            part = project(
                head, d_out, w_out, None, jnp.arange(team, dtype=jnp.int32), team, team, jnp.float32
            )
            g_parts = [
                project(1 - head, d_far, w_out, part, b[None], 1, team, jnp.bfloat16)
                for b in blocks
            ]
        else:
            d_all = lax.all_gather(d_out, "head", axis=1, tiled=True)
            g_parts = [
                project(jnp.int32(0), d_all, w_out, None, b[None], 1, team, jnp.bfloat16)
                for b in blocks
            ]
        g_parts = [x if m == 0 else swap(m, x) for m, x in enumerate(g_parts)]
        g = ordered(g_parts, 0)

        if layers <= 4:
            kvs = [kv]
            for d in range(1, layers):
                kvs.append(shift(3, kv) if d == 3 else shift(1, kvs[d - 1]))
            state = None
            for d in range(layers):
                state = stats(scalars(d), docs, tile, q, kvs[d], state)
            log_total, delta = finish(g, *state)
            dq = None
            carried = None
            late = None
            for d in reversed(range(layers)):
                dq, dkv = grads(scalars(d), docs, tile, q, g, kvs[d], log_total, delta, dq)
                if carried is not None:
                    dkv = dkv + carried.astype(jnp.float32)
                    carried = None
                if d == 3:
                    late = shift(-3, dkv.astype(jnp.bfloat16))
                elif d > 0:
                    carried = shift(-1, dkv.astype(jnp.bfloat16))
                elif late is not None:
                    dkv = dkv + late.astype(jnp.float32)
            dkv = dkv.astype(jnp.bfloat16)
        else:
            rings = [[z * team + a for z in range(layers)] for a in range(team)]
            every = lax.all_gather(kv, "seq", axis_index_groups=rings)

            def chunk_at(d):
                return lax.dynamic_index_in_dim(every, jnp.maximum(layer - d, 0), 0, keepdims=False)

            def one(d, state):
                return tuple(stats(scalars(d), docs, tile, q, chunk_at(d), state))

            state = (
                jnp.full((heads, chunk), NEG, jnp.float32),
                jnp.zeros((heads, chunk), jnp.float32),
                jnp.zeros((width, chunk), jnp.float32),
            )
            state = lax.fori_loop(0, layers, one, state)
            log_total, delta = finish(g, *state)

            def two(d, carry):
                dq, total = carry
                dq, dkv = grads(scalars(d), docs, tile, q, g, chunk_at(d), log_total, delta, dq)
                place = jnp.maximum(layer - d, 0)
                old = lax.dynamic_index_in_dim(total, place, 0, keepdims=False)
                total = lax.dynamic_update_index_in_dim(
                    total, old + jnp.where(layer >= d, dkv, 0.0), place, 0
                )
                return dq, total

            dq = jnp.zeros((chunk, width), jnp.float32)
            total = jnp.zeros((layers, chunk, 2 * DH), jnp.float32)
            dq, total = lax.fori_loop(0, layers, two, (dq, total))
            dkv = lax.psum_scatter(
                total.astype(jnp.bfloat16).reshape(layers * chunk, 2 * DH),
                "seq",
                axis_index_groups=rings,
                tiled=True,
            )

        dq = dq.astype(jnp.bfloat16)

        def back(x, m):
            return lax.dynamic_slice_in_dim(x, (mine ^ m) * rows, rows, 0)

        dq_parts = [back(dq, m) for m in range(team)]
        dq_parts = [x if m == 0 else swap(m, x) for m, x in enumerate(dq_parts)]
        dkv_parts = [back(dkv, m) for m in range(team)]
        dkv_parts = [x if m == 0 else swap(m, x) for m, x in enumerate(dkv_parts)]
        query_grad = ordered(dq_parts, 1)
        key_grad = ordered([x[:, :DH] for x in dkv_parts], 1)
        value_grad = ordered([x[:, DH:] for x in dkv_parts], 1)
        return (query_grad, key_grad, value_grad)

    return jax.shard_map(
        shards,
        mesh=mesh,
        in_specs=(
            P("seq", "head"),
            P("seq", "head"),
            P("seq", "head"),
            P("seq", "head"),
            P("head", None),
            P(),
        ),
        out_specs=(P("seq", "head"), P("seq", "head"), P("seq", "head")),
        check_vma=False,
    )
```

```python
import functools
import math

import jax
import jax.numpy as jnp
from jax import lax
from jax.experimental import pallas as pl
from jax.experimental.pallas import tpu as pltpu
from jax.sharding import PartitionSpec as P

DH = 128
ONES = 16
LOG2E = 1.4426950408889634
NEG = -1e30
VMEM_LIMIT = 28 * 1024 * 1024

NT = (((1,), (1,)), ((), ()))
NN = (((1,), (0,)), ((), ()))


def dot(a, b, dims):
    return lax.dot_general(a, b, dims, preferred_element_type=jnp.float32)


def params():
    return pltpu.CompilerParams(vmem_limit_bytes=VMEM_LIMIT)


def whole(memory_space=pltpu.VMEM):
    return pl.BlockSpec(memory_space=memory_space)


def cost(flops, nbytes, exps=0):
    return pl.CostEstimate(flops=int(flops), bytes_accessed=int(nbytes), transcendentals=int(exps))


FIRST_DOC = 4


def row_starts(scal, docs, pos):
    low = jnp.zeros_like(pos)
    for n in range(docs):
        low = jnp.where(pos >= scal[FIRST_DOC + n], scal[FIRST_DOC + n], low)
    return low


def doc_start_at(scal, docs, pos):
    low = jnp.int32(0)
    for n in range(docs):
        low = jnp.where(pos >= scal[FIRST_DOC + n], scal[FIRST_DOC + n], low)
    return low


def allowed(scal, docs, q0, k0, tq, tk):
    qpos = q0 + lax.broadcasted_iota(jnp.int32, (1, tq), 1)
    kpos = k0 + lax.broadcasted_iota(jnp.int32, (tk, 1), 0)
    return (kpos <= qpos) & (kpos >= row_starts(scal, docs, qpos))


def over_tiles(scal, docs, d, chunk, tile, body):
    tiles = chunk // tile

    def one(qo, ko, q0, tk, need):
        k0 = scal[1] - d * chunk + ko
        clean = (k0 + tk - 1 <= q0) & (k0 >= doc_start_at(scal, docs, q0 + tile - 1))
        pl.when(need & clean)(lambda: body(qo, ko, tk, None))

        @pl.when(need & jnp.logical_not(clean))
        def _():
            body(qo, ko, tk, allowed(scal, docs, q0, k0, tile, tk))

    def step(qt, _):
        qo = pl.multiple_of(qt * tile, tile)
        q0 = scal[0] + qo
        low = doc_start_at(scal, docs, q0)
        k0 = scal[1] - d * chunk
        if tiles == 1:
            one(qo, 0, q0, tile, (k0 <= q0 + tile - 1) & (k0 + tile - 1 >= low))
            return 0
        all_of = (k0 + chunk - tile <= q0 + tile - 1) & (k0 + tile - 1 >= low)
        one(qo, 0, q0, chunk, all_of)

        @pl.when(jnp.logical_not(all_of))
        def _():
            def inner(kt, _):
                ko = pl.multiple_of(kt * tile, tile)
                need = (k0 + ko <= q0 + tile - 1) & (k0 + ko + tile - 1 >= low)
                one(qo, ko, q0, tile, need)
                return 0

            lax.fori_loop(0, tiles, inner, 0)

        return 0

    lax.fori_loop(0, tiles, step, 0)


def stats_kernel(docs, tile, heads, d, first, scal, q_ref, kv_ref, *refs):
    if first:
        m_ref, o_ref, vt_ref = refs
        m_ref[...] = jnp.full_like(m_ref, NEG)
        o_ref[...] = jnp.zeros_like(o_ref)
    else:
        m_in, o_in, m_ref, o_ref, vt_ref = refs
        m_ref[...] = m_in[...]
        o_ref[...] = o_in[...]
    chunk = q_ref.shape[0]
    factor = LOG2E / math.sqrt(DH)
    ext = DH + ONES
    vt_ref[:DH] = kv_ref[:, DH:].T
    vt_ref[DH:] = jnp.ones((vt_ref.shape[0] - DH, chunk), jnp.bfloat16)

    def body(qo, ko, tk, mask):
        k = kv_ref[pl.ds(ko, tk), :DH]
        vt = vt_ref[:ext, pl.ds(ko, tk)]
        rows = pl.ds(qo, tile)
        m_old = m_ref[:, rows]
        scores = [dot(k, q_ref[rows, h * DH : (h + 1) * DH], NT) for h in range(heads)]
        if mask is not None:
            scores = [jnp.where(mask, s, NEG) for s in scores]
        tops = [jnp.max(s, axis=0, keepdims=True) for s in scores]
        m_new = jnp.maximum(m_old, factor * jnp.concatenate(tops, 0))
        alpha = jnp.exp2(m_old - m_new)
        m_ref[:, rows] = m_new
        for h in range(heads):
            p = jnp.exp2(scores[h] * factor - m_new[h : h + 1]).astype(jnp.bfloat16)
            part = slice(h * ext, (h + 1) * ext)
            o_ref[part, rows] = alpha[h : h + 1] * o_ref[part, rows] + dot(vt, p, NN)

    over_tiles(scal, docs, d, chunk, tile, body)


def stats(scal, docs, tile, d, q, kv, state):
    chunk, width = q.shape
    heads = width // DH
    shapes = (
        jax.ShapeDtypeStruct((heads, chunk), jnp.float32),
        jax.ShapeDtypeStruct((heads * (DH + ONES), chunk), jnp.float32),
    )
    first = state is None
    extra = () if first else state
    return pl.pallas_call(
        functools.partial(stats_kernel, docs, tile, heads, d, first),
        out_shape=shapes,
        in_specs=[whole(pltpu.SMEM)] + [whole()] * (2 + len(extra)),
        out_specs=(whole(),) * 2,
        scratch_shapes=[pltpu.VMEM((DH + ONES, chunk), jnp.bfloat16)],
        compiler_params=params(),
        cost_estimate=cost(4 * chunk * chunk * width, 12 * chunk * width, chunk * chunk * heads),
        name="row_stats",
    )(scal, q, kv, *extra)


def finish_kernel(heads, g_ref, m_ref, o_ref, log_ref, delta_ref):
    ext = DH + ONES
    for h in range(heads):
        total = o_ref[h * ext + DH : h * ext + DH + 1, :]
        gt = g_ref[:, h * DH : (h + 1) * DH].T.astype(jnp.float32)
        part = jnp.sum(gt * o_ref[h * ext : h * ext + DH, :], axis=0, keepdims=True)
        log_ref[h : h + 1, :] = m_ref[h : h + 1, :] + jnp.log2(total)
        delta_ref[h : h + 1, :] = part / total


def finish(g, m, o):
    heads, chunk = m.shape
    shape = jax.ShapeDtypeStruct((heads, chunk), jnp.float32)
    return pl.pallas_call(
        functools.partial(finish_kernel, heads),
        out_shape=(shape, shape),
        in_specs=[whole()] * 3,
        out_specs=(whole(),) * 2,
        compiler_params=params(),
        cost_estimate=cost(2 * chunk * heads * DH, 6 * chunk * heads * DH),
        name="row_delta",
    )(g, m, o)


def grads_kernel(
    docs, tile, heads, d, first, team, scal, q_ref, g_ref, kv_ref, log_ref, delta_ref, *refs
):
    refs = list(refs)
    dq_in = None if first else refs.pop(0)
    acc_ref, kt_ref = refs.pop(), refs.pop()
    dkv_ref = refs.pop()
    last = team is not None
    if last:
        full_ref = acc_ref
        acc_ref, dq_ref = refs.pop(), refs.pop()
        outs = refs
    else:
        dq_ref = refs.pop()
    chunk = q_ref.shape[0]
    scaling = 1.0 / math.sqrt(DH)
    factor = LOG2E * scaling
    if first:
        dq_ref[...] = jnp.zeros_like(dq_ref)
    else:
        dq_ref[...] = dq_in[...]
    acc_ref[...] = jnp.zeros_like(acc_ref)
    kt_ref[...] = kv_ref[:, :DH].T

    def body(qo, ko, tk, mask):
        rows = pl.ds(qo, tile)
        keys = pl.ds(ko, tk)
        k = kv_ref[keys, :DH]
        v = kv_ref[keys, DH:]
        qs = [q_ref[rows, h * DH : (h + 1) * DH] for h in range(heads)]
        gs = [g_ref[rows, h * DH : (h + 1) * DH] for h in range(heads)]
        scores = [dot(k, q, NT) for q in qs]
        dots = [dot(v, g, NT) for g in gs]
        if mask is not None:
            scores = [jnp.where(mask, s, NEG) for s in scores]
        probs = [
            jnp.exp2(scores[h] * factor - log_ref[h : h + 1, rows]) for h in range(heads)
        ]
        ds = [
            (probs[h] * (dots[h] - delta_ref[h : h + 1, rows])).astype(jnp.bfloat16)
            for h in range(heads)
        ]
        probs = [p.astype(jnp.bfloat16) for p in probs]
        dv = dot(jnp.concatenate(probs, 1), jnp.concatenate(gs, 0), NN)
        dk = dot(jnp.concatenate(ds, 1), jnp.concatenate(qs, 0), NN)
        kt = kt_ref[:, keys]
        for h in range(heads):
            dq_ref[h * DH : (h + 1) * DH, rows] += dot(kt, ds[h], NN)
        acc_ref[keys, :DH] += dk
        acc_ref[keys, DH:] += dv

    over_tiles(scal, docs, d, chunk, tile, body)
    dkv_ref[:, :DH] = (acc_ref[:, :DH] * scaling).astype(dkv_ref.dtype)
    dkv_ref[:, DH:] = acc_ref[:, DH:].astype(dkv_ref.dtype)
    if last:
        for h in range(heads):
            full_ref[:, h * DH : (h + 1) * DH] = (
                (dq_ref[h * DH : (h + 1) * DH, :] * scaling).T.astype(jnp.bfloat16)
            )
        size = chunk // team
        for m in range(team):
            outs[m][...] = full_ref[pl.ds(pl.multiple_of((scal[2] ^ m) * size, size), size), :]


def grads(scal, docs, tile, d, q, g, kv, log_total, delta, dq, team=None, dtype=jnp.bfloat16):
    chunk, width = q.shape
    heads = width // DH
    first = dq is None
    extra = () if first else (dq,)
    dkv_shape = jax.ShapeDtypeStruct((chunk, 2 * DH), dtype)
    scratch = [pltpu.VMEM((DH, chunk), jnp.bfloat16)]
    dq_rows = pltpu.VMEM((width, chunk), jnp.float32)
    acc = pltpu.VMEM((chunk, 2 * DH), jnp.float32)
    if team is None:
        shapes = (jax.ShapeDtypeStruct((width, chunk), jnp.float32), dkv_shape)
        scratch = scratch + [acc]
        kernel = functools.partial(grads_kernel, docs, tile, heads, d, first, None)
    else:
        shapes = (jax.ShapeDtypeStruct((chunk // team, width), jnp.bfloat16),) * team + (dkv_shape,)
        scratch = [dq_rows, acc] + scratch + [pltpu.VMEM((chunk, width), jnp.bfloat16)]

        def kernel(*refs):
            refs = list(refs)
            full, kt, acc_ref, dq_ref = refs.pop(), refs.pop(), refs.pop(), refs.pop()
            dkv_ref = refs.pop()
            refs = refs + [dq_ref, acc_ref, dkv_ref, kt, full]
            grads_kernel(docs, tile, heads, d, first, team, *refs)

    return pl.pallas_call(
        kernel,
        out_shape=shapes,
        in_specs=[whole(pltpu.SMEM)] + [whole()] * (5 + len(extra)),
        out_specs=(whole(),) * len(shapes),
        scratch_shapes=scratch,
        compiler_params=params(),
        cost_estimate=cost(10 * chunk * chunk * width, 12 * chunk * width, chunk * chunk * heads),
        name="pair_grads",
    )(scal, q, g, kv, log_total, delta, *extra)


def project(scal, d, w, part, far, blocks, dtype):
    rows, depth = d.shape
    wide = w.shape[0] // blocks
    split = w.shape[1] // depth

    def kernel(*refs):
        scal, d_ref, w_ref = refs[:3]
        total = dot(d_ref[...], w_ref[...], NT)
        if part is not None:
            total = total + refs[3][...]
        if part is None:
            refs[-1][...] = total.astype(dtype)
        else:
            for m in range(blocks):

                @pl.when(pl.program_id(0) == m)
                def _():
                    refs[4 + m][...] = total.astype(dtype)

    def order(i):
        return blocks - 1 - i

    def column(s):
        if split == 1:
            return 0
        return 1 - s[3] if far else s[3]

    w_spec = pl.BlockSpec((wide, depth), lambda i, s: (s[2] ^ i, column(s)))
    part_spec = pl.BlockSpec((rows, wide), lambda i, s: (0, i))
    if part is None:
        out_shape = jax.ShapeDtypeStruct((rows, wide * blocks), dtype)
        out_specs = part_spec
    else:
        out_shape = (jax.ShapeDtypeStruct((rows, wide), dtype),) * blocks
        out_specs = (pl.BlockSpec((rows, wide), lambda i, s: (0, 0)),) * blocks
    grid_spec = pltpu.PrefetchScalarGridSpec(
        num_scalar_prefetch=1,
        grid=(blocks,),
        in_specs=[pl.BlockSpec((rows, depth), lambda i, s: (0, 0)), w_spec]
        + ([] if part is None else [part_spec]),
        out_specs=out_specs,
    )
    return pl.pallas_call(
        kernel,
        out_shape=out_shape,
        grid_spec=grid_spec,
        compiler_params=params(),
        cost_estimate=cost(2 * rows * depth * wide * blocks, 2 * depth * wide * blocks),
        name="project",
    )(scal, d, w, *(() if part is None else (part,)))


def copies(scal, inputs, out_shapes, plan, name):
    n_in = len(inputs)

    def kernel(scal, *refs):
        ins, outs, sems = refs[:n_in], refs[n_in:-1], refs[-1]
        started = []
        for i, (a, src, b, dst) in enumerate(plan(scal[2])):
            copy = pltpu.make_async_copy(ins[a].at[src], outs[b].at[dst], sems.at[i])
            copy.start()
            started.append(copy)
        for copy in started:
            copy.wait()

    count = len(plan(0))
    size = sum(math.prod(s.shape) * 2 for s in out_shapes)
    return pl.pallas_call(
        kernel,
        out_shape=tuple(out_shapes),
        in_specs=[whole(pltpu.SMEM)] + [whole(pl.ANY)] * n_in,
        out_specs=(whole(pl.ANY),) * len(out_shapes),
        scratch_shapes=[pltpu.SemaphoreType.DMA((count,))],
        compiler_params=params(),
        cost_estimate=cost(0, 2 * size),
        name=name,
    )(scal, *inputs)


def span(start, size):
    if isinstance(start, int):
        return pl.ds(start, size)
    return pl.ds(pl.multiple_of(start * size, size), size)


ALL = slice(None)


def solution(mesh):
    n_seq = mesh.shape["seq"]
    n_head = mesh.shape["head"]

    def shards(queries, keys, values, d_out, w_out, doc_starts):
        rows = queries.shape[0]
        groups = keys.shape[1] // DH
        heads = queries.shape[1] // keys.shape[1]
        width = heads * DH
        docs = doc_starts.shape[0]
        team = groups
        layers = n_seq // team
        chunk = team * rows
        tile = 256 if chunk % 256 == 0 else rows
        me = lax.axis_index("seq")
        layer = me // team
        head = lax.axis_index("head")
        base = layer * chunk
        scal = jnp.concatenate([jnp.stack([base, base, me % team, head]), doc_starts])

        def half(*shape):
            return jax.ShapeDtypeStruct(shape, jnp.bfloat16)

        def swap(m, x):
            return lax.ppermute(x, "seq", [(i, i ^ m) for i in range(n_seq)])

        def swapped(parts):
            got = list(parts)
            for m in reversed(range(1, team)):
                got[m] = swap(m, parts[m])
            return got

        def shift(d, x):
            pairs = [(i, i + d * team) for i in range(n_seq) if 0 <= i + d * team < n_seq]
            return lax.ppermute(x, "seq", pairs)

        def pack(arrays, sizes, name):
            def plan(place):
                out = []
                for m in range(1, team):
                    at = 0
                    for a, size in enumerate(sizes):
                        out.append((a, (ALL, span(place ^ m, size)), m - 1, (ALL, pl.ds(at, size))))
                        at += size
                return out

            shapes = [half(rows, sum(sizes))] * (team - 1)
            return copies(scal, arrays, shapes, plan, name)

        def stack(arrays, sizes, parts, name):
            def plan(place):
                out = []
                at = 0
                for a, size in enumerate(sizes):
                    src = (ALL, ALL) if arrays[a].shape[1] == size else (ALL, span(place, size))
                    out.append((a, src, 0, (span(place, rows), pl.ds(at, size))))
                    at += size
                for m in range(1, team):
                    out.append((len(arrays) + m - 1, (ALL, ALL), 0, (span(place ^ m, rows), ALL)))
                return out

            shapes = [half(chunk, sum(sizes))]
            return copies(scal, list(arrays) + list(parts), shapes, plan, name)[0]

        def beside(parts, sizes, name):
            def plan(place):
                out = []
                for m in range(team):
                    at = 0
                    for b, size in enumerate(sizes):
                        out.append((m, (ALL, pl.ds(at, size)), b, (ALL, span(place ^ m, size))))
                        at += size
                return out

            shapes = [half(rows, team * size) for size in sizes]
            return copies(scal, parts, shapes, plan, name)

        if team > 1:
            kv_sent = pack([keys, values], [DH, DH], "pack_keys_values")
            kv_got = swapped([None, *kv_sent])[1:]
            if n_head == 2:
                d_far = lax.ppermute(d_out, "head", [(0, 1), (1, 0)])
            q_sent = pack([queries], [width], "pack_queries")
            q_got = swapped([None, *q_sent])[1:]
            kv = stack([keys, values], [DH, DH], kv_got, "stack_keys_values")
            q = stack([queries], [width], q_got, "stack_queries")
        else:
            kv = jnp.concatenate([keys, values], axis=1)
            q = queries
            if n_head == 2:
                d_far = lax.ppermute(d_out, "head", [(0, 1), (1, 0)])

        if n_head == 2:
            part = project(scal, d_out, w_out, None, False, team, jnp.float32)
            g_parts = project(scal, d_far, w_out, part, True, team, jnp.bfloat16)
        else:
            d_all = lax.all_gather(d_out, "head", axis=1, tiled=True)
            zero = jnp.zeros((rows, width * team), jnp.float32)
            g_parts = project(scal, d_all, w_out, zero, False, team, jnp.bfloat16)
        if team > 1:
            g_got = swapped(g_parts)
            g = stack([g_got[0]], [width], g_got[1:], "stack_attn_grad")
        else:
            g = g_parts[0]

        if layers <= 4:
            kvs = [kv]
            for d in range(1, layers):
                kvs.append(shift(1, kvs[d - 1]) if d == 2 else shift(d, kv))
            state = None
            for d in range(layers):
                state = stats(scal, docs, tile, d, q, kvs[d], state)
            log_total, delta = finish(g, *state)
            dq = None
            terms = []
            for d in reversed(range(1, layers)):
                dq, dkv = grads(scal, docs, tile, d, q, g, kvs[d], log_total, delta, dq)
                terms.append(shift(-d, dkv))
            *dq_parts, dkv = grads(
                scal, docs, tile, 0, q, g, kv, log_total, delta, dq, team, jnp.float32
            )
        else:
            rings = [[z * team + a for z in range(layers)] for a in range(team)]
            every = lax.all_gather(kv, "seq", axis_index_groups=rings)

            def chunk_at(d):
                return lax.dynamic_index_in_dim(every, jnp.maximum(layer - d, 0), 0, keepdims=False)

            def scalars(d):
                return scal - jnp.where(jnp.arange(scal.shape[0]) == 1, d * chunk, 0)

            def one(d, state):
                return tuple(stats(scalars(d), docs, tile, 0, q, chunk_at(d), state))

            state = lax.fori_loop(1, layers, one, tuple(stats(scal, docs, tile, 0, q, kv, None)))
            log_total, delta = finish(g, *state)

            def two(d, carry):
                dq, total = carry
                dq, dkv = grads(
                    scalars(d), docs, tile, 0, q, g, chunk_at(d), log_total, delta, dq
                )
                place = jnp.maximum(layer - d, 0)
                old = lax.dynamic_index_in_dim(total, place, 0, keepdims=False)
                total = lax.dynamic_update_index_in_dim(
                    total, jnp.where(layer >= d, dkv, old), place, 0
                )
                return dq, total

            dq = jnp.zeros((width, chunk), jnp.float32)
            total = jnp.zeros((layers, chunk, 2 * DH), jnp.bfloat16)
            dq, total = lax.fori_loop(1, layers, two, (dq, total))
            *dq_parts, dkv = grads(
                scal, docs, tile, 0, q, g, kv, log_total, delta, dq, team, jnp.float32
            )
            terms = [
                lax.psum_scatter(
                    total.reshape(layers * chunk, 2 * DH), "seq", axis_index_groups=rings, tiled=True
                )
            ]

        def sum_kernel(scal, *refs):
            total = refs[0][...]
            for x in refs[1 : 1 + len(terms)]:
                total = total + x[...].astype(jnp.float32)
            full = refs[-1]
            full[...] = total.astype(jnp.bfloat16)
            for m in range(team):
                refs[1 + len(terms) + m][...] = full[span(scal[2] ^ m, rows), :]

        dkv_parts = pl.pallas_call(
            sum_kernel,
            out_shape=(half(rows, 2 * DH),) * team,
            in_specs=[whole(pltpu.SMEM)] + [whole()] * (1 + len(terms)),
            out_specs=(whole(),) * team,
            scratch_shapes=[pltpu.VMEM((chunk, 2 * DH), jnp.bfloat16)],
            compiler_params=params(),
            name="sum_terms",
        )(scal, dkv, *terms)
        if team > 1:
            dq_parts = swapped(dq_parts)
            dkv_parts = swapped(dkv_parts)
            (query_grad,) = beside(dq_parts, [width], "place_query_grad")
            key_grad, value_grad = beside(dkv_parts, [DH, DH], "place_key_value_grad")
        else:
            query_grad = dq_parts[0]
            key_grad = dkv_parts[0][:, :DH]
            value_grad = dkv_parts[0][:, DH:]
        return (query_grad, key_grad, value_grad)

    return jax.shard_map(
        shards,
        mesh=mesh,
        in_specs=(
            P("seq", "head"),
            P("seq", "head"),
            P("seq", "head"),
            P("seq", "head"),
            P("head", None),
            P(),
        ),
        out_specs=(P("seq", "head"), P("seq", "head"), P("seq", "head")),
        check_vma=False,
    )
```

```python
import functools
import math

import jax
import jax.numpy as jnp
from jax import lax
from jax.experimental import pallas as pl
from jax.experimental.pallas import tpu as pltpu
from jax.sharding import PartitionSpec as P

DH = 128
ONES = 16
LOG2E = 1.4426950408889634
NEG = -1e30
VMEM_LIMIT = 28 * 1024 * 1024
PROJECT_LIMIT = 52 * 1024 * 1024

NT = (((1,), (1,)), ((), ()))
NN = (((1,), (0,)), ((), ()))


def dot(a, b, dims):
    return lax.dot_general(a, b, dims, preferred_element_type=jnp.float32)


def params(limit=VMEM_LIMIT):
    return pltpu.CompilerParams(vmem_limit_bytes=limit)


def whole(memory_space=pltpu.VMEM):
    return pl.BlockSpec(memory_space=memory_space)


def ordered_call(kernel, scal, operands, after, **kwargs):
    count = len(after)

    def body(*refs):
        kernel(*refs[: 1 + len(operands)], *refs[1 + len(operands) + count :])

    specs = kwargs.pop("in_specs", [whole()] * len(operands))
    return pl.pallas_call(
        body,
        in_specs=[whole(pltpu.SMEM)] + specs + [whole(pl.ANY)] * count,
        compiler_params=params(),
        **kwargs,
    )(scal, *operands, *after)


def cost(flops, nbytes, exps=0):
    return pl.CostEstimate(flops=1024, bytes_accessed=1024, transcendentals=0)


FIRST_DOC = 4


def row_starts(scal, docs, pos):
    low = jnp.zeros_like(pos)
    for n in range(docs):
        low = jnp.where(pos >= scal[FIRST_DOC + n], scal[FIRST_DOC + n], low)
    return low


def doc_start_at(scal, docs, pos):
    low = jnp.int32(0)
    for n in range(docs):
        low = jnp.where(pos >= scal[FIRST_DOC + n], scal[FIRST_DOC + n], low)
    return low


def allowed(scal, docs, q0, k0, tq, tk):
    qpos = q0 + lax.broadcasted_iota(jnp.int32, (1, tq), 1)
    kpos = k0 + lax.broadcasted_iota(jnp.int32, (tk, 1), 0)
    return (kpos <= qpos) & (kpos >= row_starts(scal, docs, qpos))


def over_tiles(scal, docs, d, chunk, tile, body):
    tiles = chunk // tile

    def one(qo, ko, q0, tk, need):
        k0 = scal[1] - d * chunk + ko
        clean = (k0 + tk - 1 <= q0) & (k0 >= doc_start_at(scal, docs, q0 + tile - 1))
        pl.when(need & clean)(lambda: body(qo, ko, tk, None))

        @pl.when(need & jnp.logical_not(clean))
        def _():
            body(qo, ko, tk, allowed(scal, docs, q0, k0, tile, tk))

    def step(qt, _):
        qo = pl.multiple_of(qt * tile, tile)
        q0 = scal[0] + qo
        low = doc_start_at(scal, docs, q0)
        k0 = scal[1] - d * chunk
        if tiles == 1:
            one(qo, 0, q0, tile, (k0 <= q0 + tile - 1) & (k0 + tile - 1 >= low))
            return 0
        all_of = (k0 + chunk - tile <= q0 + tile - 1) & (k0 + tile - 1 >= low)
        one(qo, 0, q0, chunk, all_of)

        @pl.when(jnp.logical_not(all_of))
        def _():
            def inner(kt, _):
                ko = pl.multiple_of(kt * tile, tile)
                need = (k0 + ko <= q0 + tile - 1) & (k0 + ko + tile - 1 >= low)
                one(qo, ko, q0, tile, need)
                return 0

            lax.fori_loop(0, tiles, inner, 0)

        return 0

    lax.fori_loop(0, tiles, step, 0)


def stats_kernel(docs, tile, heads, d, first, scal, q_ref, kv_ref, *refs):
    if first:
        m_ref, o_ref, vt_ref = refs
        m_ref[...] = jnp.full_like(m_ref, NEG)
        o_ref[...] = jnp.zeros_like(o_ref)
    else:
        m_in, o_in, m_ref, o_ref, vt_ref = refs
        m_ref[...] = m_in[...]
        o_ref[...] = o_in[...]
    chunk = q_ref.shape[0]
    factor = LOG2E / math.sqrt(DH)
    ext = DH + ONES
    vt_ref[:DH] = kv_ref[:, DH:].T
    vt_ref[DH:] = jnp.ones((vt_ref.shape[0] - DH, chunk), jnp.bfloat16)

    def body(qo, ko, tk, mask):
        k = kv_ref[pl.ds(ko, tk), :DH]
        vt = vt_ref[:ext, pl.ds(ko, tk)]
        rows = pl.ds(qo, tile)
        m_old = m_ref[:, rows]
        scores = [dot(k, q_ref[rows, h * DH : (h + 1) * DH], NT) for h in range(heads)]
        if mask is not None:
            scores = [jnp.where(mask, s, NEG) for s in scores]
        tops = [jnp.max(s, axis=0, keepdims=True) for s in scores]
        m_new = jnp.maximum(m_old, factor * jnp.concatenate(tops, 0))
        alpha = jnp.exp2(m_old - m_new)
        m_ref[:, rows] = m_new
        for h in range(heads):
            p = jnp.exp2(scores[h] * factor - m_new[h : h + 1]).astype(jnp.bfloat16)
            part = slice(h * ext, (h + 1) * ext)
            o_ref[part, rows] = alpha[h : h + 1] * o_ref[part, rows] + dot(vt, p, NN)

    over_tiles(scal, docs, d, chunk, tile, body)


def stats(scal, docs, tile, d, q, kv, state, after=()):
    chunk, width = q.shape
    heads = width // DH
    shapes = (
        jax.ShapeDtypeStruct((heads, chunk), jnp.float32),
        jax.ShapeDtypeStruct((heads * (DH + ONES), chunk), jnp.float32),
    )
    first = state is None
    extra = () if first else state
    return ordered_call(
        functools.partial(stats_kernel, docs, tile, heads, d, first),
        scal,
        (q, kv, *extra),
        after,
        out_shape=shapes,
        out_specs=(whole(),) * 2,
        scratch_shapes=[pltpu.VMEM((DH + ONES, chunk), jnp.bfloat16)],
        cost_estimate=cost(4 * chunk * chunk * width, 12 * chunk * width, chunk * chunk * heads),
        name="row_stats",
    )


def finish_kernel(heads, g_ref, m_ref, o_ref, log_ref, delta_ref):
    ext = DH + ONES
    for h in range(heads):
        total = o_ref[h * ext + DH : h * ext + DH + 1, :]
        gt = g_ref[:, h * DH : (h + 1) * DH].T.astype(jnp.float32)
        part = jnp.sum(gt * o_ref[h * ext : h * ext + DH, :], axis=0, keepdims=True)
        log_ref[h : h + 1, :] = m_ref[h : h + 1, :] + jnp.log2(total)
        delta_ref[h : h + 1, :] = part / total


def finish(g, m, o):
    heads, chunk = m.shape
    shape = jax.ShapeDtypeStruct((heads, chunk), jnp.float32)
    return pl.pallas_call(
        functools.partial(finish_kernel, heads),
        out_shape=(shape, shape),
        in_specs=[whole()] * 3,
        out_specs=(whole(),) * 2,
        compiler_params=params(),
        cost_estimate=cost(2 * chunk * heads * DH, 6 * chunk * heads * DH),
        name="row_delta",
    )(g, m, o)


def grads_kernel(
    docs, tile, heads, d, first, team, scal, q_ref, g_ref, kv_ref, log_ref, delta_ref, *refs
):
    refs = list(refs)
    dq_in = None if first else refs.pop(0)
    acc_ref, kt_ref = refs.pop(), refs.pop()
    dkv_ref = refs.pop()
    last = team is not None
    if last:
        full_ref = acc_ref
        acc_ref, dq_ref = refs.pop(), refs.pop()
        outs = refs
    else:
        dq_ref = refs.pop()
    chunk = q_ref.shape[0]
    scaling = 1.0 / math.sqrt(DH)
    factor = LOG2E * scaling
    if first:
        dq_ref[...] = jnp.zeros_like(dq_ref)
    else:
        dq_ref[...] = dq_in[...]
    acc_ref[...] = jnp.zeros_like(acc_ref)
    kt_ref[...] = kv_ref[:, :DH].T

    def body(qo, ko, tk, mask):
        rows = pl.ds(qo, tile)
        keys = pl.ds(ko, tk)
        k = kv_ref[keys, :DH]
        v = kv_ref[keys, DH:]
        qs = [q_ref[rows, h * DH : (h + 1) * DH] for h in range(heads)]
        gs = [g_ref[rows, h * DH : (h + 1) * DH] for h in range(heads)]
        scores = [dot(k, q, NT) for q in qs]
        dots = [dot(v, g, NT) for g in gs]
        if mask is not None:
            scores = [jnp.where(mask, s, NEG) for s in scores]
        probs = [
            jnp.exp2(scores[h] * factor - log_ref[h : h + 1, rows]) for h in range(heads)
        ]
        ds = [
            (probs[h] * (dots[h] - delta_ref[h : h + 1, rows])).astype(jnp.bfloat16)
            for h in range(heads)
        ]
        probs = [p.astype(jnp.bfloat16) for p in probs]
        dv = dot(jnp.concatenate(probs, 1), jnp.concatenate(gs, 0), NN)
        dk = dot(jnp.concatenate(ds, 1), jnp.concatenate(qs, 0), NN)
        kt = kt_ref[:, keys]
        for h in range(heads):
            dq_ref[h * DH : (h + 1) * DH, rows] += dot(kt, ds[h], NN)
        acc_ref[keys, :DH] += dk
        acc_ref[keys, DH:] += dv

    over_tiles(scal, docs, d, chunk, tile, body)
    dkv_ref[:, :DH] = (acc_ref[:, :DH] * scaling).astype(dkv_ref.dtype)
    dkv_ref[:, DH:] = acc_ref[:, DH:].astype(dkv_ref.dtype)
    if last:
        for h in range(heads):
            full_ref[:, h * DH : (h + 1) * DH] = (
                (dq_ref[h * DH : (h + 1) * DH, :] * scaling).T.astype(jnp.bfloat16)
            )
        size = chunk // team
        for m in range(team):
            outs[m][...] = full_ref[pl.ds(pl.multiple_of((scal[2] ^ m) * size, size), size), :]


def grads(
    scal, docs, tile, d, q, g, kv, log_total, delta, dq, team=None, dtype=jnp.bfloat16, after=()
):
    chunk, width = q.shape
    heads = width // DH
    first = dq is None
    extra = () if first else (dq,)
    dkv_shape = jax.ShapeDtypeStruct((chunk, 2 * DH), dtype)
    scratch = [pltpu.VMEM((DH, chunk), jnp.bfloat16)]
    dq_rows = pltpu.VMEM((width, chunk), jnp.float32)
    acc = pltpu.VMEM((chunk, 2 * DH), jnp.float32)
    if team is None:
        shapes = (jax.ShapeDtypeStruct((width, chunk), jnp.float32), dkv_shape)
        scratch = scratch + [acc]
        kernel = functools.partial(grads_kernel, docs, tile, heads, d, first, None)
    else:
        shapes = (jax.ShapeDtypeStruct((chunk // team, width), jnp.bfloat16),) * team + (dkv_shape,)
        scratch = [dq_rows, acc] + scratch + [pltpu.VMEM((chunk, width), jnp.bfloat16)]

        def kernel(*refs):
            refs = list(refs)
            full, kt, acc_ref, dq_ref = refs.pop(), refs.pop(), refs.pop(), refs.pop()
            dkv_ref = refs.pop()
            refs = refs + [dq_ref, acc_ref, dkv_ref, kt, full]
            grads_kernel(docs, tile, heads, d, first, team, *refs)

    return ordered_call(
        kernel,
        scal,
        (q, g, kv, log_total, delta, *extra),
        after,
        out_shape=shapes,
        out_specs=(whole(),) * len(shapes),
        scratch_shapes=scratch,
        cost_estimate=cost(10 * chunk * chunk * width, 12 * chunk * width, chunk * chunk * heads),
        name="pair_grads",
    )


def project(scal, d, w, part, far, blocks, dtype, after=()):
    rows, depth = d.shape
    wide = w.shape[0] // blocks
    split = w.shape[1] // depth

    def kernel(*refs):
        scal, d_ref, w_ref = refs[:3]
        total = dot(d_ref[...], w_ref[...], NT)
        if part is not None:
            total = total + refs[3][...]
        if part is None:
            refs[-1][...] = total.astype(dtype)
        else:
            for m in range(blocks):

                @pl.when(pl.program_id(0) == m)
                def _():
                    refs[4 + len(after) + m][...] = total.astype(dtype)

    def column(s):
        if split == 1:
            return 0
        return 1 - s[3] if far else s[3]

    w_spec = pl.BlockSpec((wide, depth), lambda i, s: (s[2] ^ i, column(s)))
    part_spec = pl.BlockSpec((rows, wide), lambda i, s: (0, i))
    if part is None:
        out_shape = jax.ShapeDtypeStruct((rows, wide * blocks), dtype)
        out_specs = part_spec
    else:
        out_shape = (jax.ShapeDtypeStruct((rows, wide), dtype),) * blocks
        out_specs = (pl.BlockSpec((rows, wide), lambda i, s: (0, 0)),) * blocks
    grid_spec = pltpu.PrefetchScalarGridSpec(
        num_scalar_prefetch=1,
        grid=(blocks,),
        in_specs=[pl.BlockSpec((rows, depth), lambda i, s: (0, 0)), w_spec]
        + ([] if part is None else [part_spec])
        + [whole(pl.ANY)] * len(after),
        out_specs=out_specs,
    )
    return pl.pallas_call(
        kernel,
        out_shape=out_shape,
        grid_spec=grid_spec,
        compiler_params=params(PROJECT_LIMIT),
        cost_estimate=cost(2 * rows * depth * wide * blocks, 2 * depth * wide * blocks),
        name="project",
    )(scal, d, w, *(() if part is None else (part,)), *after)


def copies(scal, inputs, out_shapes, plan, name, after=()):
    n_in = len(inputs)

    def kernel(scal, *refs):
        ins, outs, sems = refs[:n_in], refs[n_in:-1], refs[-1]
        started = []
        for i, (a, src, b, dst) in enumerate(plan(scal[2])):
            copy = pltpu.make_async_copy(ins[a].at[src], outs[b].at[dst], sems.at[i])
            copy.start()
            started.append(copy)
        for copy in started:
            copy.wait()

    count = len(plan(0))
    size = sum(math.prod(s.shape) * 2 for s in out_shapes)
    return ordered_call(
        kernel,
        scal,
        inputs,
        after,
        out_shape=tuple(out_shapes),
        in_specs=[whole(pl.ANY)] * n_in,
        out_specs=(whole(pl.ANY),) * len(out_shapes),
        scratch_shapes=[pltpu.SemaphoreType.DMA((count,))],
        cost_estimate=cost(0, 2 * size),
        name=name,
    )


def add_kernel(a_ref, b_ref, out_ref):
    total = a_ref[...].astype(jnp.float32) + b_ref[...].astype(jnp.float32)
    out_ref[...] = total.astype(out_ref.dtype)


def add(a, b):
    return pl.pallas_call(
        add_kernel,
        out_shape=jax.ShapeDtypeStruct(a.shape, a.dtype),
        in_specs=[whole()] * 2,
        out_specs=whole(),
        compiler_params=params(),
        cost_estimate=cost(a.size, 6 * a.size),
        name="add_terms",
    )(a, b)


def span(start, size):
    if isinstance(start, int):
        return pl.ds(start, size)
    return pl.ds(pl.multiple_of(start * size, size), size)


ALL = slice(None)


def solution(mesh):
    n_seq = mesh.shape["seq"]
    n_head = mesh.shape["head"]

    def shards(queries, keys, values, d_out, w_out, doc_starts):
        rows = queries.shape[0]
        groups = keys.shape[1] // DH
        heads = queries.shape[1] // keys.shape[1]
        width = heads * DH
        docs = doc_starts.shape[0]
        team = groups
        layers = n_seq // team
        chunk = team * rows
        tile = 256 if chunk % 256 == 0 else rows
        me = lax.axis_index("seq")
        layer = me // team
        head = lax.axis_index("head")
        base = layer * chunk
        scal = jnp.concatenate([jnp.stack([base, base, me % team, head]), doc_starts])

        def half(*shape):
            return jax.ShapeDtypeStruct(shape, jnp.bfloat16)

        def swap(m, x):
            return lax.ppermute(x, "seq", [(i, i ^ m) for i in range(n_seq)])

        def swapped(parts):
            got = list(parts)
            for m in reversed(range(1, team)):
                got[m] = swap(m, parts[m])
            return got

        def shift(d, x):
            pairs = [(i, i + d * team) for i in range(n_seq) if 0 <= i + d * team < n_seq]
            return lax.ppermute(x, "seq", pairs)

        def pack(arrays, sizes, after=()):
            def kernel(scal, *refs):
                ins, outs = refs[: len(arrays)], refs[len(arrays) :]
                for m in range(team):
                    at = 0
                    for ref, size in zip(ins, sizes):
                        outs[m][:, at : at + size] = ref[:, span(scal[2] ^ m, size)]
                        at += size

            return ordered_call(
                kernel,
                scal,
                arrays,
                after,
                out_shape=[half(rows, sum(sizes))] * team,
                out_specs=[whole()] * team,
                name="pack_columns",
            )

        def stack(parts, name, after=()):
            def plan(place):
                return [(m, (ALL, ALL), 0, (span(place ^ m, rows), ALL)) for m in range(team)]

            return copies(scal, parts, [half(chunk, parts[0].shape[1])], plan, name, after)[0]

        def beside(parts, sizes, name):
            def plan(place):
                out = []
                for m in range(team):
                    at = 0
                    for b, size in enumerate(sizes):
                        out.append((m, (ALL, pl.ds(at, size)), b, (ALL, span(place ^ m, size))))
                        at += size
                return out

            shapes = [half(rows, team * size) for size in sizes]
            return copies(scal, parts, shapes, plan, name)

        if n_head == 2:
            d_far = lax.ppermute(d_out, "head", [(0, 1), (1, 0)])
        if team > 1:
            kv_sent = pack([keys, values], [DH, DH])
            kv_got = swapped(kv_sent)
            q_sent = pack([queries], [width], kv_sent[:1])
            q_got = swapped(q_sent)
            kv = stack(kv_got, "stack_keys_values", q_sent[:1])
        else:
            kv = jnp.concatenate([keys, values], axis=1)
        if n_head == 2:
            part = project(scal, d_out, w_out, None, False, team, jnp.float32, (kv,))
            token = (part,)
        else:
            token = ()
        if team > 1:
            q = stack(q_got, "stack_queries", token)
        else:
            q = queries
        state = stats(scal, docs, tile, 0, q, kv, None, token)
        if n_head == 2:
            g_parts = project(scal, d_far, w_out, part, True, team, jnp.bfloat16, state[:1])
        else:
            d_all = lax.all_gather(d_out, "head", axis=1, tiled=True)
            zero = jnp.zeros((rows, width * team), jnp.float32)
            g_parts = project(scal, d_all, w_out, zero, False, team, jnp.bfloat16)
        if team > 1:
            g_got = swapped(g_parts)

        def stack_g(after):
            if team > 1:
                return stack(g_got, "stack_attn_grad", after)
            return g_parts[0]

        if layers <= 4:
            kvs = [kv] + [shift(d, kv) for d in range(1, layers)]
            g = None
            for d in range(1, layers):
                state = stats(
                    scal, docs, tile, d, q, kvs[d], state, g_parts[:1] if g is None else (g,)
                )
                if g is None:
                    g = stack_g(state[:1])
            if g is None:
                g = stack_g(state[:1])
            log_total, delta = finish(g, *state)
            dq = None
            carried = None
            for d in reversed(range(1, layers)):
                dq, dkv = grads(scal, docs, tile, d, q, g, kvs[d], log_total, delta, dq)
                if carried is not None:
                    dkv = add(dkv, carried)
                carried = shift(-1, dkv)
            *dq_parts, dkv = grads(
                scal, docs, tile, 0, q, g, kv, log_total, delta, dq, team, jnp.float32
            )
            terms = [] if carried is None else [carried]
        else:
            rings = [[z * team + a for z in range(layers)] for a in range(team)]
            every = lax.all_gather(kv, "seq", axis_index_groups=rings)

            def chunk_at(d):
                return lax.dynamic_index_in_dim(every, jnp.maximum(layer - d, 0), 0, keepdims=False)

            def scalars(d):
                return scal - jnp.where(jnp.arange(scal.shape[0]) == 1, d * chunk, 0)

            def one(d, state):
                return tuple(stats(scalars(d), docs, tile, 0, q, chunk_at(d), state))

            state = lax.fori_loop(1, layers, one, tuple(state))
            g = stack_g(())
            log_total, delta = finish(g, *state)

            def two(d, carry):
                dq, total = carry
                dq, dkv = grads(
                    scalars(d), docs, tile, 0, q, g, chunk_at(d), log_total, delta, dq
                )
                place = jnp.maximum(layer - d, 0)
                old = lax.dynamic_index_in_dim(total, place, 0, keepdims=False)
                total = lax.dynamic_update_index_in_dim(
                    total, jnp.where(layer >= d, dkv, old), place, 0
                )
                return dq, total

            dq = jnp.zeros((width, chunk), jnp.float32)
            total = jnp.zeros((layers, chunk, 2 * DH), jnp.bfloat16)
            dq, total = lax.fori_loop(1, layers, two, (dq, total))
            *dq_parts, dkv = grads(
                scal, docs, tile, 0, q, g, kv, log_total, delta, dq, team, jnp.float32
            )
            terms = [
                lax.psum_scatter(
                    total.reshape(layers * chunk, 2 * DH), "seq", axis_index_groups=rings, tiled=True
                )
            ]

        def sum_kernel(scal, *refs):
            total = refs[0][...]
            for x in refs[1 : 1 + len(terms)]:
                total = total + x[...].astype(jnp.float32)
            full = refs[-1]
            full[...] = total.astype(jnp.bfloat16)
            for m in range(team):
                refs[1 + len(terms) + m][...] = full[span(scal[2] ^ m, rows), :]

        dkv_parts = pl.pallas_call(
            sum_kernel,
            out_shape=(half(rows, 2 * DH),) * team,
            in_specs=[whole(pltpu.SMEM)] + [whole()] * (1 + len(terms)),
            out_specs=(whole(),) * team,
            scratch_shapes=[pltpu.VMEM((chunk, 2 * DH), jnp.bfloat16)],
            compiler_params=params(),
            name="sum_terms",
        )(scal, dkv, *terms)
        if team > 1:
            dq_parts = swapped(dq_parts)
            dkv_parts = swapped(dkv_parts)
            (query_grad,) = beside(dq_parts, [width], "place_query_grad")
            key_grad, value_grad = beside(dkv_parts, [DH, DH], "place_key_value_grad")
        else:
            query_grad = dq_parts[0]
            key_grad = dkv_parts[0][:, :DH]
            value_grad = dkv_parts[0][:, DH:]
        return (query_grad, key_grad, value_grad)

    return jax.shard_map(
        shards,
        mesh=mesh,
        in_specs=(
            P("seq", "head"),
            P("seq", "head"),
            P("seq", "head"),
            P("seq", "head"),
            P("head", None),
            P(),
        ),
        out_specs=(P("seq", "head"), P("seq", "head"), P("seq", "head")),
        check_vma=False,
    )
```

```python
import functools
import math

import jax
import jax.numpy as jnp
from jax import lax
from jax.experimental import pallas as pl
from jax.experimental.pallas import tpu as pltpu
from jax.sharding import PartitionSpec as P

DH = 128
ONES = 16
LOG2E = 1.4426950408889634
NEG = -1e30
VMEM_LIMIT = 28 * 1024 * 1024
PROJECT_LIMIT = 52 * 1024 * 1024

NT = (((1,), (1,)), ((), ()))
NN = (((1,), (0,)), ((), ()))


def dot(a, b, dims):
    return lax.dot_general(a, b, dims, preferred_element_type=jnp.float32)


def params(limit=VMEM_LIMIT):
    return pltpu.CompilerParams(vmem_limit_bytes=limit)


def whole(memory_space=pltpu.VMEM):
    return pl.BlockSpec(memory_space=memory_space)


def ordered_call(kernel, scal, operands, after, **kwargs):
    count = len(after)

    def body(*refs):
        kernel(*refs[: 1 + len(operands)], *refs[1 + len(operands) + count :])

    specs = kwargs.pop("in_specs", [whole()] * len(operands))
    return pl.pallas_call(
        body,
        in_specs=[whole(pltpu.SMEM)] + specs + [whole(pl.ANY)] * count,
        compiler_params=params(),
        **kwargs,
    )(scal, *operands, *after)


def cost(flops, nbytes, exps=0):
    return pl.CostEstimate(flops=1024, bytes_accessed=1024, transcendentals=0)


FIRST_DOC = 4


def row_starts(scal, docs, pos):
    low = jnp.zeros_like(pos)
    for n in range(docs):
        low = jnp.where(pos >= scal[FIRST_DOC + n], scal[FIRST_DOC + n], low)
    return low


def doc_start_at(scal, docs, pos):
    low = jnp.int32(0)
    for n in range(docs):
        low = jnp.where(pos >= scal[FIRST_DOC + n], scal[FIRST_DOC + n], low)
    return low


def allowed(scal, docs, q0, k0, tq, tk):
    qpos = q0 + lax.broadcasted_iota(jnp.int32, (1, tq), 1)
    kpos = k0 + lax.broadcasted_iota(jnp.int32, (tk, 1), 0)
    return (kpos <= qpos) & (kpos >= row_starts(scal, docs, qpos))


def over_tiles(scal, docs, d, chunk, tile, body):
    tiles = chunk // tile

    def one(qo, ko, q0, tk, need):
        k0 = scal[1] - d * chunk + ko
        @pl.when(need)
        def _():
            body(qo, ko, tk, allowed(scal, docs, q0, k0, tile, tk))

    def step(qt, _):
        qo = pl.multiple_of(qt * tile, tile)
        q0 = scal[0] + qo
        low = doc_start_at(scal, docs, q0)
        k0 = scal[1] - d * chunk
        if tiles == 1:
            one(qo, 0, q0, tile, (k0 <= q0 + tile - 1) & (k0 + tile - 1 >= low))
            return 0
        all_of = (k0 + chunk - tile <= q0 + tile - 1) & (k0 + tile - 1 >= low)
        one(qo, 0, q0, chunk, all_of)

        @pl.when(jnp.logical_not(all_of))
        def _():
            def inner(kt, _):
                ko = pl.multiple_of(kt * tile, tile)
                need = (k0 + ko <= q0 + tile - 1) & (k0 + ko + tile - 1 >= low)
                one(qo, ko, q0, tile, need)
                return 0

            lax.fori_loop(0, tiles, inner, 0)

        return 0

    lax.fori_loop(0, tiles, step, 0)


def stats_kernel(docs, tile, heads, d, first, scal, q_ref, kv_ref, *refs):
    if first:
        m_ref, o_ref, vt_ref = refs
        m_ref[...] = jnp.full_like(m_ref, NEG)
        o_ref[...] = jnp.zeros_like(o_ref)
    else:
        m_in, o_in, m_ref, o_ref, vt_ref = refs
        m_ref[...] = m_in[...]
        o_ref[...] = o_in[...]
    chunk = q_ref.shape[0]
    factor = LOG2E / math.sqrt(DH)
    ext = DH + ONES
    vt_ref[:DH] = kv_ref[:, DH:].T
    vt_ref[DH:] = jnp.ones((vt_ref.shape[0] - DH, chunk), jnp.bfloat16)

    def body(qo, ko, tk, mask):
        k = kv_ref[pl.ds(ko, tk), :DH]
        vt = vt_ref[:ext, pl.ds(ko, tk)]
        rows = pl.ds(qo, tile)
        m_old = m_ref[:, rows]
        scores = [dot(k, q_ref[rows, h * DH : (h + 1) * DH], NT) for h in range(heads)]
        scores = [jnp.where(mask, s, NEG) for s in scores]
        tops = [jnp.max(s, axis=0, keepdims=True) for s in scores]
        m_new = jnp.maximum(m_old, factor * jnp.concatenate(tops, 0))
        alpha = jnp.exp2(m_old - m_new)
        m_ref[:, rows] = m_new
        for h in range(heads):
            p = jnp.exp2(scores[h] * factor - m_new[h : h + 1]).astype(jnp.bfloat16)
            part = slice(h * ext, (h + 1) * ext)
            o_ref[part, rows] = alpha[h : h + 1] * o_ref[part, rows] + dot(vt, p, NN)

    over_tiles(scal, docs, d, chunk, tile, body)


def stats(scal, docs, tile, d, q, kv, state, after=()):
    chunk, width = q.shape
    heads = width // DH
    shapes = (
        jax.ShapeDtypeStruct((heads, chunk), jnp.float32),
        jax.ShapeDtypeStruct((heads * (DH + ONES), chunk), jnp.float32),
    )
    first = state is None
    extra = () if first else state
    return ordered_call(
        functools.partial(stats_kernel, docs, tile, heads, d, first),
        scal,
        (q, kv, *extra),
        after,
        out_shape=shapes,
        out_specs=(whole(),) * 2,
        scratch_shapes=[pltpu.VMEM((DH + ONES, chunk), jnp.bfloat16)],
        cost_estimate=cost(4 * chunk * chunk * width, 12 * chunk * width, chunk * chunk * heads),
        name="row_stats",
    )


def finish_kernel(heads, g_ref, m_ref, o_ref, log_ref, delta_ref):
    ext = DH + ONES
    for h in range(heads):
        total = o_ref[h * ext + DH : h * ext + DH + 1, :]
        gt = g_ref[:, h * DH : (h + 1) * DH].T.astype(jnp.float32)
        part = jnp.sum(gt * o_ref[h * ext : h * ext + DH, :], axis=0, keepdims=True)
        log_ref[h : h + 1, :] = m_ref[h : h + 1, :] + jnp.log2(total)
        delta_ref[h : h + 1, :] = part / total


def finish(g, m, o):
    heads, chunk = m.shape
    shape = jax.ShapeDtypeStruct((heads, chunk), jnp.float32)
    return pl.pallas_call(
        functools.partial(finish_kernel, heads),
        out_shape=(shape, shape),
        in_specs=[whole()] * 3,
        out_specs=(whole(),) * 2,
        compiler_params=params(),
        cost_estimate=cost(2 * chunk * heads * DH, 6 * chunk * heads * DH),
        name="row_delta",
    )(g, m, o)


def grads_kernel(
    docs, tile, heads, d, first, team, scal, q_ref, g_ref, kv_ref, log_ref, delta_ref, *refs
):
    refs = list(refs)
    dq_in = None if first else refs.pop(0)
    acc_ref, kt_ref = refs.pop(), refs.pop()
    dkv_ref = refs.pop()
    last = team is not None
    if last:
        full_ref = acc_ref
        acc_ref, dq_ref = refs.pop(), refs.pop()
        outs = refs
    else:
        dq_ref = refs.pop()
    chunk = q_ref.shape[0]
    scaling = 1.0 / math.sqrt(DH)
    factor = LOG2E * scaling
    if first:
        dq_ref[...] = jnp.zeros_like(dq_ref)
    else:
        dq_ref[...] = dq_in[...]
    acc_ref[...] = jnp.zeros_like(acc_ref)
    kt_ref[...] = kv_ref[:, :DH].T

    def body(qo, ko, tk, mask):
        rows = pl.ds(qo, tile)
        keys = pl.ds(ko, tk)
        k = kv_ref[keys, :DH]
        v = kv_ref[keys, DH:]
        qs = [q_ref[rows, h * DH : (h + 1) * DH] for h in range(heads)]
        gs = [g_ref[rows, h * DH : (h + 1) * DH] for h in range(heads)]
        scores = [dot(k, q, NT) for q in qs]
        dots = [dot(v, g, NT) for g in gs]
        scores = [jnp.where(mask, s, NEG) for s in scores]
        probs = [
            jnp.exp2(scores[h] * factor - log_ref[h : h + 1, rows]) for h in range(heads)
        ]
        ds = [
            (probs[h] * (dots[h] - delta_ref[h : h + 1, rows])).astype(jnp.bfloat16)
            for h in range(heads)
        ]
        probs = [p.astype(jnp.bfloat16) for p in probs]
        dv = dot(jnp.concatenate(probs, 1), jnp.concatenate(gs, 0), NN)
        dk = dot(jnp.concatenate(ds, 1), jnp.concatenate(qs, 0), NN)
        kt = kt_ref[:, keys]
        for h in range(heads):
            dq_ref[h * DH : (h + 1) * DH, rows] += dot(kt, ds[h], NN)
        acc_ref[keys, :DH] += dk
        acc_ref[keys, DH:] += dv

    over_tiles(scal, docs, d, chunk, tile, body)
    dkv_ref[:, :DH] = (acc_ref[:, :DH] * scaling).astype(dkv_ref.dtype)
    dkv_ref[:, DH:] = acc_ref[:, DH:].astype(dkv_ref.dtype)
    if last:
        for h in range(heads):
            full_ref[:, h * DH : (h + 1) * DH] = (
                (dq_ref[h * DH : (h + 1) * DH, :] * scaling).T.astype(jnp.bfloat16)
            )
        size = chunk // team
        for m in range(team):
            outs[m][...] = full_ref[pl.ds(pl.multiple_of((scal[2] ^ m) * size, size), size), :]


def grads(
    scal, docs, tile, d, q, g, kv, log_total, delta, dq, team=None, dtype=jnp.bfloat16, after=()
):
    chunk, width = q.shape
    heads = width // DH
    first = dq is None
    extra = () if first else (dq,)
    dkv_shape = jax.ShapeDtypeStruct((chunk, 2 * DH), dtype)
    scratch = [pltpu.VMEM((DH, chunk), jnp.bfloat16)]
    dq_rows = pltpu.VMEM((width, chunk), jnp.float32)
    acc = pltpu.VMEM((chunk, 2 * DH), jnp.float32)
    if team is None:
        shapes = (jax.ShapeDtypeStruct((width, chunk), jnp.float32), dkv_shape)
        scratch = scratch + [acc]
        kernel = functools.partial(grads_kernel, docs, tile, heads, d, first, None)
    else:
        shapes = (jax.ShapeDtypeStruct((chunk // team, width), jnp.bfloat16),) * team + (dkv_shape,)
        scratch = [dq_rows, acc] + scratch + [pltpu.VMEM((chunk, width), jnp.bfloat16)]

        def kernel(*refs):
            refs = list(refs)
            full, kt, acc_ref, dq_ref = refs.pop(), refs.pop(), refs.pop(), refs.pop()
            dkv_ref = refs.pop()
            refs = refs + [dq_ref, acc_ref, dkv_ref, kt, full]
            grads_kernel(docs, tile, heads, d, first, team, *refs)

    return ordered_call(
        kernel,
        scal,
        (q, g, kv, log_total, delta, *extra),
        after,
        out_shape=shapes,
        out_specs=(whole(),) * len(shapes),
        scratch_shapes=scratch,
        cost_estimate=cost(10 * chunk * chunk * width, 12 * chunk * width, chunk * chunk * heads),
        name="pair_grads",
    )


def project(scal, d, w, parts, far, blocks, begin, count, after=()):
    rows, depth = d.shape
    wide = w.shape[0] // blocks
    split = w.shape[1] // depth
    each = 0 if not parts else parts[0].shape[1] // wide

    def kernel(*refs):
        scal, d_ref, w_ref = refs[:3]
        total = dot(d_ref[...], w_ref[...], NT)
        if not parts:
            refs[-1][...] = total
            return
        outs = refs[3 + len(parts) + len(after) :]
        for m in range(count):

            @pl.when(pl.program_id(0) == m)
            def _():
                outs[m][...] = (total + refs[3 + m // each][...]).astype(outs[m].dtype)

    def column(s):
        if split == 1:
            return 0
        return 1 - s[3] if far else s[3]

    def part_spec(p):
        return pl.BlockSpec((rows, wide), lambda i, s: (0, jnp.clip(i - p * each, 0, each - 1)))

    w_spec = pl.BlockSpec((wide, depth), lambda i, s: (s[2] ^ (i + begin), column(s)))
    if parts:
        out_shape = (jax.ShapeDtypeStruct((rows, wide), jnp.bfloat16),) * count
        out_specs = (pl.BlockSpec((rows, wide), lambda i, s: (0, 0)),) * count
    else:
        out_shape = jax.ShapeDtypeStruct((rows, wide * count), jnp.float32)
        out_specs = pl.BlockSpec((rows, wide), lambda i, s: (0, i))
    grid_spec = pltpu.PrefetchScalarGridSpec(
        num_scalar_prefetch=1,
        grid=(count,),
        in_specs=[pl.BlockSpec((rows, depth), lambda i, s: (0, 0)), w_spec]
        + [part_spec(p) for p in range(len(parts))]
        + [whole(pl.ANY)] * len(after),
        out_specs=out_specs,
    )
    return pl.pallas_call(
        kernel,
        out_shape=out_shape,
        grid_spec=grid_spec,
        compiler_params=params(PROJECT_LIMIT),
        cost_estimate=cost(2 * rows * depth * wide * count, 2 * depth * wide * count),
        name="project",
    )(scal, d, w, *parts, *after)


def copies(scal, inputs, out_shapes, plan, name, after=()):
    n_in = len(inputs)

    def kernel(scal, *refs):
        ins, outs, sems = refs[:n_in], refs[n_in:-1], refs[-1]
        started = []
        for i, (a, src, b, dst) in enumerate(plan(scal[2])):
            copy = pltpu.make_async_copy(ins[a].at[src], outs[b].at[dst], sems.at[i])
            copy.start()
            started.append(copy)
        for copy in started:
            copy.wait()

    count = len(plan(0))
    size = sum(math.prod(s.shape) * 2 for s in out_shapes)
    return ordered_call(
        kernel,
        scal,
        inputs,
        after,
        out_shape=tuple(out_shapes),
        in_specs=[whole(pl.ANY)] * n_in,
        out_specs=(whole(pl.ANY),) * len(out_shapes),
        scratch_shapes=[pltpu.SemaphoreType.DMA((count,))],
        cost_estimate=cost(0, 2 * size),
        name=name,
    )


def add_kernel(a_ref, b_ref, out_ref):
    total = a_ref[...].astype(jnp.float32) + b_ref[...].astype(jnp.float32)
    out_ref[...] = total.astype(out_ref.dtype)


def add(a, b):
    return pl.pallas_call(
        add_kernel,
        out_shape=jax.ShapeDtypeStruct(a.shape, a.dtype),
        in_specs=[whole()] * 2,
        out_specs=whole(),
        compiler_params=params(),
        cost_estimate=cost(a.size, 6 * a.size),
        name="add_terms",
    )(a, b)


def span(start, size):
    if isinstance(start, int):
        return pl.ds(start, size)
    return pl.ds(pl.multiple_of(start * size, size), size)


ALL = slice(None)


def solution(mesh):
    n_seq = mesh.shape["seq"]
    n_head = mesh.shape["head"]

    def shards(queries, keys, values, d_out, w_out, doc_starts):
        rows = queries.shape[0]
        groups = keys.shape[1] // DH
        heads = queries.shape[1] // keys.shape[1]
        width = heads * DH
        docs = doc_starts.shape[0]
        team = groups
        layers = n_seq // team
        chunk = team * rows
        tile = 256 if chunk % 256 == 0 else rows
        me = lax.axis_index("seq")
        layer = me // team
        head = lax.axis_index("head")
        base = layer * chunk
        scal = jnp.concatenate([jnp.stack([base, base, me % team, head]), doc_starts])

        def half(*shape):
            return jax.ShapeDtypeStruct(shape, jnp.bfloat16)

        def swap(m, x):
            return lax.ppermute(x, "seq", [(i, i ^ m) for i in range(n_seq)])

        def swapped(parts):
            got = list(parts)
            for m in reversed(range(1, team)):
                got[m] = swap(m, parts[m])
            return got

        def shift(d, x):
            pairs = [(i, i + d * team) for i in range(n_seq) if 0 <= i + d * team < n_seq]
            return lax.ppermute(x, "seq", pairs)

        def pack(arrays, sizes, after=()):
            def kernel(scal, *refs):
                ins, outs = refs[: len(arrays)], refs[len(arrays) :]
                for m in range(team):
                    at = 0
                    for ref, size in zip(ins, sizes):
                        outs[m][:, at : at + size] = ref[:, span(scal[2] ^ m, size)]
                        at += size

            return ordered_call(
                kernel,
                scal,
                arrays,
                after,
                out_shape=[half(rows, sum(sizes))] * team,
                out_specs=[whole()] * team,
                name="pack_columns",
            )

        def stack(parts, sizes, name, after=()):
            def plan(place):
                out = []
                for m in range(team):
                    at = 0
                    for b, size in enumerate(sizes):
                        out.append((m, (ALL, pl.ds(at, size)), b, (span(place ^ m, rows), ALL)))
                        at += size
                return out

            return copies(scal, parts, [half(chunk, size) for size in sizes], plan, name, after)

        def beside(parts, sizes, name):
            def plan(place):
                out = []
                for m in range(team):
                    at = 0
                    for b, size in enumerate(sizes):
                        out.append((m, (ALL, pl.ds(at, size)), b, (ALL, span(place ^ m, size))))
                        at += size
                return out

            shapes = [half(rows, team * size) for size in sizes]
            return copies(scal, parts, shapes, plan, name)

        if n_head == 2:
            d_far = lax.ppermute(d_out, "head", [(0, 1), (1, 0)])
        if team > 1:
            sent = pack([queries, keys, values], [width, DH, DH])
            got = swapped(sent)
            near = []
            if n_head == 2:
                near.append(project(scal, d_out, w_out, (), False, team, 0, team, sent[:1]))
            q, kv = stack(got, [width, 2 * DH], "stack_rows", near)
            order = (q,)
        else:
            kv = jnp.concatenate([keys, values], axis=1)
            near = [project(scal, d_out, w_out, (), False, 1, 0, 1)] if n_head == 2 else []
            q = queries
            order = ()
        if n_head == 2:
            g_parts = project(scal, d_far, w_out, near, True, team, 0, team, order)
        else:
            d_all = lax.all_gather(d_out, "head", axis=1, tiled=True)
            zero = jnp.zeros((rows, width * team), jnp.float32)
            g_parts = project(scal, d_all, w_out, [zero], False, team, 0, team, order)
        if team > 1:
            g_got = swapped(g_parts)
        state = stats(scal, docs, tile, 0, q, kv, None, g_parts[:1])

        def stack_g(after):
            if team > 1:
                return stack(g_got, [width], "stack_attn_grad", after)[0]
            return g_parts[0]

        if layers <= 4:
            kvs = [kv] + [shift(d, kv) for d in range(1, layers)]
            g = None
            for d in range(1, layers):
                state = stats(
                    scal, docs, tile, d, q, kvs[d], state, g_parts[:1] if g is None else (g,)
                )
                if g is None:
                    g = stack_g(state[:1])
            if g is None:
                g = stack_g(state[:1])
            log_total, delta = finish(g, *state)
            dq = None
            carried = None
            for d in reversed(range(1, layers)):
                dq, dkv = grads(scal, docs, tile, d, q, g, kvs[d], log_total, delta, dq)
                if carried is not None:
                    dkv = add(dkv, carried)
                carried = shift(-1, dkv)
            *dq_parts, dkv = grads(
                scal, docs, tile, 0, q, g, kv, log_total, delta, dq, team, jnp.float32
            )
            terms = [] if carried is None else [carried]
        else:
            rings = [[z * team + a for z in range(layers)] for a in range(team)]
            every = lax.all_gather(kv, "seq", axis_index_groups=rings)

            def chunk_at(d):
                return lax.dynamic_index_in_dim(every, jnp.maximum(layer - d, 0), 0, keepdims=False)

            def scalars(d):
                return scal - jnp.where(jnp.arange(scal.shape[0]) == 1, d * chunk, 0)

            def one(d, state):
                return tuple(stats(scalars(d), docs, tile, 0, q, chunk_at(d), state))

            state = lax.fori_loop(1, layers, one, tuple(state))
            g = stack_g(())
            log_total, delta = finish(g, *state)

            def two(d, carry):
                dq, total = carry
                dq, dkv = grads(
                    scalars(d), docs, tile, 0, q, g, chunk_at(d), log_total, delta, dq
                )
                place = jnp.maximum(layer - d, 0)
                old = lax.dynamic_index_in_dim(total, place, 0, keepdims=False)
                total = lax.dynamic_update_index_in_dim(
                    total, jnp.where(layer >= d, dkv, old), place, 0
                )
                return dq, total

            dq = jnp.zeros((width, chunk), jnp.float32)
            total = jnp.zeros((layers, chunk, 2 * DH), jnp.bfloat16)
            dq, total = lax.fori_loop(1, layers, two, (dq, total))
            *dq_parts, dkv = grads(
                scal, docs, tile, 0, q, g, kv, log_total, delta, dq, team, jnp.float32
            )
            terms = [
                lax.psum_scatter(
                    total.reshape(layers * chunk, 2 * DH), "seq", axis_index_groups=rings, tiled=True
                )
            ]

        def sum_kernel(scal, *refs):
            total = refs[0][...]
            for x in refs[1 : 1 + len(terms)]:
                total = total + x[...].astype(jnp.float32)
            full = refs[-1]
            full[...] = total.astype(jnp.bfloat16)
            for m in range(team):
                refs[1 + len(terms) + m][...] = full[span(scal[2] ^ m, rows), :]

        dkv_parts = pl.pallas_call(
            sum_kernel,
            out_shape=(half(rows, 2 * DH),) * team,
            in_specs=[whole(pltpu.SMEM)] + [whole()] * (1 + len(terms)),
            out_specs=(whole(),) * team,
            scratch_shapes=[pltpu.VMEM((chunk, 2 * DH), jnp.bfloat16)],
            compiler_params=params(),
            name="sum_terms",
        )(scal, dkv, *terms)
        if team > 1:
            dq_parts = swapped(dq_parts)
            dkv_parts = swapped(dkv_parts)
            (query_grad,) = beside(dq_parts, [width], "place_query_grad")
            key_grad, value_grad = beside(dkv_parts, [DH, DH], "place_key_value_grad")
        else:
            query_grad = dq_parts[0]
            key_grad = dkv_parts[0][:, :DH]
            value_grad = dkv_parts[0][:, DH:]
        return (query_grad, key_grad, value_grad)

    return jax.shard_map(
        shards,
        mesh=mesh,
        in_specs=(
            P("seq", "head"),
            P("seq", "head"),
            P("seq", "head"),
            P("seq", "head"),
            P("head", None),
            P(),
        ),
        out_specs=(P("seq", "head"), P("seq", "head"), P("seq", "head")),
        check_vma=False,
    )
```

```python
import functools
import math

import jax
import jax.numpy as jnp
from jax import lax
from jax.experimental import pallas as pl
from jax.experimental.pallas import tpu as pltpu
from jax.sharding import PartitionSpec as P

DH = 128
ONES = 16
LOG2E = 1.4426950408889634
NEG = -1e30
VMEM_LIMIT = 28 * 1024 * 1024
PROJECT_LIMIT = 52 * 1024 * 1024

NT = (((1,), (1,)), ((), ()))
NN = (((1,), (0,)), ((), ()))


def dot(a, b, dims):
    return lax.dot_general(a, b, dims, preferred_element_type=jnp.float32)


def params(limit=VMEM_LIMIT):
    return pltpu.CompilerParams(vmem_limit_bytes=limit)


def whole(memory_space=pltpu.VMEM):
    return pl.BlockSpec(memory_space=memory_space)


def ordered_call(kernel, scal, operands, after, **kwargs):
    count = len(after)

    def body(*refs):
        kernel(*refs[: 1 + len(operands)], *refs[1 + len(operands) + count :])

    specs = kwargs.pop("in_specs", [whole()] * len(operands))
    return pl.pallas_call(
        body,
        in_specs=[whole(pltpu.SMEM)] + specs + [whole(pl.ANY)] * count,
        compiler_params=params(),
        **kwargs,
    )(scal, *operands, *after)


def cost(flops, nbytes, exps=0):
    return pl.CostEstimate(flops=1024, bytes_accessed=1024, transcendentals=0)


FIRST_DOC = 4


def row_starts(scal, docs, pos):
    low = jnp.zeros_like(pos)
    for n in range(docs):
        low = jnp.where(pos >= scal[FIRST_DOC + n], scal[FIRST_DOC + n], low)
    return low


def doc_start_at(scal, docs, pos):
    low = jnp.int32(0)
    for n in range(docs):
        low = jnp.where(pos >= scal[FIRST_DOC + n], scal[FIRST_DOC + n], low)
    return low


def allowed(scal, docs, q0, k0, tq, tk):
    qpos = q0 + lax.broadcasted_iota(jnp.int32, (1, tq), 1)
    kpos = k0 + lax.broadcasted_iota(jnp.int32, (tk, 1), 0)
    return (kpos <= qpos) & (kpos >= row_starts(scal, docs, qpos))


def over_tiles(scal, docs, d, chunk, tile, body):
    tiles = chunk // tile

    def one(qo, ko, q0, tk, need):
        k0 = scal[1] - d * chunk + ko
        @pl.when(need)
        def _():
            body(qo, ko, tk, allowed(scal, docs, q0, k0, tile, tk))

    def step(qt, _):
        qo = pl.multiple_of(qt * tile, tile)
        q0 = scal[0] + qo
        low = doc_start_at(scal, docs, q0)
        k0 = scal[1] - d * chunk
        if tiles == 1:
            one(qo, 0, q0, tile, (k0 <= q0 + tile - 1) & (k0 + tile - 1 >= low))
            return 0
        all_of = (k0 + chunk - tile <= q0 + tile - 1) & (k0 + tile - 1 >= low)
        one(qo, 0, q0, chunk, all_of)

        @pl.when(jnp.logical_not(all_of))
        def _():
            def inner(kt, _):
                ko = pl.multiple_of(kt * tile, tile)
                need = (k0 + ko <= q0 + tile - 1) & (k0 + ko + tile - 1 >= low)
                one(qo, ko, q0, tile, need)
                return 0

            lax.fori_loop(0, tiles, inner, 0)

        return 0

    lax.fori_loop(0, tiles, step, 0)


def stats_kernel(docs, tile, heads, d, first, scal, q_ref, kv_ref, *refs):
    if first:
        m_ref, o_ref, vt_ref = refs
        m_ref[...] = jnp.full_like(m_ref, NEG)
        o_ref[...] = jnp.zeros_like(o_ref)
    else:
        m_in, o_in, m_ref, o_ref, vt_ref = refs
        m_ref[...] = m_in[...]
        o_ref[...] = o_in[...]
    chunk = q_ref.shape[0]
    factor = LOG2E / math.sqrt(DH)
    ext = DH + ONES
    vt_ref[:DH] = kv_ref[:, DH:].T
    vt_ref[DH:] = jnp.ones((vt_ref.shape[0] - DH, chunk), jnp.bfloat16)

    def body(qo, ko, tk, mask):
        k = kv_ref[pl.ds(ko, tk), :DH]
        vt = vt_ref[:ext, pl.ds(ko, tk)]
        rows = pl.ds(qo, tile)
        m_old = m_ref[:, rows]
        scores = [dot(k, q_ref[rows, h * DH : (h + 1) * DH], NT) for h in range(heads)]
        scores = [jnp.where(mask, s, NEG) for s in scores]
        tops = [jnp.max(s, axis=0, keepdims=True) for s in scores]
        m_new = jnp.maximum(m_old, factor * jnp.concatenate(tops, 0))
        alpha = jnp.exp2(m_old - m_new)
        m_ref[:, rows] = m_new
        for h in range(heads):
            p = jnp.exp2(scores[h] * factor - m_new[h : h + 1]).astype(jnp.bfloat16)
            part = slice(h * ext, (h + 1) * ext)
            o_ref[part, rows] = alpha[h : h + 1] * o_ref[part, rows] + dot(vt, p, NN)

    over_tiles(scal, docs, d, chunk, tile, body)


def stats(scal, docs, tile, d, q, kv, state, after=()):
    chunk, width = q.shape
    heads = width // DH
    shapes = (
        jax.ShapeDtypeStruct((heads, chunk), jnp.float32),
        jax.ShapeDtypeStruct((heads * (DH + ONES), chunk), jnp.float32),
    )
    first = state is None
    extra = () if first else state
    return ordered_call(
        functools.partial(stats_kernel, docs, tile, heads, d, first),
        scal,
        (q, kv, *extra),
        after,
        out_shape=shapes,
        out_specs=(whole(),) * 2,
        scratch_shapes=[pltpu.VMEM((DH + ONES, chunk), jnp.bfloat16)],
        cost_estimate=cost(4 * chunk * chunk * width, 12 * chunk * width, chunk * chunk * heads),
        name="row_stats",
    )


def finish_kernel(heads, g_ref, m_ref, o_ref, log_ref, delta_ref):
    ext = DH + ONES
    for h in range(heads):
        total = o_ref[h * ext + DH : h * ext + DH + 1, :]
        gt = g_ref[:, h * DH : (h + 1) * DH].T.astype(jnp.float32)
        part = jnp.sum(gt * o_ref[h * ext : h * ext + DH, :], axis=0, keepdims=True)
        log_ref[h : h + 1, :] = m_ref[h : h + 1, :] + jnp.log2(total)
        delta_ref[h : h + 1, :] = part / total


def finish(g, m, o):
    heads, chunk = m.shape
    shape = jax.ShapeDtypeStruct((heads, chunk), jnp.float32)
    return pl.pallas_call(
        functools.partial(finish_kernel, heads),
        out_shape=(shape, shape),
        in_specs=[whole()] * 3,
        out_specs=(whole(),) * 2,
        compiler_params=params(),
        cost_estimate=cost(2 * chunk * heads * DH, 6 * chunk * heads * DH),
        name="row_delta",
    )(g, m, o)


def grads_kernel(
    docs, tile, heads, d, first, team, scal, q_ref, g_ref, kv_ref, log_ref, delta_ref, *refs
):
    refs = list(refs)
    dq_in = None if first else refs.pop(0)
    acc_ref, kt_ref = refs.pop(), refs.pop()
    dkv_ref = refs.pop()
    last = team is not None
    if last:
        full_ref = acc_ref
        acc_ref, dq_ref = refs.pop(), refs.pop()
        outs = refs
    else:
        dq_ref = refs.pop()
    chunk = q_ref.shape[0]
    scaling = 1.0 / math.sqrt(DH)
    factor = LOG2E * scaling
    if first:
        dq_ref[...] = jnp.zeros_like(dq_ref)
    else:
        dq_ref[...] = dq_in[...]
    acc_ref[...] = jnp.zeros_like(acc_ref)
    kt_ref[...] = kv_ref[:, :DH].T

    def body(qo, ko, tk, mask):
        rows = pl.ds(qo, tile)
        keys = pl.ds(ko, tk)
        k = kv_ref[keys, :DH]
        v = kv_ref[keys, DH:]
        qs = [q_ref[rows, h * DH : (h + 1) * DH] for h in range(heads)]
        gs = [g_ref[rows, h * DH : (h + 1) * DH] for h in range(heads)]
        scores = [dot(k, q, NT) for q in qs]
        dots = [dot(v, g, NT) for g in gs]
        scores = [jnp.where(mask, s, NEG) for s in scores]
        probs = [
            jnp.exp2(scores[h] * factor - log_ref[h : h + 1, rows]) for h in range(heads)
        ]
        ds = [
            (probs[h] * (dots[h] - delta_ref[h : h + 1, rows])).astype(jnp.bfloat16)
            for h in range(heads)
        ]
        probs = [p.astype(jnp.bfloat16) for p in probs]
        dv = dot(jnp.concatenate(probs, 1), jnp.concatenate(gs, 0), NN)
        dk = dot(jnp.concatenate(ds, 1), jnp.concatenate(qs, 0), NN)
        kt = kt_ref[:, keys]
        for h in range(heads):
            dq_ref[h * DH : (h + 1) * DH, rows] += dot(kt, ds[h], NN)
        acc_ref[keys, :DH] += dk
        acc_ref[keys, DH:] += dv

    over_tiles(scal, docs, d, chunk, tile, body)
    dkv_ref[:, :DH] = (acc_ref[:, :DH] * scaling).astype(dkv_ref.dtype)
    dkv_ref[:, DH:] = acc_ref[:, DH:].astype(dkv_ref.dtype)
    if last:
        for h in range(heads):
            full_ref[:, h * DH : (h + 1) * DH] = (
                (dq_ref[h * DH : (h + 1) * DH, :] * scaling).T.astype(jnp.bfloat16)
            )
        size = chunk // team
        for m in range(team):
            outs[m][...] = full_ref[pl.ds(pl.multiple_of((scal[2] ^ m) * size, size), size), :]


def grads(
    scal, docs, tile, d, q, g, kv, log_total, delta, dq, team=None, dtype=jnp.bfloat16, after=()
):
    chunk, width = q.shape
    heads = width // DH
    first = dq is None
    extra = () if first else (dq,)
    dkv_shape = jax.ShapeDtypeStruct((chunk, 2 * DH), dtype)
    scratch = [pltpu.VMEM((DH, chunk), jnp.bfloat16)]
    dq_rows = pltpu.VMEM((width, chunk), jnp.float32)
    acc = pltpu.VMEM((chunk, 2 * DH), jnp.float32)
    if team is None:
        shapes = (jax.ShapeDtypeStruct((width, chunk), jnp.float32), dkv_shape)
        scratch = scratch + [acc]
        kernel = functools.partial(grads_kernel, docs, tile, heads, d, first, None)
    else:
        shapes = (jax.ShapeDtypeStruct((chunk // team, width), jnp.bfloat16),) * team + (dkv_shape,)
        scratch = [dq_rows, acc] + scratch + [pltpu.VMEM((chunk, width), jnp.bfloat16)]

        def kernel(*refs):
            refs = list(refs)
            full, kt, acc_ref, dq_ref = refs.pop(), refs.pop(), refs.pop(), refs.pop()
            dkv_ref = refs.pop()
            refs = refs + [dq_ref, acc_ref, dkv_ref, kt, full]
            grads_kernel(docs, tile, heads, d, first, team, *refs)

    return ordered_call(
        kernel,
        scal,
        (q, g, kv, log_total, delta, *extra),
        after,
        out_shape=shapes,
        out_specs=(whole(),) * len(shapes),
        scratch_shapes=scratch,
        cost_estimate=cost(10 * chunk * chunk * width, 12 * chunk * width, chunk * chunk * heads),
        name="pair_grads",
    )


def project(scal, d, w, parts, far, blocks, begin, count, after=()):
    rows, depth = d.shape
    wide = w.shape[0] // blocks
    split = w.shape[1] // depth
    each = 0 if not parts else parts[0].shape[1] // wide

    def kernel(*refs):
        scal, d_ref, w_ref = refs[:3]
        total = dot(d_ref[...], w_ref[...], NT)
        if not parts:
            refs[-1][...] = total
            return
        outs = refs[3 + len(parts) + len(after) :]
        for m in range(count):

            @pl.when(pl.program_id(0) == m)
            def _():
                outs[m][...] = (total + refs[3 + m // each][...]).astype(outs[m].dtype)

    def column(s):
        if split == 1:
            return 0
        return 1 - s[3] if far else s[3]

    def part_spec(p):
        return pl.BlockSpec((rows, wide), lambda i, s: (0, jnp.clip(i - p * each, 0, each - 1)))

    w_spec = pl.BlockSpec((wide, depth), lambda i, s: (s[2] ^ (i + begin), column(s)))
    if parts:
        out_shape = (jax.ShapeDtypeStruct((rows, wide), jnp.bfloat16),) * count
        out_specs = (pl.BlockSpec((rows, wide), lambda i, s: (0, 0)),) * count
    else:
        out_shape = jax.ShapeDtypeStruct((rows, wide * count), jnp.float32)
        out_specs = pl.BlockSpec((rows, wide), lambda i, s: (0, i))
    grid_spec = pltpu.PrefetchScalarGridSpec(
        num_scalar_prefetch=1,
        grid=(count,),
        in_specs=[pl.BlockSpec((rows, depth), lambda i, s: (0, 0)), w_spec]
        + [part_spec(p) for p in range(len(parts))]
        + [whole(pl.ANY)] * len(after),
        out_specs=out_specs,
    )
    return pl.pallas_call(
        kernel,
        out_shape=out_shape,
        grid_spec=grid_spec,
        compiler_params=params(PROJECT_LIMIT),
        cost_estimate=cost(2 * rows * depth * wide * count, 2 * depth * wide * count),
        name="project",
    )(scal, d, w, *parts, *after)


def copies(scal, inputs, out_shapes, plan, name, after=()):
    n_in = len(inputs)

    def kernel(scal, *refs):
        ins, outs, sems = refs[:n_in], refs[n_in:-1], refs[-1]
        started = []
        for i, (a, src, b, dst) in enumerate(plan(scal[2])):
            copy = pltpu.make_async_copy(ins[a].at[src], outs[b].at[dst], sems.at[i])
            copy.start()
            started.append(copy)
        for copy in started:
            copy.wait()

    count = len(plan(0))
    size = sum(math.prod(s.shape) * 2 for s in out_shapes)
    return ordered_call(
        kernel,
        scal,
        inputs,
        after,
        out_shape=tuple(out_shapes),
        in_specs=[whole(pl.ANY)] * n_in,
        out_specs=(whole(pl.ANY),) * len(out_shapes),
        scratch_shapes=[pltpu.SemaphoreType.DMA((count,))],
        cost_estimate=cost(0, 2 * size),
        name=name,
    )


def add_kernel(a_ref, b_ref, out_ref):
    total = a_ref[...].astype(jnp.float32) + b_ref[...].astype(jnp.float32)
    out_ref[...] = total.astype(out_ref.dtype)


def add(a, b):
    return pl.pallas_call(
        add_kernel,
        out_shape=jax.ShapeDtypeStruct(a.shape, a.dtype),
        in_specs=[whole()] * 2,
        out_specs=whole(),
        compiler_params=params(),
        cost_estimate=cost(a.size, 6 * a.size),
        name="add_terms",
    )(a, b)


def span(start, size):
    if isinstance(start, int):
        return pl.ds(start, size)
    return pl.ds(pl.multiple_of(start * size, size), size)


ALL = slice(None)


def solution(mesh):
    n_seq = mesh.shape["seq"]
    n_head = mesh.shape["head"]

    def shards(*args):
        doc_starts = args[-1]
        layers = n_seq // (args[1].shape[1] // DH)
        chunk = args[0].shape[0] * n_seq // layers
        if layers > 4 or layers < 3:
            return part_of(layers - 1, *args)
        total = jnp.full((1,), chunk * layers, doc_starts.dtype)
        ends = jnp.concatenate([doc_starts[1:], total]) - 1
        reach = jnp.max(ends // chunk - doc_starts // chunk)
        branches = [functools.partial(part_of, r) for r in range(1, layers)]
        return lax.switch(jnp.clip(reach - 1, 0, layers - 2), branches, *args)

    def part_of(reach, queries, keys, values, d_out, w_out, doc_starts):
        rows = queries.shape[0]
        groups = keys.shape[1] // DH
        heads = queries.shape[1] // keys.shape[1]
        width = heads * DH
        docs = doc_starts.shape[0]
        team = groups
        layers = n_seq // team
        chunk = team * rows
        tile = 256 if chunk % 256 == 0 else rows
        me = lax.axis_index("seq")
        layer = me // team
        head = lax.axis_index("head")
        base = layer * chunk
        scal = jnp.concatenate([jnp.stack([base, base, me % team, head]), doc_starts])

        def half(*shape):
            return jax.ShapeDtypeStruct(shape, jnp.bfloat16)

        def swap(m, x):
            return lax.ppermute(x, "seq", [(i, i ^ m) for i in range(n_seq)])

        def swapped(parts):
            got = list(parts)
            for m in reversed(range(1, team)):
                got[m] = swap(m, parts[m])
            return got

        def shift(d, x):
            pairs = [(i, i + d * team) for i in range(n_seq) if 0 <= i + d * team < n_seq]
            return lax.ppermute(x, "seq", pairs)

        def pack(arrays, sizes, after=()):
            def kernel(scal, *refs):
                ins, outs = refs[: len(arrays)], refs[len(arrays) :]
                for m in range(team):
                    at = 0
                    for ref, size in zip(ins, sizes):
                        outs[m][:, at : at + size] = ref[:, span(scal[2] ^ m, size)]
                        at += size

            return ordered_call(
                kernel,
                scal,
                arrays,
                after,
                out_shape=[half(rows, sum(sizes))] * team,
                out_specs=[whole()] * team,
                name="pack_columns",
            )

        def stack(parts, sizes, name, after=()):
            def plan(place):
                out = []
                for m in range(team):
                    at = 0
                    for b, size in enumerate(sizes):
                        out.append((m, (ALL, pl.ds(at, size)), b, (span(place ^ m, rows), ALL)))
                        at += size
                return out

            return copies(scal, parts, [half(chunk, size) for size in sizes], plan, name, after)

        def beside(parts, sizes, name):
            def plan(place):
                out = []
                for m in range(team):
                    at = 0
                    for b, size in enumerate(sizes):
                        out.append((m, (ALL, pl.ds(at, size)), b, (ALL, span(place ^ m, size))))
                        at += size
                return out

            shapes = [half(rows, team * size) for size in sizes]
            return copies(scal, parts, shapes, plan, name)

        if n_head == 2:
            d_far = lax.ppermute(d_out, "head", [(0, 1), (1, 0)])
        if team > 1:
            kv_sent = pack([keys, values], [DH, DH])
            kv_got = swapped(kv_sent)
            near = []
            if n_head == 2:
                near.append(project(scal, d_out, w_out, (), False, team, 0, team, kv_sent[:1]))
            q_sent = pack([queries], [width], kv_sent[:1])
            q_got = swapped(q_sent)
            (kv,) = stack(kv_got, [2 * DH], "stack_keys_values", near + list(q_sent[:1]))
            order = (kv,)
        else:
            kv = jnp.concatenate([keys, values], axis=1)
            near = [project(scal, d_out, w_out, (), False, 1, 0, 1)] if n_head == 2 else []
            q = queries
            order = ()
        if n_head == 2:
            g_parts = project(scal, d_far, w_out, near, True, team, 0, team, order)
        else:
            d_all = lax.all_gather(d_out, "head", axis=1, tiled=True)
            zero = jnp.zeros((rows, width * team), jnp.float32)
            g_parts = project(scal, d_all, w_out, [zero], False, team, 0, team, order)
        if team > 1:
            g_got = swapped(g_parts)
            (q,) = stack(q_got, [width], "stack_queries", g_parts[:1])
        state = stats(scal, docs, tile, 0, q, kv, None, g_parts[:1])

        def stack_g(after):
            if team > 1:
                return stack(g_got, [width], "stack_attn_grad", after)[0]
            return g_parts[0]

        if layers <= 4:
            kvs = [kv]
            for d in range(1, reach + 1):
                kvs.append(shift(1, kvs[1]) if d == 2 and reach > 2 else shift(d, kv))
            g = None
            for d in range(1, reach + 1):
                state = stats(
                    scal, docs, tile, d, q, kvs[d], state, g_parts[:1] if g is None else (g,)
                )
                if g is None:
                    g = stack_g(state[:1])
            if g is None:
                g = stack_g(state[:1])
            log_total, delta = finish(g, *state)
            dq = None
            carried = None
            for d in reversed(range(1, reach + 1)):
                dq, dkv = grads(scal, docs, tile, d, q, g, kvs[d], log_total, delta, dq)
                if carried is not None:
                    dkv = add(dkv, carried)
                carried = shift(-1, dkv)
            *dq_parts, dkv = grads(
                scal, docs, tile, 0, q, g, kv, log_total, delta, dq, team, jnp.float32
            )
            terms = [] if carried is None else [carried]
        else:
            rings = [[z * team + a for z in range(layers)] for a in range(team)]
            every = lax.all_gather(kv, "seq", axis_index_groups=rings)

            def chunk_at(d):
                return lax.dynamic_index_in_dim(every, jnp.maximum(layer - d, 0), 0, keepdims=False)

            def scalars(d):
                return scal - jnp.where(jnp.arange(scal.shape[0]) == 1, d * chunk, 0)

            def one(d, state):
                return tuple(stats(scalars(d), docs, tile, 0, q, chunk_at(d), state))

            state = lax.fori_loop(1, layers, one, tuple(state))
            g = stack_g(())
            log_total, delta = finish(g, *state)

            def two(d, carry):
                dq, total = carry
                dq, dkv = grads(
                    scalars(d), docs, tile, 0, q, g, chunk_at(d), log_total, delta, dq
                )
                place = jnp.maximum(layer - d, 0)
                old = lax.dynamic_index_in_dim(total, place, 0, keepdims=False)
                total = lax.dynamic_update_index_in_dim(
                    total, jnp.where(layer >= d, dkv, old), place, 0
                )
                return dq, total

            dq = jnp.zeros((width, chunk), jnp.float32)
            total = jnp.zeros((layers, chunk, 2 * DH), jnp.bfloat16)
            dq, total = lax.fori_loop(1, layers, two, (dq, total))
            *dq_parts, dkv = grads(
                scal, docs, tile, 0, q, g, kv, log_total, delta, dq, team, jnp.float32
            )
            terms = [
                lax.psum_scatter(
                    total.reshape(layers * chunk, 2 * DH), "seq", axis_index_groups=rings, tiled=True
                )
            ]

        def sum_kernel(scal, *refs):
            total = refs[0][...]
            for x in refs[1 : 1 + len(terms)]:
                total = total + x[...].astype(jnp.float32)
            full = refs[-1]
            full[...] = total.astype(jnp.bfloat16)
            for m in range(team):
                refs[1 + len(terms) + m][...] = full[span(scal[2] ^ m, rows), :]

        dkv_parts = pl.pallas_call(
            sum_kernel,
            out_shape=(half(rows, 2 * DH),) * team,
            in_specs=[whole(pltpu.SMEM)] + [whole()] * (1 + len(terms)),
            out_specs=(whole(),) * team,
            scratch_shapes=[pltpu.VMEM((chunk, 2 * DH), jnp.bfloat16)],
            compiler_params=params(),
            name="sum_terms",
        )(scal, dkv, *terms)
        if team > 1:
            dq_parts = swapped(dq_parts)
            dkv_parts = swapped(dkv_parts)
            (query_grad,) = beside(dq_parts, [width], "place_query_grad")
            key_grad, value_grad = beside(dkv_parts, [DH, DH], "place_key_value_grad")
        else:
            query_grad = dq_parts[0]
            key_grad = dkv_parts[0][:, :DH]
            value_grad = dkv_parts[0][:, DH:]
        return (query_grad, key_grad, value_grad)

    return jax.shard_map(
        shards,
        mesh=mesh,
        in_specs=(
            P("seq", "head"),
            P("seq", "head"),
            P("seq", "head"),
            P("seq", "head"),
            P("head", None),
            P(),
        ),
        out_specs=(P("seq", "head"), P("seq", "head"), P("seq", "head")),
        check_vma=False,
    )
```

```python
import functools
import math

import jax
import jax.numpy as jnp
from jax import lax
from jax.experimental import pallas as pl
from jax.experimental.pallas import tpu as pltpu
from jax.sharding import PartitionSpec as P

DH = 128
ONES = 16
LOG2E = 1.4426950408889634
NEG = -1e30
VMEM_LIMIT = 28 * 1024 * 1024
PROJECT_LIMIT = 52 * 1024 * 1024

NT = (((1,), (1,)), ((), ()))
NN = (((1,), (0,)), ((), ()))


def dot(a, b, dims):
    return lax.dot_general(a, b, dims, preferred_element_type=jnp.float32)


def params(limit=VMEM_LIMIT):
    return pltpu.CompilerParams(vmem_limit_bytes=limit)


def whole(memory_space=pltpu.VMEM):
    return pl.BlockSpec(memory_space=memory_space)


def ordered_call(kernel, scal, operands, after, **kwargs):
    count = len(after)

    def body(*refs):
        kernel(*refs[: 1 + len(operands)], *refs[1 + len(operands) + count :])

    specs = kwargs.pop("in_specs", [whole()] * len(operands))
    return pl.pallas_call(
        body,
        in_specs=[whole(pltpu.SMEM)] + specs + [whole(pl.ANY)] * count,
        compiler_params=params(),
        **kwargs,
    )(scal, *operands, *after)


def cost(flops, nbytes, exps=0):
    return pl.CostEstimate(flops=1024, bytes_accessed=1024, transcendentals=0)


FIRST_DOC = 4


def row_starts(scal, docs, pos):
    low = jnp.zeros_like(pos)
    for n in range(docs):
        low = jnp.where(pos >= scal[FIRST_DOC + n], scal[FIRST_DOC + n], low)
    return low


def doc_start_at(scal, docs, pos):
    low = jnp.int32(0)
    for n in range(docs):
        low = jnp.where(pos >= scal[FIRST_DOC + n], scal[FIRST_DOC + n], low)
    return low


def allowed(scal, docs, q0, k0, tq, tk):
    qpos = q0 + lax.broadcasted_iota(jnp.int32, (1, tq), 1)
    kpos = k0 + lax.broadcasted_iota(jnp.int32, (tk, 1), 0)
    return (kpos <= qpos) & (kpos >= row_starts(scal, docs, qpos))


def over_tiles(scal, docs, d, chunk, tile, body):
    tiles = chunk // tile

    def one(qo, ko, q0, tk, need):
        k0 = scal[1] - d * chunk + ko
        @pl.when(need)
        def _():
            body(qo, ko, tk, allowed(scal, docs, q0, k0, tile, tk))

    def step(qt, _):
        qo = pl.multiple_of(qt * tile, tile)
        q0 = scal[0] + qo
        low = doc_start_at(scal, docs, q0)
        k0 = scal[1] - d * chunk
        if tiles == 1:
            one(qo, 0, q0, tile, (k0 <= q0 + tile - 1) & (k0 + tile - 1 >= low))
            return 0
        all_of = (k0 + chunk - tile <= q0 + tile - 1) & (k0 + tile - 1 >= low)
        one(qo, 0, q0, chunk, all_of)

        @pl.when(jnp.logical_not(all_of))
        def _():
            def inner(kt, _):
                ko = pl.multiple_of(kt * tile, tile)
                need = (k0 + ko <= q0 + tile - 1) & (k0 + ko + tile - 1 >= low)
                one(qo, ko, q0, tile, need)
                return 0

            lax.fori_loop(0, tiles, inner, 0)

        return 0

    lax.fori_loop(0, tiles, step, 0)


def stats_kernel(docs, tile, heads, d, first, scal, q_ref, kv_ref, *refs):
    if first:
        m_ref, o_ref, vt_ref = refs
        m_ref[...] = jnp.full_like(m_ref, NEG)
        o_ref[...] = jnp.zeros_like(o_ref)
    else:
        m_in, o_in, m_ref, o_ref, vt_ref = refs
        m_ref[...] = m_in[...]
        o_ref[...] = o_in[...]
    chunk = q_ref.shape[0]
    factor = LOG2E / math.sqrt(DH)
    ext = DH + ONES
    vt_ref[:DH] = kv_ref[:, DH:].T
    vt_ref[DH:] = jnp.ones((vt_ref.shape[0] - DH, chunk), jnp.bfloat16)

    def body(qo, ko, tk, mask):
        k = kv_ref[pl.ds(ko, tk), :DH]
        vt = vt_ref[:ext, pl.ds(ko, tk)]
        rows = pl.ds(qo, tile)
        m_old = m_ref[:, rows]
        scores = [dot(k, q_ref[rows, h * DH : (h + 1) * DH], NT) for h in range(heads)]
        scores = [jnp.where(mask, s, NEG) for s in scores]
        tops = [jnp.max(s, axis=0, keepdims=True) for s in scores]
        m_new = jnp.maximum(m_old, factor * jnp.concatenate(tops, 0))
        alpha = jnp.exp2(m_old - m_new)
        m_ref[:, rows] = m_new
        for h in range(heads):
            p = jnp.exp2(scores[h] * factor - m_new[h : h + 1]).astype(jnp.bfloat16)
            part = slice(h * ext, (h + 1) * ext)
            o_ref[part, rows] = alpha[h : h + 1] * o_ref[part, rows] + dot(vt, p, NN)

    over_tiles(scal, docs, d, chunk, tile, body)


def stats(scal, docs, tile, d, q, kv, state, after=()):
    chunk, width = q.shape
    heads = width // DH
    shapes = (
        jax.ShapeDtypeStruct((heads, chunk), jnp.float32),
        jax.ShapeDtypeStruct((heads * (DH + ONES), chunk), jnp.float32),
    )
    first = state is None
    extra = () if first else state
    return ordered_call(
        functools.partial(stats_kernel, docs, tile, heads, d, first),
        scal,
        (q, kv, *extra),
        after,
        out_shape=shapes,
        out_specs=(whole(),) * 2,
        scratch_shapes=[pltpu.VMEM((DH + ONES, chunk), jnp.bfloat16)],
        cost_estimate=cost(4 * chunk * chunk * width, 12 * chunk * width, chunk * chunk * heads),
        name="row_stats",
    )


def finish_kernel(heads, g_ref, m_ref, o_ref, log_ref, delta_ref):
    ext = DH + ONES
    for h in range(heads):
        total = o_ref[h * ext + DH : h * ext + DH + 1, :]
        gt = g_ref[:, h * DH : (h + 1) * DH].T.astype(jnp.float32)
        part = jnp.sum(gt * o_ref[h * ext : h * ext + DH, :], axis=0, keepdims=True)
        log_ref[h : h + 1, :] = m_ref[h : h + 1, :] + jnp.log2(total)
        delta_ref[h : h + 1, :] = part / total


def finish(g, m, o):
    heads, chunk = m.shape
    shape = jax.ShapeDtypeStruct((heads, chunk), jnp.float32)
    return pl.pallas_call(
        functools.partial(finish_kernel, heads),
        out_shape=(shape, shape),
        in_specs=[whole()] * 3,
        out_specs=(whole(),) * 2,
        compiler_params=params(),
        cost_estimate=cost(2 * chunk * heads * DH, 6 * chunk * heads * DH),
        name="row_delta",
    )(g, m, o)


def grads_kernel(
    docs, tile, heads, d, first, team, scal, q_ref, g_ref, kv_ref, log_ref, delta_ref, *refs
):
    refs = list(refs)
    dq_in = None if first else refs.pop(0)
    acc_ref, kt_ref = refs.pop(), refs.pop()
    dkv_ref = refs.pop()
    last = team is not None
    if last:
        full_ref = acc_ref
        acc_ref, dq_ref = refs.pop(), refs.pop()
        outs = refs
    else:
        dq_ref = refs.pop()
    chunk = q_ref.shape[0]
    scaling = 1.0 / math.sqrt(DH)
    factor = LOG2E * scaling
    if first:
        dq_ref[...] = jnp.zeros_like(dq_ref)
    else:
        dq_ref[...] = dq_in[...]
    acc_ref[...] = jnp.zeros_like(acc_ref)
    kt_ref[...] = kv_ref[:, :DH].T

    def body(qo, ko, tk, mask):
        rows = pl.ds(qo, tile)
        keys = pl.ds(ko, tk)
        k = kv_ref[keys, :DH]
        v = kv_ref[keys, DH:]
        qs = [q_ref[rows, h * DH : (h + 1) * DH] for h in range(heads)]
        gs = [g_ref[rows, h * DH : (h + 1) * DH] for h in range(heads)]
        scores = [dot(k, q, NT) for q in qs]
        dots = [dot(v, g, NT) for g in gs]
        scores = [jnp.where(mask, s, NEG) for s in scores]
        probs = [
            jnp.exp2(scores[h] * factor - log_ref[h : h + 1, rows]) for h in range(heads)
        ]
        ds = [
            (probs[h] * (dots[h] - delta_ref[h : h + 1, rows])).astype(jnp.bfloat16)
            for h in range(heads)
        ]
        probs = [p.astype(jnp.bfloat16) for p in probs]
        dv = dot(jnp.concatenate(probs, 1), jnp.concatenate(gs, 0), NN)
        dk = dot(jnp.concatenate(ds, 1), jnp.concatenate(qs, 0), NN)
        kt = kt_ref[:, keys]
        for h in range(heads):
            dq_ref[h * DH : (h + 1) * DH, rows] += dot(kt, ds[h], NN)
        acc_ref[keys, :DH] += dk
        acc_ref[keys, DH:] += dv

    over_tiles(scal, docs, d, chunk, tile, body)
    dkv_ref[:, :DH] = (acc_ref[:, :DH] * scaling).astype(dkv_ref.dtype)
    dkv_ref[:, DH:] = acc_ref[:, DH:].astype(dkv_ref.dtype)
    if last:
        for h in range(heads):
            full_ref[:, h * DH : (h + 1) * DH] = (
                (dq_ref[h * DH : (h + 1) * DH, :] * scaling).T.astype(jnp.bfloat16)
            )
        size = chunk // team
        for m in range(team):
            outs[m][...] = full_ref[pl.ds(pl.multiple_of((scal[2] ^ m) * size, size), size), :]


def grads(
    scal, docs, tile, d, q, g, kv, log_total, delta, dq, team=None, dtype=jnp.bfloat16, after=()
):
    chunk, width = q.shape
    heads = width // DH
    first = dq is None
    extra = () if first else (dq,)
    dkv_shape = jax.ShapeDtypeStruct((chunk, 2 * DH), dtype)
    scratch = [pltpu.VMEM((DH, chunk), jnp.bfloat16)]
    dq_rows = pltpu.VMEM((width, chunk), jnp.float32)
    acc = pltpu.VMEM((chunk, 2 * DH), jnp.float32)
    if team is None:
        shapes = (jax.ShapeDtypeStruct((width, chunk), jnp.float32), dkv_shape)
        scratch = scratch + [acc]
        kernel = functools.partial(grads_kernel, docs, tile, heads, d, first, None)
    else:
        shapes = (jax.ShapeDtypeStruct((chunk // team, width), jnp.bfloat16),) * team + (dkv_shape,)
        scratch = [dq_rows, acc] + scratch + [pltpu.VMEM((chunk, width), jnp.bfloat16)]

        def kernel(*refs):
            refs = list(refs)
            full, kt, acc_ref, dq_ref = refs.pop(), refs.pop(), refs.pop(), refs.pop()
            dkv_ref = refs.pop()
            refs = refs + [dq_ref, acc_ref, dkv_ref, kt, full]
            grads_kernel(docs, tile, heads, d, first, team, *refs)

    return ordered_call(
        kernel,
        scal,
        (q, g, kv, log_total, delta, *extra),
        after,
        out_shape=shapes,
        out_specs=(whole(),) * len(shapes),
        scratch_shapes=scratch,
        cost_estimate=cost(10 * chunk * chunk * width, 12 * chunk * width, chunk * chunk * heads),
        name="pair_grads",
    )


def project(scal, d, w, parts, far, blocks, begin, count, after=()):
    rows, depth = d.shape
    wide = w.shape[0] // blocks
    split = w.shape[1] // depth
    each = 0 if not parts else parts[0].shape[1] // wide

    def kernel(*refs):
        scal, d_ref, w_ref = refs[:3]
        total = dot(d_ref[...], w_ref[...], NT)
        if not parts:
            refs[-1][...] = total
            return
        outs = refs[3 + len(parts) + len(after) :]
        for m in range(count):

            @pl.when(pl.program_id(0) == m)
            def _():
                outs[m][...] = (total + refs[3 + m // each][...]).astype(outs[m].dtype)

    def column(s):
        if split == 1:
            return 0
        return 1 - s[3] if far else s[3]

    def part_spec(p):
        return pl.BlockSpec((rows, wide), lambda i, s: (0, jnp.clip(i - p * each, 0, each - 1)))

    w_spec = pl.BlockSpec((wide, depth), lambda i, s: (s[2] ^ (i + begin), column(s)))
    if parts:
        out_shape = (jax.ShapeDtypeStruct((rows, wide), jnp.bfloat16),) * count
        out_specs = (pl.BlockSpec((rows, wide), lambda i, s: (0, 0)),) * count
    else:
        out_shape = jax.ShapeDtypeStruct((rows, wide * count), jnp.float32)
        out_specs = pl.BlockSpec((rows, wide), lambda i, s: (0, i))
    grid_spec = pltpu.PrefetchScalarGridSpec(
        num_scalar_prefetch=1,
        grid=(count,),
        in_specs=[pl.BlockSpec((rows, depth), lambda i, s: (0, 0)), w_spec]
        + [part_spec(p) for p in range(len(parts))]
        + [whole(pl.ANY)] * len(after),
        out_specs=out_specs,
    )
    return pl.pallas_call(
        kernel,
        out_shape=out_shape,
        grid_spec=grid_spec,
        compiler_params=params(PROJECT_LIMIT),
        cost_estimate=cost(2 * rows * depth * wide * count, 2 * depth * wide * count),
        name="project",
    )(scal, d, w, *parts, *after)


def copies(scal, inputs, out_shapes, plan, name, after=()):
    n_in = len(inputs)

    def kernel(scal, *refs):
        ins, outs, sems = refs[:n_in], refs[n_in:-1], refs[-1]
        started = []
        for i, (a, src, b, dst) in enumerate(plan(scal[2])):
            copy = pltpu.make_async_copy(ins[a].at[src], outs[b].at[dst], sems.at[i])
            copy.start()
            started.append(copy)
        for copy in started:
            copy.wait()

    count = len(plan(0))
    size = sum(math.prod(s.shape) * 2 for s in out_shapes)
    return ordered_call(
        kernel,
        scal,
        inputs,
        after,
        out_shape=tuple(out_shapes),
        in_specs=[whole(pl.ANY)] * n_in,
        out_specs=(whole(pl.ANY),) * len(out_shapes),
        scratch_shapes=[pltpu.SemaphoreType.DMA((count,))],
        cost_estimate=cost(0, 2 * size),
        name=name,
    )


def add_kernel(a_ref, b_ref, out_ref):
    total = a_ref[...].astype(jnp.float32) + b_ref[...].astype(jnp.float32)
    out_ref[...] = total.astype(out_ref.dtype)


def add(a, b):
    return pl.pallas_call(
        add_kernel,
        out_shape=jax.ShapeDtypeStruct(a.shape, a.dtype),
        in_specs=[whole()] * 2,
        out_specs=whole(),
        compiler_params=params(),
        cost_estimate=cost(a.size, 6 * a.size),
        name="add_terms",
    )(a, b)


def span(start, size):
    if isinstance(start, int):
        return pl.ds(start, size)
    return pl.ds(pl.multiple_of(start * size, size), size)


ALL = slice(None)


def solution(mesh):
    n_seq = mesh.shape["seq"]
    n_head = mesh.shape["head"]

    def shards(*args):
        doc_starts = args[-1]
        layers = n_seq // (args[1].shape[1] // DH)
        chunk = args[0].shape[0] * n_seq // layers
        if layers != 4:
            return part_of(layers - 1, *args)
        total = jnp.full((1,), chunk * layers, doc_starts.dtype)
        ends = jnp.concatenate([doc_starts[1:], total]) - 1
        reach = jnp.max(ends // chunk - doc_starts // chunk)
        near, far = [functools.partial(part_of, r) for r in (2, layers - 1)]
        return lax.switch((reach > 2).astype(jnp.int32), [near, far], *args)

    def part_of(reach, queries, keys, values, d_out, w_out, doc_starts):
        rows = queries.shape[0]
        groups = keys.shape[1] // DH
        heads = queries.shape[1] // keys.shape[1]
        width = heads * DH
        docs = doc_starts.shape[0]
        team = groups
        layers = n_seq // team
        chunk = team * rows
        tile = 256 if chunk % 256 == 0 else rows
        me = lax.axis_index("seq")
        layer = me // team
        head = lax.axis_index("head")
        base = layer * chunk
        scal = jnp.concatenate([jnp.stack([base, base, me % team, head]), doc_starts])

        def half(*shape):
            return jax.ShapeDtypeStruct(shape, jnp.bfloat16)

        def swap(m, x):
            return lax.ppermute(x, "seq", [(i, i ^ m) for i in range(n_seq)])

        def swapped(parts):
            got = list(parts)
            for m in reversed(range(1, team)):
                got[m] = swap(m, parts[m])
            return got

        def shift(d, x):
            pairs = [(i, i + d * team) for i in range(n_seq) if 0 <= i + d * team < n_seq]
            return lax.ppermute(x, "seq", pairs)

        def pack(arrays, sizes, after=()):
            def kernel(scal, *refs):
                ins, outs = refs[: len(arrays)], refs[len(arrays) :]
                for m in range(team):
                    at = 0
                    for ref, size in zip(ins, sizes):
                        outs[m][:, at : at + size] = ref[:, span(scal[2] ^ m, size)]
                        at += size

            return ordered_call(
                kernel,
                scal,
                arrays,
                after,
                out_shape=[half(rows, sum(sizes))] * team,
                out_specs=[whole()] * team,
                name="pack_columns",
            )

        def stack(parts, sizes, name, after=()):
            def plan(place):
                out = []
                for m in range(team):
                    at = 0
                    for b, size in enumerate(sizes):
                        out.append((m, (ALL, pl.ds(at, size)), b, (span(place ^ m, rows), ALL)))
                        at += size
                return out

            return copies(scal, parts, [half(chunk, size) for size in sizes], plan, name, after)

        def beside(parts, sizes, name):
            def plan(place):
                out = []
                for m in range(team):
                    at = 0
                    for b, size in enumerate(sizes):
                        out.append((m, (ALL, pl.ds(at, size)), b, (ALL, span(place ^ m, size))))
                        at += size
                return out

            shapes = [half(rows, team * size) for size in sizes]
            return copies(scal, parts, shapes, plan, name)

        if n_head == 2:
            d_far = lax.ppermute(d_out, "head", [(0, 1), (1, 0)])
        if team > 1:
            kv_sent = pack([keys, values], [DH, DH])
            kv_got = swapped(kv_sent)
            near = []
            if n_head == 2:
                near.append(project(scal, d_out, w_out, (), False, team, 0, team, kv_sent[:1]))
            q_sent = pack([queries], [width], kv_sent[:1])
            q_got = swapped(q_sent)
            (kv,) = stack(kv_got, [2 * DH], "stack_keys_values", near + list(q_sent[:1]))
            order = (kv,)
        else:
            kv = jnp.concatenate([keys, values], axis=1)
            near = [project(scal, d_out, w_out, (), False, 1, 0, 1)] if n_head == 2 else []
            q = queries
            order = ()
        if n_head == 2:
            g_parts = project(scal, d_far, w_out, near, True, team, 0, team, order)
        else:
            d_all = lax.all_gather(d_out, "head", axis=1, tiled=True)
            zero = jnp.zeros((rows, width * team), jnp.float32)
            g_parts = project(scal, d_all, w_out, [zero], False, team, 0, team, order)
        if team > 1:
            g_got = swapped(g_parts)
            (q,) = stack(q_got, [width], "stack_queries", g_parts[:1])
        state = stats(scal, docs, tile, 0, q, kv, None, g_parts[:1])

        def stack_g(after):
            if team > 1:
                return stack(g_got, [width], "stack_attn_grad", after)[0]
            return g_parts[0]

        if layers <= 4:
            kvs = [kv]
            for d in range(1, reach + 1):
                kvs.append(shift(1, kvs[1]) if d == 2 and reach > 2 else shift(d, kv))
            g = None
            for d in range(1, reach + 1):
                state = stats(
                    scal, docs, tile, d, q, kvs[d], state, g_parts[:1] if g is None else (g,)
                )
                if g is None:
                    g = stack_g(state[:1])
            if g is None:
                g = stack_g(state[:1])
            log_total, delta = finish(g, *state)
            dq = None
            carried = None
            for d in reversed(range(1, reach + 1)):
                dq, dkv = grads(scal, docs, tile, d, q, g, kvs[d], log_total, delta, dq)
                if carried is not None:
                    dkv = add(dkv, carried)
                carried = shift(-1, dkv)
            *dq_parts, dkv = grads(
                scal, docs, tile, 0, q, g, kv, log_total, delta, dq, team, jnp.float32
            )
            terms = [] if carried is None else [carried]
        else:
            rings = [[z * team + a for z in range(layers)] for a in range(team)]
            every = lax.all_gather(kv, "seq", axis_index_groups=rings)

            def chunk_at(d):
                return lax.dynamic_index_in_dim(every, jnp.maximum(layer - d, 0), 0, keepdims=False)

            def scalars(d):
                return scal - jnp.where(jnp.arange(scal.shape[0]) == 1, d * chunk, 0)

            def one(d, state):
                return tuple(stats(scalars(d), docs, tile, 0, q, chunk_at(d), state))

            state = lax.fori_loop(1, layers, one, tuple(state))
            g = stack_g(())
            log_total, delta = finish(g, *state)

            def two(d, carry):
                dq, total = carry
                dq, dkv = grads(
                    scalars(d), docs, tile, 0, q, g, chunk_at(d), log_total, delta, dq
                )
                place = jnp.maximum(layer - d, 0)
                old = lax.dynamic_index_in_dim(total, place, 0, keepdims=False)
                total = lax.dynamic_update_index_in_dim(
                    total, jnp.where(layer >= d, dkv, old), place, 0
                )
                return dq, total

            dq = jnp.zeros((width, chunk), jnp.float32)
            total = jnp.zeros((layers, chunk, 2 * DH), jnp.bfloat16)
            dq, total = lax.fori_loop(1, layers, two, (dq, total))
            *dq_parts, dkv = grads(
                scal, docs, tile, 0, q, g, kv, log_total, delta, dq, team, jnp.float32
            )
            terms = [
                lax.psum_scatter(
                    total.reshape(layers * chunk, 2 * DH), "seq", axis_index_groups=rings, tiled=True
                )
            ]

        def sum_kernel(scal, *refs):
            total = refs[0][...]
            for x in refs[1 : 1 + len(terms)]:
                total = total + x[...].astype(jnp.float32)
            full = refs[-1]
            full[...] = total.astype(jnp.bfloat16)
            for m in range(team):
                refs[1 + len(terms) + m][...] = full[span(scal[2] ^ m, rows), :]

        dkv_parts = pl.pallas_call(
            sum_kernel,
            out_shape=(half(rows, 2 * DH),) * team,
            in_specs=[whole(pltpu.SMEM)] + [whole()] * (1 + len(terms)),
            out_specs=(whole(),) * team,
            scratch_shapes=[pltpu.VMEM((chunk, 2 * DH), jnp.bfloat16)],
            compiler_params=params(),
            name="sum_terms",
        )(scal, dkv, *terms)
        if team > 1:
            dq_parts = swapped(dq_parts)
            dkv_parts = swapped(dkv_parts)
            (query_grad,) = beside(dq_parts, [width], "place_query_grad")
            key_grad, value_grad = beside(dkv_parts, [DH, DH], "place_key_value_grad")
        else:
            query_grad = dq_parts[0]
            key_grad = dkv_parts[0][:, :DH]
            value_grad = dkv_parts[0][:, DH:]
        return (query_grad, key_grad, value_grad)

    return jax.shard_map(
        shards,
        mesh=mesh,
        in_specs=(
            P("seq", "head"),
            P("seq", "head"),
            P("seq", "head"),
            P("seq", "head"),
            P("head", None),
            P(),
        ),
        out_specs=(P("seq", "head"), P("seq", "head"), P("seq", "head")),
        check_vma=False,
    )
```

```python
import functools
import math

import jax
import jax.numpy as jnp
from jax import lax
from jax.experimental import pallas as pl
from jax.experimental.pallas import tpu as pltpu
from jax.sharding import PartitionSpec as P

DH = 128
ONES = 16
LOG2E = 1.4426950408889634
NEG = -1e30
VMEM_LIMIT = 28 * 1024 * 1024
PROJECT_LIMIT = 52 * 1024 * 1024

NT = (((1,), (1,)), ((), ()))
NN = (((1,), (0,)), ((), ()))


def dot(a, b, dims):
    return lax.dot_general(a, b, dims, preferred_element_type=jnp.float32)


def params(limit=VMEM_LIMIT):
    return pltpu.CompilerParams(vmem_limit_bytes=limit)


def whole(memory_space=pltpu.VMEM):
    return pl.BlockSpec(memory_space=memory_space)


def ordered_call(kernel, scal, operands, after, **kwargs):
    count = len(after)

    def body(*refs):
        kernel(*refs[: 1 + len(operands)], *refs[1 + len(operands) + count :])

    specs = kwargs.pop("in_specs", [whole()] * len(operands))
    return pl.pallas_call(
        body,
        in_specs=[whole(pltpu.SMEM)] + specs + [whole(pl.ANY)] * count,
        compiler_params=params(),
        **kwargs,
    )(scal, *operands, *after)


def cost(flops, nbytes, exps=0):
    return pl.CostEstimate(flops=1024, bytes_accessed=1024, transcendentals=0)


FAR = 4
FIRST_DOC = 5


def row_starts(scal, docs, pos):
    low = jnp.zeros_like(pos)
    for n in range(docs):
        low = jnp.where(pos >= scal[FIRST_DOC + n], scal[FIRST_DOC + n], low)
    return low


def doc_start_at(scal, docs, pos):
    low = jnp.int32(0)
    for n in range(docs):
        low = jnp.where(pos >= scal[FIRST_DOC + n], scal[FIRST_DOC + n], low)
    return low


def allowed(scal, docs, q0, k0, tq, tk):
    qpos = q0 + lax.broadcasted_iota(jnp.int32, (1, tq), 1)
    kpos = k0 + lax.broadcasted_iota(jnp.int32, (tk, 1), 0)
    return (kpos <= qpos) & (kpos >= row_starts(scal, docs, qpos))


def over_tiles(scal, docs, d, chunk, tile, body):
    tiles = chunk // tile

    def one(qo, ko, q0, tk, need):
        k0 = scal[1] - d * chunk + ko
        @pl.when(need)
        def _():
            body(qo, ko, tk, allowed(scal, docs, q0, k0, tile, tk))

    def step(qt, _):
        qo = pl.multiple_of(qt * tile, tile)
        q0 = scal[0] + qo
        low = doc_start_at(scal, docs, q0)
        k0 = scal[1] - d * chunk
        if tiles == 1:
            one(qo, 0, q0, tile, (k0 <= q0 + tile - 1) & (k0 + tile - 1 >= low))
            return 0
        all_of = (k0 + chunk - tile <= q0 + tile - 1) & (k0 + tile - 1 >= low)
        one(qo, 0, q0, chunk, all_of)

        @pl.when(jnp.logical_not(all_of))
        def _():
            def inner(kt, _):
                ko = pl.multiple_of(kt * tile, tile)
                need = (k0 + ko <= q0 + tile - 1) & (k0 + ko + tile - 1 >= low)
                one(qo, ko, q0, tile, need)
                return 0

            lax.fori_loop(0, tiles, inner, 0)

        return 0

    lax.fori_loop(0, tiles, step, 0)


def each_chunk(scal, kv_refs, now_ref, d, down, use):
    count = len(kv_refs)
    if count == 1:
        now_ref[...] = kv_refs[0][...]
        use(0, d)
        return

    def one(i, _):
        for j, ref in enumerate(kv_refs):

            @pl.when(i == j)
            def _():
                now_ref[...] = ref[...]

        use(i, d + i)
        return 0

    total = 1 + (count - 1) * scal[FAR]
    if down:
        lax.fori_loop(0, total, lambda i, c: one(total - 1 - i, c), 0)
    else:
        lax.fori_loop(0, total, one, 0)


def stats_kernel(docs, tile, heads, d, first, count, scal, q_ref, *refs):
    kv_refs, refs = refs[:count], refs[count:]
    if first:
        m_ref, o_ref, kv_ref, vt_ref = refs
        m_ref[...] = jnp.full_like(m_ref, NEG)
        o_ref[...] = jnp.zeros_like(o_ref)
    else:
        m_in, o_in, m_ref, o_ref, kv_ref, vt_ref = refs
        m_ref[...] = m_in[...]
        o_ref[...] = o_in[...]
    chunk = q_ref.shape[0]
    factor = LOG2E / math.sqrt(DH)
    ext = DH + ONES
    vt_ref[DH:] = jnp.ones((vt_ref.shape[0] - DH, chunk), jnp.bfloat16)

    def body(qo, ko, tk, mask):
        k = kv_ref[pl.ds(ko, tk), :DH]
        vt = vt_ref[:ext, pl.ds(ko, tk)]
        rows = pl.ds(qo, tile)
        scores = [dot(k, q_ref[rows, h * DH : (h + 1) * DH], NT) for h in range(heads)]
        scores = [jnp.where(mask, s, NEG) for s in scores]
        m_old = [m_ref[h : h + 1, rows] for h in range(heads)]
        m_new = [
            jnp.maximum(m, factor * jnp.max(s, axis=0, keepdims=True))
            for m, s in zip(m_old, scores)
        ]
        alpha = [jnp.exp2(a - b) for a, b in zip(m_old, m_new)]
        probs = [jnp.exp2(s * factor - m).astype(jnp.bfloat16) for s, m in zip(scores, m_new)]
        news = [dot(vt, p, NN) for p in probs]
        for h in range(heads):
            part = slice(h * ext, (h + 1) * ext)
            m_ref[h : h + 1, rows] = m_new[h]
            o_ref[part, rows] = alpha[h] * o_ref[part, rows] + news[h]

    def use(i, dist):
        vt_ref[:DH] = kv_ref[:, DH:].T
        over_tiles(scal, docs, dist, chunk, tile, body)

    each_chunk(scal, kv_refs, kv_ref, d, False, use)


def stats(scal, docs, tile, d, q, kvs, state, after=()):
    chunk, width = q.shape
    heads = width // DH
    shapes = (
        jax.ShapeDtypeStruct((heads, chunk), jnp.float32),
        jax.ShapeDtypeStruct((heads * (DH + ONES), chunk), jnp.float32),
    )
    first = state is None
    extra = () if first else state
    return ordered_call(
        functools.partial(stats_kernel, docs, tile, heads, d, first, len(kvs)),
        scal,
        (q, *kvs, *extra),
        after,
        out_shape=shapes,
        out_specs=(whole(),) * 2,
        scratch_shapes=[
            pltpu.VMEM((chunk, 2 * DH), jnp.bfloat16),
            pltpu.VMEM((DH + ONES, chunk), jnp.bfloat16),
        ],
        cost_estimate=cost(4 * chunk * chunk * width, 12 * chunk * width, chunk * chunk * heads),
        name="row_stats",
    )


def finish_kernel(heads, g_ref, m_ref, o_ref, log_ref, delta_ref):
    ext = DH + ONES
    for h in range(heads):
        total = o_ref[h * ext + DH : h * ext + DH + 1, :]
        gt = g_ref[:, h * DH : (h + 1) * DH].T.astype(jnp.float32)
        part = jnp.sum(gt * o_ref[h * ext : h * ext + DH, :], axis=0, keepdims=True)
        log_ref[h : h + 1, :] = m_ref[h : h + 1, :] + jnp.log2(total)
        delta_ref[h : h + 1, :] = part / total


def finish(g, m, o):
    heads, chunk = m.shape
    shape = jax.ShapeDtypeStruct((heads, chunk), jnp.float32)
    return pl.pallas_call(
        functools.partial(finish_kernel, heads),
        out_shape=(shape, shape),
        in_specs=[whole()] * 3,
        out_specs=(whole(),) * 2,
        compiler_params=params(),
        cost_estimate=cost(2 * chunk * heads * DH, 6 * chunk * heads * DH),
        name="row_delta",
    )(g, m, o)


def grads_kernel(docs, tile, heads, d, first, team, count, scal, q_ref, g_ref, *refs):
    kv_refs, refs = refs[:count], refs[count:]
    log_ref, delta_ref, refs = refs[0], refs[1], refs[2:]
    if not first:
        dq_in, refs = refs[0], refs[1:]
    if team is None:
        dq_ref, *dkv_refs, kv_ref, kt_ref, acc_ref = refs
    else:
        *outs, dkv_ref, kv_ref, kt_ref, acc_ref, dq_ref, full_ref = refs
        dkv_refs = [dkv_ref]
    chunk = q_ref.shape[0]
    scaling = 1.0 / math.sqrt(DH)
    factor = LOG2E * scaling
    if first:
        dq_ref[...] = jnp.zeros_like(dq_ref)
    else:
        dq_ref[...] = dq_in[...]

    def body(qo, ko, tk, mask):
        rows = pl.ds(qo, tile)
        keys = pl.ds(ko, tk)
        k = kv_ref[keys, :DH]
        v = kv_ref[keys, DH:]
        qs = [q_ref[rows, h * DH : (h + 1) * DH] for h in range(heads)]
        gs = [g_ref[rows, h * DH : (h + 1) * DH] for h in range(heads)]
        scores = [dot(k, q, NT) for q in qs]
        dots = [dot(v, g, NT) for g in gs]
        scores = [jnp.where(mask, s, NEG) for s in scores]
        probs = [
            jnp.exp2(scores[h] * factor - log_ref[h : h + 1, rows]) for h in range(heads)
        ]
        ds = [
            (probs[h] * (dots[h] - delta_ref[h : h + 1, rows])).astype(jnp.bfloat16)
            for h in range(heads)
        ]
        probs = [p.astype(jnp.bfloat16) for p in probs]
        dv = dot(jnp.concatenate(probs, 1), jnp.concatenate(gs, 0), NN)
        dk = dot(jnp.concatenate(ds, 1), jnp.concatenate(qs, 0), NN)
        kt = kt_ref[:, keys]
        news = [dot(kt, x, NN) for x in ds]
        for h in range(heads):
            dq_ref[h * DH : (h + 1) * DH, rows] += news[h]
        acc_ref[keys, :DH] += dk
        acc_ref[keys, DH:] += dv

    def use(i, dist):
        acc_ref[...] = jnp.zeros_like(acc_ref)
        kt_ref[...] = kv_ref[:, :DH].T
        over_tiles(scal, docs, dist, chunk, tile, body)
        for j, ref in enumerate(dkv_refs):

            @pl.when(i == j)
            def _():
                ref[:, :DH] = (acc_ref[:, :DH] * scaling).astype(ref.dtype)
                ref[:, DH:] = acc_ref[:, DH:].astype(ref.dtype)

    each_chunk(scal, kv_refs, kv_ref, d, True, use)
    if team is not None:
        for h in range(heads):
            full_ref[:, h * DH : (h + 1) * DH] = (
                (dq_ref[h * DH : (h + 1) * DH, :] * scaling).T.astype(jnp.bfloat16)
            )
        size = chunk // team
        for m in range(team):
            outs[m][...] = full_ref[span(scal[2] ^ m, size), :]


def grads(
    scal, docs, tile, d, q, g, kvs, log_total, delta, dq, team=None, dtype=jnp.bfloat16, after=()
):
    chunk, width = q.shape
    heads = width // DH
    first = dq is None
    extra = () if first else (dq,)
    dkv_shapes = (jax.ShapeDtypeStruct((chunk, 2 * DH), dtype),) * len(kvs)
    scratch = [
        pltpu.VMEM((chunk, 2 * DH), jnp.bfloat16),
        pltpu.VMEM((DH, chunk), jnp.bfloat16),
        pltpu.VMEM((chunk, 2 * DH), jnp.float32),
    ]
    if team is None:
        shapes = (jax.ShapeDtypeStruct((width, chunk), jnp.float32),)
    else:
        shapes = (jax.ShapeDtypeStruct((chunk // team, width), jnp.bfloat16),) * team
        scratch += [
            pltpu.VMEM((width, chunk), jnp.float32),
            pltpu.VMEM((chunk, width), jnp.bfloat16),
        ]
    return ordered_call(
        functools.partial(grads_kernel, docs, tile, heads, d, first, team, len(kvs)),
        scal,
        (q, g, *kvs, log_total, delta, *extra),
        after,
        out_shape=shapes + dkv_shapes,
        out_specs=(whole(),) * (len(shapes) + len(kvs)),
        scratch_shapes=scratch,
        cost_estimate=cost(10 * chunk * chunk * width, 12 * chunk * width, chunk * chunk * heads),
        name="pair_grads",
    )


def project(scal, d, w, parts, far, blocks, begin, count, after=()):
    rows, depth = d.shape
    wide = w.shape[0] // blocks
    split = w.shape[1] // depth
    each = 0 if not parts else parts[0].shape[1] // wide

    def kernel(*refs):
        scal, d_ref, w_ref = refs[:3]
        total = dot(d_ref[...], w_ref[...], NT)
        if not parts:
            refs[-1][...] = total
            return
        outs = refs[3 + len(parts) + len(after) :]
        for m in range(count):

            @pl.when(pl.program_id(0) == m)
            def _():
                outs[m][...] = (total + refs[3 + m // each][...]).astype(outs[m].dtype)

    def column(s):
        if split == 1:
            return 0
        return 1 - s[3] if far else s[3]

    def part_spec(p):
        return pl.BlockSpec((rows, wide), lambda i, s: (0, jnp.clip(i - p * each, 0, each - 1)))

    w_spec = pl.BlockSpec((wide, depth), lambda i, s: (s[2] ^ (i + begin), column(s)))
    if parts:
        out_shape = (jax.ShapeDtypeStruct((rows, wide), jnp.bfloat16),) * count
        out_specs = (pl.BlockSpec((rows, wide), lambda i, s: (0, 0)),) * count
    else:
        out_shape = jax.ShapeDtypeStruct((rows, wide * count), jnp.float32)
        out_specs = pl.BlockSpec((rows, wide), lambda i, s: (0, i))
    grid_spec = pltpu.PrefetchScalarGridSpec(
        num_scalar_prefetch=1,
        grid=(count,),
        in_specs=[pl.BlockSpec((rows, depth), lambda i, s: (0, 0)), w_spec]
        + [part_spec(p) for p in range(len(parts))]
        + [whole(pl.ANY)] * len(after),
        out_specs=out_specs,
    )
    return pl.pallas_call(
        kernel,
        out_shape=out_shape,
        grid_spec=grid_spec,
        compiler_params=params(PROJECT_LIMIT),
        cost_estimate=cost(2 * rows * depth * wide * count, 2 * depth * wide * count),
        name="project",
    )(scal, d, w, *parts, *after)


def copies(scal, inputs, out_shapes, plan, name, after=()):
    n_in = len(inputs)

    def kernel(scal, *refs):
        ins, outs, sems = refs[:n_in], refs[n_in:-1], refs[-1]
        started = []
        for i, (a, src, b, dst) in enumerate(plan(scal[2])):
            copy = pltpu.make_async_copy(ins[a].at[src], outs[b].at[dst], sems.at[i])
            copy.start()
            started.append(copy)
        for copy in started:
            copy.wait()

    count = len(plan(0))
    size = sum(math.prod(s.shape) * 2 for s in out_shapes)
    return ordered_call(
        kernel,
        scal,
        inputs,
        after,
        out_shape=tuple(out_shapes),
        in_specs=[whole(pl.ANY)] * n_in,
        out_specs=(whole(pl.ANY),) * len(out_shapes),
        scratch_shapes=[pltpu.SemaphoreType.DMA((count,))],
        cost_estimate=cost(0, 2 * size),
        name=name,
    )


def add_kernel(a_ref, b_ref, out_ref):
    total = a_ref[...].astype(jnp.float32) + b_ref[...].astype(jnp.float32)
    out_ref[...] = total.astype(out_ref.dtype)


def add(a, b):
    return pl.pallas_call(
        add_kernel,
        out_shape=jax.ShapeDtypeStruct(a.shape, a.dtype),
        in_specs=[whole()] * 2,
        out_specs=whole(),
        compiler_params=params(),
        cost_estimate=cost(a.size, 6 * a.size),
        name="add_terms",
    )(a, b)


def span(start, size):
    if isinstance(start, int):
        return pl.ds(start, size)
    return pl.ds(pl.multiple_of(start * size, size), size)


ALL = slice(None)


def solution(mesh):
    n_seq = mesh.shape["seq"]
    n_head = mesh.shape["head"]

    def shards(queries, keys, values, d_out, w_out, doc_starts):
        rows = queries.shape[0]
        groups = keys.shape[1] // DH
        heads = queries.shape[1] // keys.shape[1]
        width = heads * DH
        docs = doc_starts.shape[0]
        team = groups
        layers = n_seq // team
        chunk = team * rows
        tile = 256 if chunk % 256 == 0 else rows
        me = lax.axis_index("seq")
        layer = me // team
        head = lax.axis_index("head")
        base = layer * chunk
        total = jnp.full((1,), chunk * layers, doc_starts.dtype)
        ends = jnp.concatenate([doc_starts[1:], total]) - 1
        far = jnp.max(ends // chunk - doc_starts // chunk) > 2
        scal = jnp.concatenate(
            [jnp.stack([base, base, me % team, head, far.astype(jnp.int32)]), doc_starts]
        )

        def half(*shape):
            return jax.ShapeDtypeStruct(shape, jnp.bfloat16)

        def swap(m, x):
            return lax.ppermute(x, "seq", [(i, i ^ m) for i in range(n_seq)])

        def swapped(parts):
            got = list(parts)
            for m in reversed(range(1, team)):
                got[m] = swap(m, parts[m])
            return got

        def shift(d, x):
            pairs = [(i, i + d * team) for i in range(n_seq) if 0 <= i + d * team < n_seq]
            return lax.ppermute(x, "seq", pairs)

        def pack(arrays, sizes, after=()):
            def kernel(scal, *refs):
                ins, outs = refs[: len(arrays)], refs[len(arrays) :]
                for m in range(team):
                    at = 0
                    for ref, size in zip(ins, sizes):
                        outs[m][:, at : at + size] = ref[:, span(scal[2] ^ m, size)]
                        at += size

            return ordered_call(
                kernel,
                scal,
                arrays,
                after,
                out_shape=[half(rows, sum(sizes))] * team,
                out_specs=[whole()] * team,
                name="pack_columns",
            )

        def stack(parts, sizes, name, after=()):
            def plan(place):
                out = []
                for m in range(team):
                    at = 0
                    for b, size in enumerate(sizes):
                        out.append((m, (ALL, pl.ds(at, size)), b, (span(place ^ m, rows), ALL)))
                        at += size
                return out

            return copies(scal, parts, [half(chunk, size) for size in sizes], plan, name, after)

        def beside(parts, sizes, name):
            def plan(place):
                out = []
                for m in range(team):
                    at = 0
                    for b, size in enumerate(sizes):
                        out.append((m, (ALL, pl.ds(at, size)), b, (ALL, span(place ^ m, size))))
                        at += size
                return out

            shapes = [half(rows, team * size) for size in sizes]
            return copies(scal, parts, shapes, plan, name)

        if n_head == 2:
            d_far = lax.ppermute(d_out, "head", [(0, 1), (1, 0)])
        if team > 1:
            kv_sent = pack([keys, values], [DH, DH])
            kv_got = swapped(kv_sent)
            near = []
            if n_head == 2:
                near.append(project(scal, d_out, w_out, (), False, team, 0, team, kv_sent[:1]))
            q_sent = pack([queries], [width], kv_sent[:1])
            q_got = swapped(q_sent)
            (kv,) = stack(kv_got, [2 * DH], "stack_keys_values", near + list(q_sent[:1]))
            order = (kv,)
        else:
            kv = jnp.concatenate([keys, values], axis=1)
            near = [project(scal, d_out, w_out, (), False, 1, 0, 1)] if n_head == 2 else []
            q = queries
            order = ()
        if n_head == 2:
            g_parts = project(scal, d_far, w_out, near, True, team, 0, team, order)
        else:
            d_all = lax.all_gather(d_out, "head", axis=1, tiled=True)
            zero = jnp.zeros((rows, width * team), jnp.float32)
            g_parts = project(scal, d_all, w_out, [zero], False, team, 0, team, order)
        if team > 1:
            g_got = swapped(g_parts)
            (q,) = stack(q_got, [width], "stack_queries", g_parts[:1])
        state = stats(scal, docs, tile, 0, q, [kv], None, g_parts[:1])

        def stack_g(after):
            if team > 1:
                return stack(g_got, [width], "stack_attn_grad", after)[0]
            return g_parts[0]

        if layers <= 4:
            steps = [[kv]] + [[shift(d, kv)] for d in range(1, min(layers, 3))]
            if layers == 4:
                steps[2].append(lax.cond(far, lambda x: shift(3, x), lambda x: x, kv))
            g = None
            for d in range(1, len(steps)):
                state = stats(
                    scal, docs, tile, d, q, steps[d], state, g_parts[:1] if g is None else (g,)
                )
                if g is None:
                    g = stack_g(state[:1])
            if g is None:
                g = stack_g(state[:1])
            log_total, delta = finish(g, *state)
            dq = None
            carried = None
            late = None
            for d in reversed(range(1, len(steps))):
                dq, dkv, *more = grads(scal, docs, tile, d, q, g, steps[d], log_total, delta, dq)
                if more:
                    late = lax.cond(far, lambda x: shift(-3, x), lambda x: x, more[0])
                if carried is not None:
                    dkv = add(dkv, carried)
                carried = shift(-1, dkv)
            *dq_parts, dkv = grads(
                scal, docs, tile, 0, q, g, [kv], log_total, delta, dq, team, jnp.float32
            )
            terms = [] if carried is None else [carried]
            if late is not None:
                terms.append(late)
        else:
            rings = [[z * team + a for z in range(layers)] for a in range(team)]
            every = lax.all_gather(kv, "seq", axis_index_groups=rings)

            def chunk_at(d):
                return lax.dynamic_index_in_dim(every, jnp.maximum(layer - d, 0), 0, keepdims=False)

            def scalars(d):
                return scal - jnp.where(jnp.arange(scal.shape[0]) == 1, d * chunk, 0)

            def one(d, state):
                return tuple(stats(scalars(d), docs, tile, 0, q, [chunk_at(d)], state))

            state = lax.fori_loop(1, layers, one, tuple(state))
            g = stack_g(())
            log_total, delta = finish(g, *state)

            def two(d, carry):
                dq, total = carry
                dq, dkv = grads(
                    scalars(d), docs, tile, 0, q, g, [chunk_at(d)], log_total, delta, dq
                )
                place = jnp.maximum(layer - d, 0)
                old = lax.dynamic_index_in_dim(total, place, 0, keepdims=False)
                total = lax.dynamic_update_index_in_dim(
                    total, jnp.where(layer >= d, dkv, old), place, 0
                )
                return dq, total

            dq = jnp.zeros((width, chunk), jnp.float32)
            total = jnp.zeros((layers, chunk, 2 * DH), jnp.bfloat16)
            dq, total = lax.fori_loop(1, layers, two, (dq, total))
            *dq_parts, dkv = grads(
                scal, docs, tile, 0, q, g, [kv], log_total, delta, dq, team, jnp.float32
            )
            terms = [
                lax.psum_scatter(
                    total.reshape(layers * chunk, 2 * DH), "seq", axis_index_groups=rings, tiled=True
                )
            ]

        def sum_kernel(scal, *refs):
            total = refs[0][...]
            for i, x in enumerate(refs[1 : 1 + len(terms)]):
                term = x[...].astype(jnp.float32)
                total = total + (term if i == 0 else jnp.where(scal[FAR] > 0, term, 0.0))
            full = refs[-1]
            full[...] = total.astype(jnp.bfloat16)
            for m in range(team):
                refs[1 + len(terms) + m][...] = full[span(scal[2] ^ m, rows), :]

        dkv_parts = pl.pallas_call(
            sum_kernel,
            out_shape=(half(rows, 2 * DH),) * team,
            in_specs=[whole(pltpu.SMEM)] + [whole()] * (1 + len(terms)),
            out_specs=(whole(),) * team,
            scratch_shapes=[pltpu.VMEM((chunk, 2 * DH), jnp.bfloat16)],
            compiler_params=params(),
            name="sum_terms",
        )(scal, dkv, *terms)
        if team > 1:
            dq_parts = swapped(dq_parts)
            dkv_parts = swapped(dkv_parts)
            (query_grad,) = beside(dq_parts, [width], "place_query_grad")
            key_grad, value_grad = beside(dkv_parts, [DH, DH], "place_key_value_grad")
        else:
            query_grad = dq_parts[0]
            key_grad = dkv_parts[0][:, :DH]
            value_grad = dkv_parts[0][:, DH:]
        return (query_grad, key_grad, value_grad)

    return jax.shard_map(
        shards,
        mesh=mesh,
        in_specs=(
            P("seq", "head"),
            P("seq", "head"),
            P("seq", "head"),
            P("seq", "head"),
            P("head", None),
            P(),
        ),
        out_specs=(P("seq", "head"), P("seq", "head"), P("seq", "head")),
        check_vma=False,
    )
```

```python
import functools
import math

import jax
import jax.numpy as jnp
from jax import lax
from jax.experimental import pallas as pl
from jax.experimental.pallas import tpu as pltpu
from jax.sharding import PartitionSpec as P

DH = 128
ONES = 16
LOG2E = 1.4426950408889634
NEG = -1e30
VMEM_LIMIT = 28 * 1024 * 1024
PROJECT_LIMIT = 47 * 1024 * 1024

NT = (((1,), (1,)), ((), ()))
NN = (((1,), (0,)), ((), ()))


def dot(a, b, dims):
    return lax.dot_general(a, b, dims, preferred_element_type=jnp.float32)


def params(limit=VMEM_LIMIT):
    return pltpu.CompilerParams(vmem_limit_bytes=limit)


def whole(memory_space=pltpu.VMEM):
    return pl.BlockSpec(memory_space=memory_space)


def ordered_call(kernel, scal, operands, after, **kwargs):
    count = len(after)

    def body(*refs):
        kernel(*refs[: 1 + len(operands)], *refs[1 + len(operands) + count :])

    specs = kwargs.pop("in_specs", [whole()] * len(operands))
    return pl.pallas_call(
        body,
        in_specs=[whole(pltpu.SMEM)] + specs + [whole(pl.ANY)] * count,
        compiler_params=params(),
        **kwargs,
    )(scal, *operands, *after)


def cost(flops, nbytes, exps=0):
    return pl.CostEstimate(flops=1024, bytes_accessed=1024, transcendentals=0)


FIRST_DOC = 4


def row_starts(scal, docs, pos):
    low = jnp.zeros_like(pos)
    for n in range(docs):
        low = jnp.where(pos >= scal[FIRST_DOC + n], scal[FIRST_DOC + n], low)
    return low


def reaches_far(starts, docs, chunk, total):
    far = jnp.int32(0)
    for n in range(docs):
        end = (starts[n + 1] if n + 1 < docs else total) - 1
        far = jnp.where(end // chunk - starts[n] // chunk > 2, 1, far)
    return far


def doc_start_at(scal, docs, pos):
    low = jnp.int32(0)
    for n in range(docs):
        low = jnp.where(pos >= scal[FIRST_DOC + n], scal[FIRST_DOC + n], low)
    return low


def allowed(scal, docs, q0, k0, tq, tk):
    qpos = q0 + lax.broadcasted_iota(jnp.int32, (1, tq), 1)
    kpos = k0 + lax.broadcasted_iota(jnp.int32, (tk, 1), 0)
    return (kpos <= qpos) & (kpos >= row_starts(scal, docs, qpos))


def over_tiles(scal, docs, d, chunk, tile, body):
    tiles = chunk // tile

    def one(qo, ko, q0, tk, need):
        k0 = scal[1] - d * chunk + ko
        @pl.when(need)
        def _():
            body(qo, ko, tk, allowed(scal, docs, q0, k0, tile, tk))

    def step(qt, _):
        qo = pl.multiple_of(qt * tile, tile)
        q0 = scal[0] + qo
        low = doc_start_at(scal, docs, q0)
        k0 = scal[1] - d * chunk
        if tiles == 1:
            one(qo, 0, q0, tile, (k0 <= q0 + tile - 1) & (k0 + tile - 1 >= low))
            return 0
        all_of = (k0 + chunk - tile <= q0 + tile - 1) & (k0 + tile - 1 >= low)
        one(qo, 0, q0, chunk, all_of)

        @pl.when(jnp.logical_not(all_of))
        def _():
            def inner(kt, _):
                ko = pl.multiple_of(kt * tile, tile)
                need = (k0 + ko <= q0 + tile - 1) & (k0 + ko + tile - 1 >= low)
                one(qo, ko, q0, tile, need)
                return 0

            lax.fori_loop(0, tiles, inner, 0)

        return 0

    lax.fori_loop(0, tiles, step, 0)


def far_scalar(scal, docs, chunk, layers):
    return reaches_far([scal[FIRST_DOC + n] for n in range(docs)], docs, chunk, chunk * layers)


def each_chunk(far, kv_refs, now_ref, d, down, use):
    count = len(kv_refs)
    if count == 1:
        now_ref[...] = kv_refs[0][...]
        use(0, d)
        return

    def one(i, _):
        for j, ref in enumerate(kv_refs):

            @pl.when(i == j)
            def _():
                now_ref[...] = ref[...]

        use(i, d + i)
        return 0

    total = 1 + (count - 1) * far
    if down:
        lax.fori_loop(0, total, lambda i, c: one(total - 1 - i, c), 0)
    else:
        lax.fori_loop(0, total, one, 0)


def stats_kernel(docs, layers, tile, heads, d, first, count, scal, q_ref, *refs):
    kv_refs, refs = refs[:count], refs[count:]
    if first:
        m_ref, o_ref, kv_ref, vt_ref = refs
        m_ref[...] = jnp.full_like(m_ref, NEG)
        o_ref[...] = jnp.zeros_like(o_ref)
    else:
        m_in, o_in, m_ref, o_ref, kv_ref, vt_ref = refs
        m_ref[...] = m_in[...]
        o_ref[...] = o_in[...]
    chunk = q_ref.shape[0]
    factor = LOG2E / math.sqrt(DH)
    ext = DH + ONES
    vt_ref[DH:] = jnp.ones((vt_ref.shape[0] - DH, chunk), jnp.bfloat16)

    def body(qo, ko, tk, mask):
        k = kv_ref[pl.ds(ko, tk), :DH]
        vt = vt_ref[:ext, pl.ds(ko, tk)]
        rows = pl.ds(qo, tile)
        scores = [dot(k, q_ref[rows, h * DH : (h + 1) * DH], NT) for h in range(heads)]
        scores = [jnp.where(mask, s, NEG) for s in scores]
        m_old = [m_ref[h : h + 1, rows] for h in range(heads)]
        m_new = [
            jnp.maximum(m, factor * jnp.max(s, axis=0, keepdims=True))
            for m, s in zip(m_old, scores)
        ]
        alpha = [jnp.exp2(a - b) for a, b in zip(m_old, m_new)]
        probs = [jnp.exp2(s * factor - m).astype(jnp.bfloat16) for s, m in zip(scores, m_new)]
        news = [dot(vt, p, NN) for p in probs]
        for h in range(heads):
            part = slice(h * ext, (h + 1) * ext)
            m_ref[h : h + 1, rows] = m_new[h]
            o_ref[part, rows] = alpha[h] * o_ref[part, rows] + news[h]

    def use(i, dist):
        vt_ref[:DH] = kv_ref[:, DH:].T
        over_tiles(scal, docs, dist, chunk, tile, body)

    each_chunk(far_scalar(scal, docs, chunk, layers), kv_refs, kv_ref, d, False, use)


def stats(scal, docs, layers, tile, d, q, kvs, state, after=()):
    chunk, width = q.shape
    heads = width // DH
    shapes = (
        jax.ShapeDtypeStruct((heads, chunk), jnp.float32),
        jax.ShapeDtypeStruct((heads * (DH + ONES), chunk), jnp.float32),
    )
    first = state is None
    extra = () if first else state
    return ordered_call(
        functools.partial(stats_kernel, docs, layers, tile, heads, d, first, len(kvs)),
        scal,
        (q, *kvs, *extra),
        after,
        out_shape=shapes,
        out_specs=(whole(),) * 2,
        scratch_shapes=[
            pltpu.VMEM((chunk, 2 * DH), jnp.bfloat16),
            pltpu.VMEM((DH + ONES, chunk), jnp.bfloat16),
        ],
        cost_estimate=cost(4 * chunk * chunk * width, 12 * chunk * width, chunk * chunk * heads),
        name="row_stats",
    )


def finish_kernel(heads, g_ref, m_ref, o_ref, log_ref, delta_ref):
    ext = DH + ONES
    for h in range(heads):
        total = o_ref[h * ext + DH : h * ext + DH + 1, :]
        gt = g_ref[:, h * DH : (h + 1) * DH].T.astype(jnp.float32)
        part = jnp.sum(gt * o_ref[h * ext : h * ext + DH, :], axis=0, keepdims=True)
        log_ref[h : h + 1, :] = m_ref[h : h + 1, :] + jnp.log2(total)
        delta_ref[h : h + 1, :] = part / total


def finish(g, m, o):
    heads, chunk = m.shape
    shape = jax.ShapeDtypeStruct((heads, chunk), jnp.float32)
    return pl.pallas_call(
        functools.partial(finish_kernel, heads),
        out_shape=(shape, shape),
        in_specs=[whole()] * 3,
        out_specs=(whole(),) * 2,
        compiler_params=params(),
        cost_estimate=cost(2 * chunk * heads * DH, 6 * chunk * heads * DH),
        name="row_delta",
    )(g, m, o)


def grads_kernel(docs, layers, tile, heads, d, first, team, count, scal, q_ref, g_ref, *refs):
    kv_refs, refs = refs[:count], refs[count:]
    log_ref, delta_ref, refs = refs[0], refs[1], refs[2:]
    if not first:
        dq_in, refs = refs[0], refs[1:]
    if team is None:
        dq_ref, *dkv_refs, kv_ref, kt_ref, acc_ref = refs
    else:
        *outs, dkv_ref, kv_ref, kt_ref, acc_ref, dq_ref, full_ref = refs
        dkv_refs = [dkv_ref]
    chunk = q_ref.shape[0]
    scaling = 1.0 / math.sqrt(DH)
    factor = LOG2E * scaling
    if first:
        dq_ref[...] = jnp.zeros_like(dq_ref)
    else:
        dq_ref[...] = dq_in[...]

    def body(qo, ko, tk, mask):
        rows = pl.ds(qo, tile)
        keys = pl.ds(ko, tk)
        k = kv_ref[keys, :DH]
        v = kv_ref[keys, DH:]
        qs = [q_ref[rows, h * DH : (h + 1) * DH] for h in range(heads)]
        gs = [g_ref[rows, h * DH : (h + 1) * DH] for h in range(heads)]
        scores = [dot(k, q, NT) for q in qs]
        dots = [dot(v, g, NT) for g in gs]
        scores = [jnp.where(mask, s, NEG) for s in scores]
        probs = [
            jnp.exp2(scores[h] * factor - log_ref[h : h + 1, rows]) for h in range(heads)
        ]
        ds = [
            (probs[h] * (dots[h] - delta_ref[h : h + 1, rows])).astype(jnp.bfloat16)
            for h in range(heads)
        ]
        probs = [p.astype(jnp.bfloat16) for p in probs]
        dv = dot(jnp.concatenate(probs, 1), jnp.concatenate(gs, 0), NN)
        dk = dot(jnp.concatenate(ds, 1), jnp.concatenate(qs, 0), NN)
        kt = kt_ref[:, keys]
        news = [dot(kt, x, NN) for x in ds]
        for h in range(heads):
            dq_ref[h * DH : (h + 1) * DH, rows] += news[h]
        acc_ref[keys, :DH] += dk
        acc_ref[keys, DH:] += dv

    def use(i, dist):
        acc_ref[...] = jnp.zeros_like(acc_ref)
        kt_ref[...] = kv_ref[:, :DH].T
        over_tiles(scal, docs, dist, chunk, tile, body)
        for j, ref in enumerate(dkv_refs):

            @pl.when(i == j)
            def _():
                ref[:, :DH] = (acc_ref[:, :DH] * scaling).astype(ref.dtype)
                ref[:, DH:] = acc_ref[:, DH:].astype(ref.dtype)

    each_chunk(far_scalar(scal, docs, chunk, layers), kv_refs, kv_ref, d, True, use)
    if team is not None:
        for h in range(heads):
            full_ref[:, h * DH : (h + 1) * DH] = (
                (dq_ref[h * DH : (h + 1) * DH, :] * scaling).T.astype(jnp.bfloat16)
            )
        size = chunk // team
        for m in range(team):
            outs[m][...] = full_ref[span(scal[2] ^ m, size), :]


def grads(
    scal, docs, layers, tile, d, q, g, kvs, log_total, delta, dq, team=None, dtype=jnp.bfloat16
):
    chunk, width = q.shape
    heads = width // DH
    first = dq is None
    extra = () if first else (dq,)
    dkv_shapes = (jax.ShapeDtypeStruct((chunk, 2 * DH), dtype),) * len(kvs)
    scratch = [
        pltpu.VMEM((chunk, 2 * DH), jnp.bfloat16),
        pltpu.VMEM((DH, chunk), jnp.bfloat16),
        pltpu.VMEM((chunk, 2 * DH), jnp.float32),
    ]
    if team is None:
        shapes = (jax.ShapeDtypeStruct((width, chunk), jnp.float32),)
    else:
        shapes = (jax.ShapeDtypeStruct((chunk // team, width), jnp.bfloat16),) * team
        scratch += [
            pltpu.VMEM((width, chunk), jnp.float32),
            pltpu.VMEM((chunk, width), jnp.bfloat16),
        ]
    return ordered_call(
        functools.partial(grads_kernel, docs, layers, tile, heads, d, first, team, len(kvs)),
        scal,
        (q, g, *kvs, log_total, delta, *extra),
        (),
        out_shape=shapes + dkv_shapes,
        out_specs=(whole(),) * (len(shapes) + len(kvs)),
        scratch_shapes=scratch,
        cost_estimate=cost(10 * chunk * chunk * width, 12 * chunk * width, chunk * chunk * heads),
        name="pair_grads",
    )


def project(scal, d, w, parts, far, blocks, begin, count, after=()):
    rows, depth = d.shape
    wide = w.shape[0] // blocks
    split = w.shape[1] // depth
    each = 0 if not parts else parts[0].shape[1] // wide

    def kernel(*refs):
        scal, d_ref, w_ref = refs[:3]
        total = dot(d_ref[...], w_ref[...], NT)
        if not parts:
            refs[-1][...] = total
            return
        outs = refs[3 + len(parts) + len(after) :]
        for m in range(count):

            @pl.when(pl.program_id(0) == m)
            def _():
                outs[m][...] = (total + refs[3 + m // each][...]).astype(outs[m].dtype)

    def column(s):
        if split == 1:
            return 0
        return 1 - s[3] if far else s[3]

    def part_spec(p):
        return pl.BlockSpec((rows, wide), lambda i, s: (0, jnp.clip(i - p * each, 0, each - 1)))

    w_spec = pl.BlockSpec((wide, depth), lambda i, s: (s[2] ^ (i + begin), column(s)))
    if parts:
        out_shape = (jax.ShapeDtypeStruct((rows, wide), jnp.bfloat16),) * count
        out_specs = (pl.BlockSpec((rows, wide), lambda i, s: (0, 0)),) * count
    else:
        out_shape = jax.ShapeDtypeStruct((rows, wide * count), jnp.float32)
        out_specs = pl.BlockSpec((rows, wide), lambda i, s: (0, i))
    grid_spec = pltpu.PrefetchScalarGridSpec(
        num_scalar_prefetch=1,
        grid=(count,),
        in_specs=[pl.BlockSpec((rows, depth), lambda i, s: (0, 0)), w_spec]
        + [part_spec(p) for p in range(len(parts))]
        + [whole(pl.ANY)] * len(after),
        out_specs=out_specs,
    )
    return pl.pallas_call(
        kernel,
        out_shape=out_shape,
        grid_spec=grid_spec,
        compiler_params=params(PROJECT_LIMIT),
        cost_estimate=cost(2 * rows * depth * wide * count, 2 * depth * wide * count),
        name="project",
    )(scal, d, w, *parts, *after)


def copies(scal, inputs, out_shapes, plan, name, after=()):
    n_in = len(inputs)

    def kernel(scal, *refs):
        ins, outs, sems = refs[:n_in], refs[n_in:-1], refs[-1]
        started = []
        for i, (a, src, b, dst) in enumerate(plan(scal[2])):
            copy = pltpu.make_async_copy(ins[a].at[src], outs[b].at[dst], sems.at[i])
            copy.start()
            started.append(copy)
        for copy in started:
            copy.wait()

    count = len(plan(0))
    size = sum(math.prod(s.shape) * 2 for s in out_shapes)
    return ordered_call(
        kernel,
        scal,
        inputs,
        after,
        out_shape=tuple(out_shapes),
        in_specs=[whole(pl.ANY)] * n_in,
        out_specs=(whole(pl.ANY),) * len(out_shapes),
        scratch_shapes=[pltpu.SemaphoreType.DMA((count,))],
        cost_estimate=cost(0, 2 * size),
        name=name,
    )


def add(scal, a, b, after):
    def kernel(scal, a_ref, b_ref, out_ref):
        total = a_ref[...].astype(jnp.float32) + b_ref[...].astype(jnp.float32)
        out_ref[...] = total.astype(out_ref.dtype)

    return ordered_call(
        kernel,
        scal,
        (a, b),
        after,
        out_shape=jax.ShapeDtypeStruct(a.shape, a.dtype),
        out_specs=whole(),
        cost_estimate=cost(a.size, 6 * a.size),
        name="add_terms",
    )


def span(start, size):
    if isinstance(start, int):
        return pl.ds(start, size)
    return pl.ds(pl.multiple_of(start * size, size), size)


ALL = slice(None)


def solution(mesh):
    n_seq = mesh.shape["seq"]
    n_head = mesh.shape["head"]

    def shards(queries, keys, values, d_out, w_out, doc_starts):
        rows = queries.shape[0]
        groups = keys.shape[1] // DH
        heads = queries.shape[1] // keys.shape[1]
        width = heads * DH
        docs = doc_starts.shape[0]
        team = groups
        layers = n_seq // team
        chunk = team * rows
        tile = 256 if chunk % 256 == 0 else rows
        me = lax.axis_index("seq")
        layer = me // team
        head = lax.axis_index("head")
        base = layer * chunk
        scal = jnp.concatenate([jnp.stack([base, base, me % team, head]), doc_starts])
        far = reaches_far(doc_starts, docs, chunk, chunk * layers) > 0

        def half(*shape):
            return jax.ShapeDtypeStruct(shape, jnp.bfloat16)

        def swap(m, x):
            return lax.ppermute(x, "seq", [(i, i ^ m) for i in range(n_seq)])

        def swapped(parts):
            got = list(parts)
            for m in reversed(range(1, team)):
                got[m] = swap(m, parts[m])
            return got

        def shift(d, x):
            pairs = [(i, i + d * team) for i in range(n_seq) if 0 <= i + d * team < n_seq]
            return lax.ppermute(x, "seq", pairs)

        def pack(groups_of):
            arrays = [x for group in groups_of for x, _ in group]

            def kernel(scal, *refs):
                ins, outs = list(refs[: len(arrays)]), list(refs[len(arrays) :])
                for group in groups_of:
                    own, ins = ins[: len(group)], ins[len(group) :]
                    for m in range(team):
                        at = 0
                        out = outs.pop(0)
                        for ref, (_, size) in zip(own, group):
                            out[:, at : at + size] = ref[:, span(scal[2] ^ m, size)]
                            at += size

            shapes = [half(rows, sum(n for _, n in group)) for group in groups_of for _ in range(team)]
            outs = ordered_call(
                kernel,
                scal,
                arrays,
                (),
                out_shape=shapes,
                out_specs=[whole()] * len(shapes),
                name="pack_columns",
            )
            return [outs[i : i + team] for i in range(0, len(outs), team)]

        def stack(parts, sizes, name, after=(), also=()):
            def plan(place):
                out = []
                for m in range(team):
                    at = 0
                    for b, size in enumerate(sizes):
                        out.append((m, (ALL, pl.ds(at, size)), b, (span(place ^ m, rows), ALL)))
                        at += size
                for i in range(len(also)):
                    out.append((team + i, (ALL, ALL), len(sizes) + i, (ALL, ALL)))
                return out

            shapes = [half(chunk, size) for size in sizes] + [half(*x.shape) for x in also]
            return copies(scal, list(parts) + list(also), shapes, plan, name, after)

        def beside(parts, sizes, name):
            def plan(place):
                out = []
                for m in range(team):
                    at = 0
                    for b, size in enumerate(sizes):
                        out.append((m, (ALL, pl.ds(at, size)), b, (ALL, span(place ^ m, size))))
                        at += size
                return out

            shapes = [half(rows, team * size) for size in sizes]
            return copies(scal, parts, shapes, plan, name)

        if n_head == 2:
            d_far = lax.ppermute(d_out, "head", [(0, 1), (1, 0)])
        if team > 1:
            kv_sent, q_sent = pack([[(keys, DH), (values, DH)], [(queries, width)]])
            kv_got = swapped(kv_sent)
            q_got = swapped(q_sent)
            near = []
            if n_head == 2:
                near.append(project(scal, d_out, w_out, (), False, team, 0, team, kv_sent[:1]))
            (kv,) = stack(kv_got, [2 * DH], "stack_keys_values", near + list(q_sent[:1]))
            order = (kv,)
        else:
            kv = jnp.concatenate([keys, values], axis=1)
            near = [project(scal, d_out, w_out, (), False, 1, 0, 1)] if n_head == 2 else []
            q = queries
            order = ()
        if n_head == 2:
            g_parts = project(scal, d_far, w_out, near, True, team, 0, team, order)
        else:
            d_all = lax.all_gather(d_out, "head", axis=1, tiled=True)
            zero = jnp.zeros((rows, width * team), jnp.float32)
            g_parts = project(scal, d_all, w_out, [zero], False, team, 0, team, order)
        if team > 1:
            g_got = swapped(g_parts)
            (q,) = stack(q_got, [width], "stack_queries", g_parts[:1])
        state = stats(scal, docs, layers, tile, 0, q, [kv], None, g_parts[:1])

        def stack_g(after, also=()):
            if team > 1:
                return stack(g_got, [width], "stack_attn_grad", after, also)
            return (g_parts[0], *also)

        if layers <= 4:
            steps = [[kv]] + [[shift(d, kv)] for d in range(1, min(layers, 3))]
            g = None
            for d in range(1, len(steps)):
                state = stats(
                    scal, docs, layers, tile, d, q, steps[d], state, g_parts[:1] if g is None else (g,)
                )
                if g is None:
                    g, kv_again = stack_g(state[:1], (kv,))
                    if layers == 4:
                        third = lax.cond(far, lambda x: shift(3, x), lambda x: x, kv_again)
                        steps[2].append(third)
            if g is None:
                (g,) = stack_g(state[:1])
            log_total, delta = finish(g, *state)
            dq = None
            late = None
            sums = []
            for d in reversed(range(1, len(steps))):
                dq, dkv, *more = grads(
                    scal, docs, layers, tile, d, q, g, steps[d], log_total, delta, dq
                )
                if more:
                    late = lax.cond(far, lambda x: shift(-3, x), lambda x: x, more[0])
                sums.append(dkv)
            *dq_parts, dkv = grads(
                scal, docs, layers, tile, 0, q, g, [kv], log_total, delta, dq, team, jnp.float32
            )
            carried = None
            for x in sums:
                carried = shift(-1, x if carried is None else add(scal, x, carried, (dkv,)))
            terms = [] if carried is None else [carried]
            if late is not None:
                terms.append(late)
        else:
            rings = [[z * team + a for z in range(layers)] for a in range(team)]
            every = lax.all_gather(kv, "seq", axis_index_groups=rings)

            def chunk_at(d):
                return lax.dynamic_index_in_dim(every, jnp.maximum(layer - d, 0), 0, keepdims=False)

            def scalars(d):
                return scal - jnp.where(jnp.arange(scal.shape[0]) == 1, d * chunk, 0)

            def one(d, state):
                return tuple(stats(scalars(d), docs, layers, tile, 0, q, [chunk_at(d)], state))

            state = lax.fori_loop(1, layers, one, tuple(state))
            (g,) = stack_g(())
            log_total, delta = finish(g, *state)

            def two(d, carry):
                dq, total = carry
                dq, dkv = grads(
                    scalars(d), docs, layers, tile, 0, q, g, [chunk_at(d)], log_total, delta, dq
                )
                place = jnp.maximum(layer - d, 0)
                old = lax.dynamic_index_in_dim(total, place, 0, keepdims=False)
                total = lax.dynamic_update_index_in_dim(
                    total, jnp.where(layer >= d, dkv, old), place, 0
                )
                return dq, total

            dq = jnp.zeros((width, chunk), jnp.float32)
            total = jnp.zeros((layers, chunk, 2 * DH), jnp.bfloat16)
            dq, total = lax.fori_loop(1, layers, two, (dq, total))
            *dq_parts, dkv = grads(
                scal, docs, layers, tile, 0, q, g, [kv], log_total, delta, dq, team, jnp.float32
            )
            terms = [
                lax.psum_scatter(
                    total.reshape(layers * chunk, 2 * DH), "seq", axis_index_groups=rings, tiled=True
                )
            ]

        def sum_kernel(scal, *refs):
            total = refs[0][...]
            many = far_scalar(scal, docs, chunk, layers) > 0
            for i, x in enumerate(refs[1 : 1 + len(terms)]):
                term = x[...].astype(jnp.float32)
                total = total + (term if i == 0 else jnp.where(many, term, 0.0))
            full = refs[-1]
            full[...] = total.astype(jnp.bfloat16)
            for m in range(team):
                refs[1 + len(terms) + m][...] = full[span(scal[2] ^ m, rows), :]

        dkv_parts = pl.pallas_call(
            sum_kernel,
            out_shape=(half(rows, 2 * DH),) * team,
            in_specs=[whole(pltpu.SMEM)] + [whole()] * (1 + len(terms)),
            out_specs=(whole(),) * team,
            scratch_shapes=[pltpu.VMEM((chunk, 2 * DH), jnp.bfloat16)],
            compiler_params=params(),
            name="sum_terms",
        )(scal, dkv, *terms)
        if team > 1:
            dq_parts = swapped(dq_parts)
            dkv_parts = swapped(dkv_parts)
            (query_grad,) = beside(dq_parts, [width], "place_query_grad")
            key_grad, value_grad = beside(dkv_parts, [DH, DH], "place_key_value_grad")
        else:
            query_grad = dq_parts[0]
            key_grad = dkv_parts[0][:, :DH]
            value_grad = dkv_parts[0][:, DH:]
        return (query_grad, key_grad, value_grad)

    return jax.shard_map(
        shards,
        mesh=mesh,
        in_specs=(
            P("seq", "head"),
            P("seq", "head"),
            P("seq", "head"),
            P("seq", "head"),
            P("head", None),
            P(),
        ),
        out_specs=(P("seq", "head"), P("seq", "head"), P("seq", "head")),
        check_vma=False,
    )
```

```python
import functools
import math

import jax
import jax.numpy as jnp
from jax import lax
from jax.experimental import pallas as pl
from jax.experimental.pallas import tpu as pltpu
from jax.sharding import PartitionSpec as P

DH = 128
ONES = 16
LOG2E = 1.4426950408889634
NEG = -1e30
VMEM_LIMIT = 28 * 1024 * 1024
PROJECT_LIMIT = 52 * 1024 * 1024

NT = (((1,), (1,)), ((), ()))
NN = (((1,), (0,)), ((), ()))


def dot(a, b, dims):
    return lax.dot_general(a, b, dims, preferred_element_type=jnp.float32)


def params(limit=VMEM_LIMIT):
    return pltpu.CompilerParams(vmem_limit_bytes=limit)


def whole(memory_space=pltpu.VMEM):
    return pl.BlockSpec(memory_space=memory_space)


def ordered_call(kernel, scal, operands, after, **kwargs):
    count = len(after)

    def body(*refs):
        kernel(*refs[: 1 + len(operands)], *refs[1 + len(operands) + count :])

    specs = kwargs.pop("in_specs", [whole()] * len(operands))
    return pl.pallas_call(
        body,
        in_specs=[whole(pltpu.SMEM)] + specs + [whole(pl.ANY)] * count,
        compiler_params=params(),
        **kwargs,
    )(scal, *operands, *after)


def cost(flops, nbytes, exps=0):
    return pl.CostEstimate(flops=1024, bytes_accessed=1024, transcendentals=0)


FIRST_DOC = 4


def row_starts(scal, docs, pos):
    low = jnp.zeros_like(pos)
    for n in range(docs):
        low = jnp.where(pos >= scal[FIRST_DOC + n], scal[FIRST_DOC + n], low)
    return low


def reaches_far(starts, docs, chunk, total):
    far = jnp.int32(0)
    for n in range(docs):
        end = (starts[n + 1] if n + 1 < docs else total) - 1
        far = jnp.where(end // chunk - starts[n] // chunk > 2, 1, far)
    return far


def doc_start_at(scal, docs, pos):
    low = jnp.int32(0)
    for n in range(docs):
        low = jnp.where(pos >= scal[FIRST_DOC + n], scal[FIRST_DOC + n], low)
    return low


def allowed(scal, docs, q0, k0, tq, tk):
    qpos = q0 + lax.broadcasted_iota(jnp.int32, (1, tq), 1)
    kpos = k0 + lax.broadcasted_iota(jnp.int32, (tk, 1), 0)
    return (kpos <= qpos) & (kpos >= row_starts(scal, docs, qpos))


def over_tiles(scal, docs, d, chunk, tile, body):
    tiles = chunk // tile

    def one(qo, ko, q0, tk, need):
        k0 = scal[1] - d * chunk + ko
        @pl.when(need)
        def _():
            body(qo, ko, tk, allowed(scal, docs, q0, k0, tile, tk))

    def step(qt, _):
        qo = pl.multiple_of(qt * tile, tile)
        q0 = scal[0] + qo
        low = doc_start_at(scal, docs, q0)
        k0 = scal[1] - d * chunk
        if tiles == 1:
            one(qo, 0, q0, tile, (k0 <= q0 + tile - 1) & (k0 + tile - 1 >= low))
            return 0
        all_of = (k0 + chunk - tile <= q0 + tile - 1) & (k0 + tile - 1 >= low)
        one(qo, 0, q0, chunk, all_of)

        @pl.when(jnp.logical_not(all_of))
        def _():
            def inner(kt, _):
                ko = pl.multiple_of(kt * tile, tile)
                need = (k0 + ko <= q0 + tile - 1) & (k0 + ko + tile - 1 >= low)
                one(qo, ko, q0, tile, need)
                return 0

            lax.fori_loop(0, tiles, inner, 0)

        return 0

    lax.fori_loop(0, tiles, step, 0)


def far_scalar(scal, docs, chunk, layers):
    return reaches_far([scal[FIRST_DOC + n] for n in range(docs)], docs, chunk, chunk * layers)


def each_chunk(far, kv_refs, now_ref, d, down, use):
    count = len(kv_refs)
    if count == 1:
        now_ref[...] = kv_refs[0][...]
        use(0, d)
        return

    def one(i, _):
        for j, ref in enumerate(kv_refs):

            @pl.when(i == j)
            def _():
                now_ref[...] = ref[...]

        use(i, d + i)
        return 0

    total = 1 + (count - 1) * far
    if down:
        lax.fori_loop(0, total, lambda i, c: one(total - 1 - i, c), 0)
    else:
        lax.fori_loop(0, total, one, 0)


def stats_kernel(docs, layers, tile, heads, d, first, count, scal, q_ref, *refs):
    kv_refs, refs = refs[:count], refs[count:]
    if first:
        m_ref, o_ref, kv_ref, vt_ref = refs
        m_ref[...] = jnp.full_like(m_ref, NEG)
        o_ref[...] = jnp.zeros_like(o_ref)
    else:
        m_in, o_in, m_ref, o_ref, kv_ref, vt_ref = refs
        m_ref[...] = m_in[...]
        o_ref[...] = o_in[...]
    chunk = q_ref.shape[0]
    factor = LOG2E / math.sqrt(DH)
    ext = DH + ONES
    vt_ref[DH:] = jnp.ones((vt_ref.shape[0] - DH, chunk), jnp.bfloat16)

    def body(qo, ko, tk, mask):
        k = kv_ref[pl.ds(ko, tk), :DH]
        vt = vt_ref[:ext, pl.ds(ko, tk)]
        rows = pl.ds(qo, tile)
        scores = [dot(k, q_ref[rows, h * DH : (h + 1) * DH], NT) for h in range(heads)]
        scores = [jnp.where(mask, s, NEG) for s in scores]
        m_old = [m_ref[h : h + 1, rows] for h in range(heads)]
        m_new = [
            jnp.maximum(m, factor * jnp.max(s, axis=0, keepdims=True))
            for m, s in zip(m_old, scores)
        ]
        alpha = [jnp.exp2(a - b) for a, b in zip(m_old, m_new)]
        probs = [jnp.exp2(s * factor - m).astype(jnp.bfloat16) for s, m in zip(scores, m_new)]
        news = [dot(vt, p, NN) for p in probs]
        for h in range(heads):
            part = slice(h * ext, (h + 1) * ext)
            m_ref[h : h + 1, rows] = m_new[h]
            o_ref[part, rows] = alpha[h] * o_ref[part, rows] + news[h]

    def use(i, dist):
        vt_ref[:DH] = kv_ref[:, DH:].T
        over_tiles(scal, docs, dist, chunk, tile, body)

    each_chunk(far_scalar(scal, docs, chunk, layers), kv_refs, kv_ref, d, False, use)


def stats(scal, docs, layers, tile, d, q, kvs, state, after=()):
    chunk, width = q.shape
    heads = width // DH
    shapes = (
        jax.ShapeDtypeStruct((heads, chunk), jnp.float32),
        jax.ShapeDtypeStruct((heads * (DH + ONES), chunk), jnp.float32),
    )
    first = state is None
    extra = () if first else state
    return ordered_call(
        functools.partial(stats_kernel, docs, layers, tile, heads, d, first, len(kvs)),
        scal,
        (q, *kvs, *extra),
        after,
        out_shape=shapes,
        out_specs=(whole(),) * 2,
        scratch_shapes=[
            pltpu.VMEM((chunk, 2 * DH), jnp.bfloat16),
            pltpu.VMEM((DH + ONES, chunk), jnp.bfloat16),
        ],
        cost_estimate=cost(4 * chunk * chunk * width, 12 * chunk * width, chunk * chunk * heads),
        name="row_stats",
    )


def finish_kernel(heads, g_ref, m_ref, o_ref, log_ref, delta_ref):
    ext = DH + ONES
    for h in range(heads):
        total = o_ref[h * ext + DH : h * ext + DH + 1, :]
        gt = g_ref[:, h * DH : (h + 1) * DH].T.astype(jnp.float32)
        part = jnp.sum(gt * o_ref[h * ext : h * ext + DH, :], axis=0, keepdims=True)
        log_ref[h : h + 1, :] = m_ref[h : h + 1, :] + jnp.log2(total)
        delta_ref[h : h + 1, :] = part / total


def finish(g, m, o):
    heads, chunk = m.shape
    shape = jax.ShapeDtypeStruct((heads, chunk), jnp.float32)
    return pl.pallas_call(
        functools.partial(finish_kernel, heads),
        out_shape=(shape, shape),
        in_specs=[whole()] * 3,
        out_specs=(whole(),) * 2,
        compiler_params=params(),
        cost_estimate=cost(2 * chunk * heads * DH, 6 * chunk * heads * DH),
        name="row_delta",
    )(g, m, o)


def grads_kernel(docs, layers, tile, heads, d, first, team, count, scal, q_ref, g_ref, *refs):
    kv_refs, refs = refs[:count], refs[count:]
    log_ref, delta_ref, refs = refs[0], refs[1], refs[2:]
    if not first:
        dq_in, refs = refs[0], refs[1:]
    if team is None:
        dq_ref, *dkv_refs, kv_ref, kt_ref, acc_ref = refs
    else:
        *outs, dkv_ref, kv_ref, kt_ref, acc_ref, dq_ref, full_ref = refs
        dkv_refs = [dkv_ref]
    chunk = q_ref.shape[0]
    scaling = 1.0 / math.sqrt(DH)
    factor = LOG2E * scaling
    if first:
        dq_ref[...] = jnp.zeros_like(dq_ref)
    else:
        dq_ref[...] = dq_in[...]

    def body(qo, ko, tk, mask):
        rows = pl.ds(qo, tile)
        keys = pl.ds(ko, tk)
        k = kv_ref[keys, :DH]
        v = kv_ref[keys, DH:]
        qs = [q_ref[rows, h * DH : (h + 1) * DH] for h in range(heads)]
        gs = [g_ref[rows, h * DH : (h + 1) * DH] for h in range(heads)]
        scores = [dot(k, q, NT) for q in qs]
        dots = [dot(v, g, NT) for g in gs]
        scores = [jnp.where(mask, s, NEG) for s in scores]
        probs = [
            jnp.exp2(scores[h] * factor - log_ref[h : h + 1, rows]) for h in range(heads)
        ]
        ds = [
            (probs[h] * (dots[h] - delta_ref[h : h + 1, rows])).astype(jnp.bfloat16)
            for h in range(heads)
        ]
        probs = [p.astype(jnp.bfloat16) for p in probs]
        dv = dot(jnp.concatenate(probs, 1), jnp.concatenate(gs, 0), NN)
        dk = dot(jnp.concatenate(ds, 1), jnp.concatenate(qs, 0), NN)
        kt = kt_ref[:, keys]
        news = [dot(kt, x, NN) for x in ds]
        for h in range(heads):
            dq_ref[h * DH : (h + 1) * DH, rows] += news[h]
        acc_ref[keys, :DH] += dk
        acc_ref[keys, DH:] += dv

    def use(i, dist):
        acc_ref[...] = jnp.zeros_like(acc_ref)
        kt_ref[...] = kv_ref[:, :DH].T
        over_tiles(scal, docs, dist, chunk, tile, body)
        for j, ref in enumerate(dkv_refs):

            @pl.when(i == j)
            def _():
                ref[:, :DH] = (acc_ref[:, :DH] * scaling).astype(ref.dtype)
                ref[:, DH:] = acc_ref[:, DH:].astype(ref.dtype)

    each_chunk(far_scalar(scal, docs, chunk, layers), kv_refs, kv_ref, d, True, use)
    if team is not None:
        for h in range(heads):
            full_ref[:, h * DH : (h + 1) * DH] = (
                (dq_ref[h * DH : (h + 1) * DH, :] * scaling).T.astype(jnp.bfloat16)
            )
        size = chunk // team
        for m in range(team):
            outs[m][...] = full_ref[span(scal[2] ^ m, size), :]


def grads(
    scal, docs, layers, tile, d, q, g, kvs, log_total, delta, dq, team=None, dtype=jnp.bfloat16
):
    chunk, width = q.shape
    heads = width // DH
    first = dq is None
    extra = () if first else (dq,)
    dkv_shapes = (jax.ShapeDtypeStruct((chunk, 2 * DH), dtype),) * len(kvs)
    scratch = [
        pltpu.VMEM((chunk, 2 * DH), jnp.bfloat16),
        pltpu.VMEM((DH, chunk), jnp.bfloat16),
        pltpu.VMEM((chunk, 2 * DH), jnp.float32),
    ]
    if team is None:
        shapes = (jax.ShapeDtypeStruct((width, chunk), jnp.float32),)
    else:
        shapes = (jax.ShapeDtypeStruct((chunk // team, width), jnp.bfloat16),) * team
        scratch += [
            pltpu.VMEM((width, chunk), jnp.float32),
            pltpu.VMEM((chunk, width), jnp.bfloat16),
        ]
    return ordered_call(
        functools.partial(grads_kernel, docs, layers, tile, heads, d, first, team, len(kvs)),
        scal,
        (q, g, *kvs, log_total, delta, *extra),
        (),
        out_shape=shapes + dkv_shapes,
        out_specs=(whole(),) * (len(shapes) + len(kvs)),
        scratch_shapes=scratch,
        cost_estimate=cost(10 * chunk * chunk * width, 12 * chunk * width, chunk * chunk * heads),
        name="pair_grads",
    )


def project(scal, d, w, parts, far, blocks, begin, count, after=()):
    rows, depth = d.shape
    wide = w.shape[0] // blocks
    split = w.shape[1] // depth
    each = 0 if not parts else parts[0].shape[1] // wide

    def kernel(*refs):
        scal, d_ref, w_ref = refs[:3]
        total = dot(d_ref[...], w_ref[...], NT)
        if not parts:
            refs[-1][...] = total
            return
        outs = refs[3 + len(parts) + len(after) :]
        for m in range(count):

            @pl.when(pl.program_id(0) == m)
            def _():
                outs[m][...] = (total + refs[3 + m // each][...]).astype(outs[m].dtype)

    def column(s):
        if split == 1:
            return 0
        return 1 - s[3] if far else s[3]

    def part_spec(p):
        return pl.BlockSpec((rows, wide), lambda i, s: (0, jnp.clip(i - p * each, 0, each - 1)))

    w_spec = pl.BlockSpec((wide, depth), lambda i, s: (s[2] ^ (i + begin), column(s)))
    if parts:
        out_shape = (jax.ShapeDtypeStruct((rows, wide), jnp.bfloat16),) * count
        out_specs = (pl.BlockSpec((rows, wide), lambda i, s: (0, 0)),) * count
    else:
        out_shape = jax.ShapeDtypeStruct((rows, wide * count), jnp.float32)
        out_specs = pl.BlockSpec((rows, wide), lambda i, s: (0, i))
    grid_spec = pltpu.PrefetchScalarGridSpec(
        num_scalar_prefetch=1,
        grid=(count,),
        in_specs=[pl.BlockSpec((rows, depth), lambda i, s: (0, 0)), w_spec]
        + [part_spec(p) for p in range(len(parts))]
        + [whole(pl.ANY)] * len(after),
        out_specs=out_specs,
    )
    return pl.pallas_call(
        kernel,
        out_shape=out_shape,
        grid_spec=grid_spec,
        compiler_params=params(PROJECT_LIMIT),
        cost_estimate=cost(2 * rows * depth * wide * count, 2 * depth * wide * count),
        name="project",
    )(scal, d, w, *parts, *after)


def copies(scal, inputs, out_shapes, plan, name, after=()):
    n_in = len(inputs)

    def kernel(scal, *refs):
        ins, outs, sems = refs[:n_in], refs[n_in:-1], refs[-1]
        started = []
        for i, (a, src, b, dst) in enumerate(plan(scal[2])):
            copy = pltpu.make_async_copy(ins[a].at[src], outs[b].at[dst], sems.at[i])
            copy.start()
            started.append(copy)
        for copy in started:
            copy.wait()

    count = len(plan(0))
    size = sum(math.prod(s.shape) * 2 for s in out_shapes)
    return ordered_call(
        kernel,
        scal,
        inputs,
        after,
        out_shape=tuple(out_shapes),
        in_specs=[whole(pl.ANY)] * n_in,
        out_specs=(whole(pl.ANY),) * len(out_shapes),
        scratch_shapes=[pltpu.SemaphoreType.DMA((count,))],
        cost_estimate=cost(0, 2 * size),
        name=name,
    )


def add(scal, a, b, after):
    def kernel(scal, a_ref, b_ref, out_ref):
        total = a_ref[...].astype(jnp.float32) + b_ref[...].astype(jnp.float32)
        out_ref[...] = total.astype(out_ref.dtype)

    return ordered_call(
        kernel,
        scal,
        (a, b),
        after,
        out_shape=jax.ShapeDtypeStruct(a.shape, a.dtype),
        out_specs=whole(),
        cost_estimate=cost(a.size, 6 * a.size),
        name="add_terms",
    )


def span(start, size):
    if isinstance(start, int):
        return pl.ds(start, size)
    return pl.ds(pl.multiple_of(start * size, size), size)


ALL = slice(None)


def solution(mesh):
    n_seq = mesh.shape["seq"]
    n_head = mesh.shape["head"]

    def shards(queries, keys, values, d_out, w_out, doc_starts):
        rows = queries.shape[0]
        groups = keys.shape[1] // DH
        heads = queries.shape[1] // keys.shape[1]
        width = heads * DH
        docs = doc_starts.shape[0]
        team = groups
        layers = n_seq // team
        chunk = team * rows
        tile = 256 if chunk % 256 == 0 else rows
        me = lax.axis_index("seq")
        layer = me // team
        head = lax.axis_index("head")
        base = layer * chunk
        scal = jnp.concatenate([jnp.stack([base, base, me % team, head]), doc_starts])
        ends = jnp.concatenate([doc_starts[1:], jnp.full((1,), chunk * layers, jnp.int32)])
        far = jnp.any((ends - 1) // chunk - doc_starts // chunk > 2)

        def half(*shape):
            return jax.ShapeDtypeStruct(shape, jnp.bfloat16)

        def swap(m, x):
            return lax.ppermute(x, "seq", [(i, i ^ m) for i in range(n_seq)])

        def swapped(parts):
            got = list(parts)
            for m in reversed(range(1, team)):
                got[m] = swap(m, parts[m])
            return got

        def shift(d, x):
            pairs = [(i, i + d * team) for i in range(n_seq) if 0 <= i + d * team < n_seq]
            return lax.ppermute(x, "seq", pairs)

        def pack(groups_of):
            arrays = [x for group in groups_of for x, _ in group]

            def kernel(scal, *refs):
                ins, outs = list(refs[: len(arrays)]), list(refs[len(arrays) :])
                for group in groups_of:
                    own, ins = ins[: len(group)], ins[len(group) :]
                    for m in range(team):
                        at = 0
                        out = outs.pop(0)
                        for ref, (_, size) in zip(own, group):
                            out[:, at : at + size] = ref[:, span(scal[2] ^ m, size)]
                            at += size

            shapes = [half(rows, sum(n for _, n in group)) for group in groups_of for _ in range(team)]
            outs = ordered_call(
                kernel,
                scal,
                arrays,
                (),
                out_shape=shapes,
                out_specs=[whole()] * len(shapes),
                name="pack_columns",
            )
            return [outs[i : i + team] for i in range(0, len(outs), team)]

        def stack(parts, sizes, name, after=(), also=()):
            def plan(place):
                out = []
                for m in range(team):
                    at = 0
                    for b, size in enumerate(sizes):
                        out.append((m, (ALL, pl.ds(at, size)), b, (span(place ^ m, rows), ALL)))
                        at += size
                for i in range(len(also)):
                    out.append((team + i, (ALL, ALL), len(sizes) + i, (ALL, ALL)))
                return out

            shapes = [half(chunk, size) for size in sizes] + [half(*x.shape) for x in also]
            return copies(scal, list(parts) + list(also), shapes, plan, name, after)

        def beside(parts, sizes, name):
            def plan(place):
                out = []
                for m in range(team):
                    at = 0
                    for b, size in enumerate(sizes):
                        out.append((m, (ALL, pl.ds(at, size)), b, (ALL, span(place ^ m, size))))
                        at += size
                return out

            shapes = [half(rows, team * size) for size in sizes]
            return copies(scal, parts, shapes, plan, name)

        if n_head == 2:
            d_far = lax.ppermute(d_out, "head", [(0, 1), (1, 0)])
        if team > 1:
            kv_sent, q_sent = pack([[(keys, DH), (values, DH)], [(queries, width)]])
            kv_got = swapped(kv_sent)
            q_got = swapped(q_sent)
            near = []
            if n_head == 2:
                near.append(project(scal, d_out, w_out, (), False, team, 0, team, kv_sent[:1]))
            (kv,) = stack(kv_got, [2 * DH], "stack_keys_values", near + list(q_sent[:1]))
            order = (kv,)
        else:
            kv = jnp.concatenate([keys, values], axis=1)
            near = [project(scal, d_out, w_out, (), False, 1, 0, 1)] if n_head == 2 else []
            q = queries
            order = ()
        if n_head == 2:
            g_parts = project(scal, d_far, w_out, near, True, team, 0, team, order)
        else:
            d_all = lax.all_gather(d_out, "head", axis=1, tiled=True)
            zero = jnp.zeros((rows, width * team), jnp.float32)
            g_parts = project(scal, d_all, w_out, [zero], False, team, 0, team, order)
        if team > 1:
            g_got = swapped(g_parts)
            (q,) = stack(q_got, [width], "stack_queries", g_parts[:1])
        state = stats(scal, docs, layers, tile, 0, q, [kv], None, g_parts[:1])

        def stack_g(after, also=()):
            if team > 1:
                return stack(g_got, [width], "stack_attn_grad", after, also)
            return (g_parts[0], *also)

        if layers <= 4:
            steps = [[kv]] + [[shift(d, kv)] for d in range(1, min(layers, 3))]
            g = None
            for d in range(1, len(steps)):
                state = stats(
                    scal, docs, layers, tile, d, q, steps[d], state, g_parts[:1] if g is None else (g,)
                )
                if g is None:
                    g, kv_again = stack_g(state[:1], (kv,))
                    if layers == 4:
                        third = lax.cond(far, lambda x: shift(3, x), lambda x: x, kv_again)
                        steps[2].append(third)
            if g is None:
                (g,) = stack_g(state[:1])
            log_total, delta = finish(g, *state)
            dq = None
            late = None
            sums = []
            for d in reversed(range(1, len(steps))):
                dq, dkv, *more = grads(
                    scal, docs, layers, tile, d, q, g, steps[d], log_total, delta, dq
                )
                if more:
                    late = lax.cond(far, lambda x: shift(-3, x), lambda x: x, more[0])
                sums.append(dkv)
            *dq_parts, dkv = grads(
                scal, docs, layers, tile, 0, q, g, [kv], log_total, delta, dq, team, jnp.float32
            )
            carried = None
            for x in sums:
                carried = shift(-1, x if carried is None else add(scal, x, carried, (dkv,)))
            terms = [] if carried is None else [carried]
            if late is not None:
                terms.append(late)
        else:
            rings = [[z * team + a for z in range(layers)] for a in range(team)]
            every = lax.all_gather(kv, "seq", axis_index_groups=rings)

            def chunk_at(d):
                return lax.dynamic_index_in_dim(every, jnp.maximum(layer - d, 0), 0, keepdims=False)

            def scalars(d):
                return scal - jnp.where(jnp.arange(scal.shape[0]) == 1, d * chunk, 0)

            def one(d, state):
                return tuple(stats(scalars(d), docs, layers, tile, 0, q, [chunk_at(d)], state))

            state = lax.fori_loop(1, layers, one, tuple(state))
            (g,) = stack_g(())
            log_total, delta = finish(g, *state)

            def two(d, carry):
                dq, total = carry
                dq, dkv = grads(
                    scalars(d), docs, layers, tile, 0, q, g, [chunk_at(d)], log_total, delta, dq
                )
                place = jnp.maximum(layer - d, 0)
                old = lax.dynamic_index_in_dim(total, place, 0, keepdims=False)
                total = lax.dynamic_update_index_in_dim(
                    total, jnp.where(layer >= d, dkv, old), place, 0
                )
                return dq, total

            dq = jnp.zeros((width, chunk), jnp.float32)
            total = jnp.zeros((layers, chunk, 2 * DH), jnp.bfloat16)
            dq, total = lax.fori_loop(1, layers, two, (dq, total))
            *dq_parts, dkv = grads(
                scal, docs, layers, tile, 0, q, g, [kv], log_total, delta, dq, team, jnp.float32
            )
            terms = [
                lax.psum_scatter(
                    total.reshape(layers * chunk, 2 * DH), "seq", axis_index_groups=rings, tiled=True
                )
            ]

        def sum_kernel(scal, *refs):
            total = refs[0][...]
            many = far_scalar(scal, docs, chunk, layers) > 0
            for i, x in enumerate(refs[1 : 1 + len(terms)]):
                term = x[...].astype(jnp.float32)
                total = total + (term if i == 0 else jnp.where(many, term, 0.0))
            full = refs[-1]
            full[...] = total.astype(jnp.bfloat16)
            for m in range(team):
                refs[1 + len(terms) + m][...] = full[span(scal[2] ^ m, rows), :]

        dkv_parts = pl.pallas_call(
            sum_kernel,
            out_shape=(half(rows, 2 * DH),) * team,
            in_specs=[whole(pltpu.SMEM)] + [whole()] * (1 + len(terms)),
            out_specs=(whole(),) * team,
            scratch_shapes=[pltpu.VMEM((chunk, 2 * DH), jnp.bfloat16)],
            compiler_params=params(),
            name="sum_terms",
        )(scal, dkv, *terms)
        if team > 1:
            dq_parts = swapped(dq_parts)
            dkv_parts = swapped(dkv_parts)
            (query_grad,) = beside(dq_parts, [width], "place_query_grad")
            key_grad, value_grad = beside(dkv_parts, [DH, DH], "place_key_value_grad")
        else:
            query_grad = dq_parts[0]
            key_grad = dkv_parts[0][:, :DH]
            value_grad = dkv_parts[0][:, DH:]
        return (query_grad, key_grad, value_grad)

    return jax.shard_map(
        shards,
        mesh=mesh,
        in_specs=(
            P("seq", "head"),
            P("seq", "head"),
            P("seq", "head"),
            P("seq", "head"),
            P("head", None),
            P(),
        ),
        out_specs=(P("seq", "head"), P("seq", "head"), P("seq", "head")),
        check_vma=False,
    )
```

```python
import functools
import math

import jax
import jax.numpy as jnp
from jax import lax
from jax.experimental import pallas as pl
from jax.experimental.pallas import tpu as pltpu
from jax.sharding import PartitionSpec as P

DH = 128
ONES = 16
LOG2E = 1.4426950408889634
NEG = -1e30
VMEM_LIMIT = 28 * 1024 * 1024
PROJECT_LIMIT = 52 * 1024 * 1024

NT = (((1,), (1,)), ((), ()))
NN = (((1,), (0,)), ((), ()))


def dot(a, b, dims):
    return lax.dot_general(a, b, dims, preferred_element_type=jnp.float32)


def params(limit=VMEM_LIMIT):
    return pltpu.CompilerParams(vmem_limit_bytes=limit)


def whole(memory_space=pltpu.VMEM):
    return pl.BlockSpec(memory_space=memory_space)


def ordered_call(kernel, scal, operands, after, **kwargs):
    count = len(after)

    def body(*refs):
        kernel(*refs[: 1 + len(operands)], *refs[1 + len(operands) + count :])

    specs = kwargs.pop("in_specs", [whole()] * len(operands))
    return pl.pallas_call(
        body,
        in_specs=[whole(pltpu.SMEM)] + specs + [whole(pl.ANY)] * count,
        compiler_params=params(),
        **kwargs,
    )(scal, *operands, *after)


def cost(flops, nbytes, exps=0):
    return pl.CostEstimate(flops=1024, bytes_accessed=1024, transcendentals=0)


FIRST_DOC = 4


def row_starts(scal, docs, pos):
    low = jnp.zeros_like(pos)
    for n in range(docs):
        low = jnp.where(pos >= scal[FIRST_DOC + n], scal[FIRST_DOC + n], low)
    return low


def reaches_far(starts, docs, chunk, total):
    far = jnp.int32(0)
    for n in range(docs):
        end = (starts[n + 1] if n + 1 < docs else total) - 1
        far = jnp.where(end // chunk - starts[n] // chunk > 2, 1, far)
    return far


def doc_start_at(scal, docs, pos):
    low = jnp.int32(0)
    for n in range(docs):
        low = jnp.where(pos >= scal[FIRST_DOC + n], scal[FIRST_DOC + n], low)
    return low


def allowed(scal, docs, q0, k0, tq, tk):
    qpos = q0 + lax.broadcasted_iota(jnp.int32, (1, tq), 1)
    kpos = k0 + lax.broadcasted_iota(jnp.int32, (tk, 1), 0)
    return (kpos <= qpos) & (kpos >= row_starts(scal, docs, qpos))


def over_tiles(scal, docs, d, chunk, tile, body):
    tiles = chunk // tile

    def one(qo, ko, q0, tk, need):
        k0 = scal[1] - d * chunk + ko
        @pl.when(need)
        def _():
            body(qo, ko, tk, allowed(scal, docs, q0, k0, tile, tk))

    def step(qt, _):
        qo = pl.multiple_of(qt * tile, tile)
        q0 = scal[0] + qo
        low = doc_start_at(scal, docs, q0)
        k0 = scal[1] - d * chunk
        if tiles == 1:
            one(qo, 0, q0, tile, (k0 <= q0 + tile - 1) & (k0 + tile - 1 >= low))
            return 0
        all_of = (k0 + chunk - tile <= q0 + tile - 1) & (k0 + tile - 1 >= low)
        one(qo, 0, q0, chunk, all_of)

        @pl.when(jnp.logical_not(all_of))
        def _():
            def inner(kt, _):
                ko = pl.multiple_of(kt * tile, tile)
                need = (k0 + ko <= q0 + tile - 1) & (k0 + ko + tile - 1 >= low)
                one(qo, ko, q0, tile, need)
                return 0

            lax.fori_loop(0, tiles, inner, 0)

        return 0

    lax.fori_loop(0, tiles, step, 0)


def each_chunk(total, kv_refs, now_ref, d, down, use):
    count = len(kv_refs)
    if count == 1:
        now_ref[...] = kv_refs[0][...]
        use(0, d)
        return

    def one(i, _):
        for j, ref in enumerate(kv_refs):

            @pl.when(i == j)
            def _():
                now_ref[...] = ref[...]

        use(i, d + i)
        return 0

    if down:
        lax.fori_loop(0, total, lambda i, c: one(total - 1 - i, c), 0)
    else:
        lax.fori_loop(0, total, one, 0)


def chunk_count(scal, docs, chunk, layers, d, count):
    always = min(count, max(1, 3 - d))
    if always == count:
        return count
    far = reaches_far([scal[FIRST_DOC + n] for n in range(docs)], docs, chunk, chunk * layers)
    return always + (count - always) * far


def stats_kernel(docs, layers, tile, heads, d, first, count, scal, q_ref, *refs):
    kv_refs, refs = refs[:count], refs[count:]
    if first:
        m_ref, o_ref, kv_ref, vt_ref = refs
        m_ref[...] = jnp.full_like(m_ref, NEG)
        o_ref[...] = jnp.zeros_like(o_ref)
    else:
        m_in, o_in, m_ref, o_ref, kv_ref, vt_ref = refs
        m_ref[...] = m_in[...]
        o_ref[...] = o_in[...]
    chunk = q_ref.shape[0]
    factor = LOG2E / math.sqrt(DH)
    ext = DH + ONES
    vt_ref[DH:] = jnp.ones((vt_ref.shape[0] - DH, chunk), jnp.bfloat16)

    def body(qo, ko, tk, mask):
        k = kv_ref[pl.ds(ko, tk), :DH]
        vt = vt_ref[:ext, pl.ds(ko, tk)]
        rows = pl.ds(qo, tile)
        scores = [dot(k, q_ref[rows, h * DH : (h + 1) * DH], NT) for h in range(heads)]
        scores = [jnp.where(mask, s, NEG) for s in scores]
        m_old = [m_ref[h : h + 1, rows] for h in range(heads)]
        m_new = [
            jnp.maximum(m, factor * jnp.max(s, axis=0, keepdims=True))
            for m, s in zip(m_old, scores)
        ]
        alpha = [jnp.exp2(a - b) for a, b in zip(m_old, m_new)]
        probs = [jnp.exp2(s * factor - m).astype(jnp.bfloat16) for s, m in zip(scores, m_new)]
        news = [dot(vt, p, NN) for p in probs]
        for h in range(heads):
            part = slice(h * ext, (h + 1) * ext)
            m_ref[h : h + 1, rows] = m_new[h]
            o_ref[part, rows] = alpha[h] * o_ref[part, rows] + news[h]

    def use(i, dist):
        vt_ref[:DH] = kv_ref[:, DH:].T
        over_tiles(scal, docs, dist, chunk, tile, body)

    each_chunk(chunk_count(scal, docs, chunk, layers, d, count), kv_refs, kv_ref, d, False, use)


def stats(scal, docs, layers, tile, d, q, kvs, state, after=()):
    chunk, width = q.shape
    heads = width // DH
    shapes = (
        jax.ShapeDtypeStruct((heads, chunk), jnp.float32),
        jax.ShapeDtypeStruct((heads * (DH + ONES), chunk), jnp.float32),
    )
    first = state is None
    extra = () if first else state
    return ordered_call(
        functools.partial(stats_kernel, docs, layers, tile, heads, d, first, len(kvs)),
        scal,
        (q, *kvs, *extra),
        after,
        out_shape=shapes,
        out_specs=(whole(),) * 2,
        scratch_shapes=[
            pltpu.VMEM((chunk, 2 * DH), jnp.bfloat16),
            pltpu.VMEM((DH + ONES, chunk), jnp.bfloat16),
        ],
        cost_estimate=cost(4 * chunk * chunk * width, 12 * chunk * width, chunk * chunk * heads),
        name="row_stats",
    )


def finish_kernel(heads, g_ref, m_ref, o_ref, log_ref, delta_ref):
    ext = DH + ONES
    for h in range(heads):
        total = o_ref[h * ext + DH : h * ext + DH + 1, :]
        gt = g_ref[:, h * DH : (h + 1) * DH].T.astype(jnp.float32)
        part = jnp.sum(gt * o_ref[h * ext : h * ext + DH, :], axis=0, keepdims=True)
        log_ref[h : h + 1, :] = m_ref[h : h + 1, :] + jnp.log2(total)
        delta_ref[h : h + 1, :] = part / total


def finish(g, m, o):
    heads, chunk = m.shape
    shape = jax.ShapeDtypeStruct((heads, chunk), jnp.float32)
    return pl.pallas_call(
        functools.partial(finish_kernel, heads),
        out_shape=(shape, shape),
        in_specs=[whole()] * 3,
        out_specs=(whole(),) * 2,
        compiler_params=params(),
        cost_estimate=cost(2 * chunk * heads * DH, 6 * chunk * heads * DH),
        name="row_delta",
    )(g, m, o)


def grads_kernel(docs, layers, tile, heads, d, first, team, count, scal, q_ref, g_ref, *refs):
    kv_refs, refs = refs[:count], refs[count:]
    log_ref, delta_ref, refs = refs[0], refs[1], refs[2:]
    if not first:
        dq_in, refs = refs[0], refs[1:]
    if team is None:
        dq_ref, *dkv_refs, kv_ref, kt_ref, acc_ref = refs
    else:
        outs, refs = refs[:team], refs[team:]
        *dkv_refs, kv_ref, kt_ref, acc_ref, dq_ref, full_ref = refs
    chunk = q_ref.shape[0]
    scaling = 1.0 / math.sqrt(DH)
    factor = LOG2E * scaling
    if first:
        dq_ref[...] = jnp.zeros_like(dq_ref)
    else:
        dq_ref[...] = dq_in[...]

    def body(qo, ko, tk, mask):
        rows = pl.ds(qo, tile)
        keys = pl.ds(ko, tk)
        k = kv_ref[keys, :DH]
        v = kv_ref[keys, DH:]
        qs = [q_ref[rows, h * DH : (h + 1) * DH] for h in range(heads)]
        gs = [g_ref[rows, h * DH : (h + 1) * DH] for h in range(heads)]
        scores = [dot(k, q, NT) for q in qs]
        dots = [dot(v, g, NT) for g in gs]
        scores = [jnp.where(mask, s, NEG) for s in scores]
        probs = [
            jnp.exp2(scores[h] * factor - log_ref[h : h + 1, rows]) for h in range(heads)
        ]
        ds = [
            (probs[h] * (dots[h] - delta_ref[h : h + 1, rows])).astype(jnp.bfloat16)
            for h in range(heads)
        ]
        probs = [p.astype(jnp.bfloat16) for p in probs]
        dv = dot(jnp.concatenate(probs, 1), jnp.concatenate(gs, 0), NN)
        dk = dot(jnp.concatenate(ds, 1), jnp.concatenate(qs, 0), NN)
        kt = kt_ref[:, keys]
        news = [dot(kt, x, NN) for x in ds]
        for h in range(heads):
            dq_ref[h * DH : (h + 1) * DH, rows] += news[h]
        acc_ref[keys, :DH] += dk
        acc_ref[keys, DH:] += dv

    def use(i, dist):
        acc_ref[...] = jnp.zeros_like(acc_ref)
        kt_ref[...] = kv_ref[:, :DH].T
        over_tiles(scal, docs, dist, chunk, tile, body)
        for j, ref in enumerate(dkv_refs):

            @pl.when(i == j)
            def _():
                ref[:, :DH] = (acc_ref[:, :DH] * scaling).astype(ref.dtype)
                ref[:, DH:] = acc_ref[:, DH:].astype(ref.dtype)

    each_chunk(chunk_count(scal, docs, chunk, layers, d, count), kv_refs, kv_ref, d, True, use)
    if team is not None:
        for h in range(heads):
            full_ref[:, h * DH : (h + 1) * DH] = (
                (dq_ref[h * DH : (h + 1) * DH, :] * scaling).T.astype(jnp.bfloat16)
            )
        size = chunk // team
        for m in range(team):
            outs[m][...] = full_ref[span(scal[2] ^ m, size), :]


def grads(
    scal, docs, layers, tile, d, q, g, kvs, log_total, delta, dq, team=None, dtypes=()
):
    chunk, width = q.shape
    heads = width // DH
    first = dq is None
    extra = () if first else (dq,)
    dtypes = dtypes or (jnp.bfloat16,) * len(kvs)
    dkv_shapes = tuple(jax.ShapeDtypeStruct((chunk, 2 * DH), dtype) for dtype in dtypes)
    scratch = [
        pltpu.VMEM((chunk, 2 * DH), jnp.bfloat16),
        pltpu.VMEM((DH, chunk), jnp.bfloat16),
        pltpu.VMEM((chunk, 2 * DH), jnp.float32),
    ]
    if team is None:
        shapes = (jax.ShapeDtypeStruct((width, chunk), jnp.float32),)
    else:
        shapes = (jax.ShapeDtypeStruct((chunk // team, width), jnp.bfloat16),) * team
        scratch += [
            pltpu.VMEM((width, chunk), jnp.float32),
            pltpu.VMEM((chunk, width), jnp.bfloat16),
        ]
    return ordered_call(
        functools.partial(grads_kernel, docs, layers, tile, heads, d, first, team, len(kvs)),
        scal,
        (q, g, *kvs, log_total, delta, *extra),
        (),
        out_shape=shapes + dkv_shapes,
        out_specs=(whole(),) * (len(shapes) + len(kvs)),
        scratch_shapes=scratch,
        cost_estimate=cost(10 * chunk * chunk * width, 12 * chunk * width, chunk * chunk * heads),
        name="pair_grads",
    )


def project(scal, d, w, parts, far, blocks, begin, count, after=()):
    rows, depth = d.shape
    wide = w.shape[0] // blocks
    split = w.shape[1] // depth
    each = 0 if not parts else parts[0].shape[1] // wide

    def kernel(*refs):
        scal, d_ref, w_ref = refs[:3]
        total = dot(d_ref[...], w_ref[...], NT)
        if not parts:
            refs[-2][...] = total
            refs[-1][...] = jnp.zeros_like(refs[-1])
            return
        outs = refs[3 + len(parts) + len(after) :]
        for m in range(count):

            @pl.when(pl.program_id(0) == m)
            def _():
                outs[m][...] = (total + refs[3 + m // each][...]).astype(outs[m].dtype)

    def column(s):
        if split == 1:
            return 0
        return 1 - s[3] if far else s[3]

    def part_spec(p):
        return pl.BlockSpec((rows, wide), lambda i, s: (0, jnp.clip(i - p * each, 0, each - 1)))

    w_spec = pl.BlockSpec((wide, depth), lambda i, s: (s[2] ^ (i + begin), column(s)))
    if parts:
        out_shape = (jax.ShapeDtypeStruct((rows, wide), jnp.bfloat16),) * count
        out_specs = (pl.BlockSpec((rows, wide), lambda i, s: (0, 0)),) * count
    else:
        out_shape = (
            jax.ShapeDtypeStruct((rows, wide * count), jnp.float32),
            jax.ShapeDtypeStruct((8, 128), jnp.float32),
        )
        out_specs = (
            pl.BlockSpec((rows, wide), lambda i, s: (0, i)),
            pl.BlockSpec((8, 128), lambda i, s: (0, 0)),
        )
    grid_spec = pltpu.PrefetchScalarGridSpec(
        num_scalar_prefetch=1,
        grid=(count,),
        in_specs=[pl.BlockSpec((rows, depth), lambda i, s: (0, 0)), w_spec]
        + [part_spec(p) for p in range(len(parts))]
        + [whole(pl.ANY)] * len(after),
        out_specs=out_specs,
    )
    return pl.pallas_call(
        kernel,
        out_shape=out_shape,
        grid_spec=grid_spec,
        compiler_params=params(PROJECT_LIMIT),
        cost_estimate=cost(2 * rows * depth * wide * count, 2 * depth * wide * count),
        name="project",
    )(scal, d, w, *parts, *after)


def copies(scal, inputs, out_shapes, plan, name, after=()):
    n_in = len(inputs)

    def kernel(scal, *refs):
        ins, outs, sems = refs[:n_in], refs[n_in:-1], refs[-1]
        started = []
        for i, (a, src, b, dst) in enumerate(plan(scal[2])):
            copy = pltpu.make_async_copy(ins[a].at[src], outs[b].at[dst], sems.at[i])
            copy.start()
            started.append(copy)
        for copy in started:
            copy.wait()

    count = len(plan(0))
    size = sum(math.prod(s.shape) * 2 for s in out_shapes)
    return ordered_call(
        kernel,
        scal,
        inputs,
        after,
        out_shape=tuple(out_shapes),
        in_specs=[whole(pl.ANY)] * n_in,
        out_specs=(whole(pl.ANY),) * len(out_shapes),
        scratch_shapes=[pltpu.SemaphoreType.DMA((count,))],
        cost_estimate=cost(0, 2 * size),
        name=name,
    )


def add(scal, a, b, after):
    def kernel(scal, a_ref, b_ref, out_ref):
        total = a_ref[...].astype(jnp.float32) + b_ref[...].astype(jnp.float32)
        out_ref[...] = total.astype(out_ref.dtype)

    return ordered_call(
        kernel,
        scal,
        (a, b),
        after,
        out_shape=jax.ShapeDtypeStruct(a.shape, a.dtype),
        out_specs=whole(),
        cost_estimate=cost(a.size, 6 * a.size),
        name="add_terms",
    )


def span(start, size):
    if isinstance(start, int):
        return pl.ds(start, size)
    return pl.ds(pl.multiple_of(start * size, size), size)


ALL = slice(None)


def solution(mesh):
    n_seq = mesh.shape["seq"]
    n_head = mesh.shape["head"]

    def shards(queries, keys, values, d_out, w_out, doc_starts):
        rows = queries.shape[0]
        groups = keys.shape[1] // DH
        heads = queries.shape[1] // keys.shape[1]
        width = heads * DH
        docs = doc_starts.shape[0]
        team = groups
        layers = n_seq // team
        chunk = team * rows
        tile = 256 if chunk % 256 == 0 else rows
        me = lax.axis_index("seq")
        layer = me // team
        head = lax.axis_index("head")
        base = layer * chunk
        scal = jnp.concatenate([jnp.stack([base, base, me % team, head]), doc_starts])
        ends = jnp.concatenate([doc_starts[1:], jnp.full((1,), chunk * layers, jnp.int32)])
        far = jnp.any((ends - 1) // chunk - doc_starts // chunk > 2)

        def half(*shape):
            return jax.ShapeDtypeStruct(shape, jnp.bfloat16)

        def swap(m, x):
            return lax.ppermute(x, "seq", [(i, i ^ m) for i in range(n_seq)])

        def swapped(parts):
            got = list(parts)
            for m in reversed(range(1, team)):
                got[m] = swap(m, parts[m])
            return got

        def shift(d, x, first=0):
            pairs = [
                (i, i + d * team)
                for i in range(first * team, n_seq)
                if 0 <= i + d * team < n_seq
            ]
            return lax.ppermute(x, "seq", pairs)

        def pack(groups_of):
            arrays = [x for group in groups_of for x, _ in group]

            def kernel(scal, *refs):
                ins, outs = list(refs[: len(arrays)]), list(refs[len(arrays) :])
                for group in groups_of:
                    own, ins = ins[: len(group)], ins[len(group) :]
                    for m in range(team):
                        at = 0
                        out = outs.pop(0)
                        for ref, (_, size) in zip(own, group):
                            out[:, at : at + size] = ref[:, span(scal[2] ^ m, size)]
                            at += size

            shapes = [half(rows, sum(n for _, n in group)) for group in groups_of for _ in range(team)]
            outs = ordered_call(
                kernel,
                scal,
                arrays,
                (),
                out_shape=shapes,
                out_specs=[whole()] * len(shapes),
                name="pack_columns",
            )
            return [outs[i : i + team] for i in range(0, len(outs), team)]

        def stack(parts, sizes, name, after=()):
            def plan(place):
                out = []
                for m in range(team):
                    at = 0
                    for b, size in enumerate(sizes):
                        out.append((m, (ALL, pl.ds(at, size)), b, (span(place ^ m, rows), ALL)))
                        at += size
                return out

            return copies(scal, parts, [half(chunk, size) for size in sizes], plan, name, after)

        def beside(parts, sizes, name):
            def plan(place):
                out = []
                for m in range(team):
                    at = 0
                    for b, size in enumerate(sizes):
                        out.append((m, (ALL, pl.ds(at, size)), b, (ALL, span(place ^ m, size))))
                        at += size
                return out

            shapes = [half(rows, team * size) for size in sizes]
            return copies(scal, parts, shapes, plan, name)

        if n_head == 2:
            d_far = lax.ppermute(d_out, "head", [(0, 1), (1, 0)])
        if team > 1:
            kv_sent, q_sent = pack([[(keys, DH), (values, DH)], [(queries, width)]])
            kv_got = swapped(kv_sent)
            q_got = swapped(q_sent)
            near = []
            marks = []
            if n_head == 2:
                part, end = project(scal, d_out, w_out, (), False, team, 0, team, kv_sent[:1])
                near.append(part)
                marks.append(end)
            (kv,) = stack(kv_got, [2 * DH], "stack_keys_values", marks)
            order = (kv,)
        else:
            kv = jnp.concatenate([keys, values], axis=1)
            near = [project(scal, d_out, w_out, (), False, 1, 0, 1)[0]] if n_head == 2 else []
            q = queries
            order = ()
        if n_head == 2:
            g_parts = project(scal, d_far, w_out, near, True, team, 0, team, order)
        else:
            d_all = lax.all_gather(d_out, "head", axis=1, tiled=True)
            zero = jnp.zeros((rows, width * team), jnp.float32)
            g_parts = project(scal, d_all, w_out, [zero], False, team, 0, team, order)
        if team > 1:
            g_got = swapped(g_parts)
            (q,) = stack(q_got, [width], "stack_queries", g_parts[:1])
        def stack_g(after):
            if team > 1:
                return stack(g_got, [width], "stack_attn_grad", after)[0]
            return g_parts[0]

        if layers <= 4:
            steps = [kv] + [shift(d, kv) for d in range(1, min(layers, 3))]
            if layers == 4:
                steps.append(lax.cond(far, lambda x: shift(3, x), lambda x: x, kv))
            state = stats(scal, docs, layers, tile, 0, q, steps[:2], None, g_parts[:1])
            g = stack_g(state[:1])
            if layers > 2:
                state = stats(scal, docs, layers, tile, 2, q, steps[2:], state, (g,))
            log_total, delta = finish(g, *state)
            dq = None
            terms = []
            far_sum = None
            if layers > 2:
                dq, far_sum, *late = grads(
                    scal, docs, layers, tile, 2, q, g, steps[2:], log_total, delta, dq
                )
                far_sum = shift(-1, far_sum, 2)
                if late:
                    terms = [lax.cond(far, lambda x: shift(-3, x), lambda x: x, late[0])]
            dtypes = (jnp.float32, jnp.bfloat16)[: min(layers, 2)]
            *dq_parts, dkv, near_sum = grads(
                scal, docs, layers, tile, 0, q, g, steps[:2], log_total, delta, dq, team, dtypes
            )
            if far_sum is not None:
                near_sum = add(scal, near_sum, far_sum, ())
            terms = [shift(-1, near_sum, 1)] + terms
        else:
            rings = [[z * team + a for z in range(layers)] for a in range(team)]
            every = lax.all_gather(kv, "seq", axis_index_groups=rings)

            def chunk_at(d):
                return lax.dynamic_index_in_dim(every, jnp.maximum(layer - d, 0), 0, keepdims=False)

            def scalars(d):
                return scal - jnp.where(jnp.arange(scal.shape[0]) == 1, d * chunk, 0)

            def one(d, state):
                return tuple(stats(scalars(d), docs, layers, tile, 0, q, [chunk_at(d)], state))

            state = stats(scal, docs, layers, tile, 0, q, [kv], None)
            state = lax.fori_loop(1, layers, one, tuple(state))
            g = stack_g(())
            log_total, delta = finish(g, *state)

            def two(d, carry):
                dq, total = carry
                dq, dkv = grads(
                    scalars(d), docs, layers, tile, 0, q, g, [chunk_at(d)], log_total, delta, dq
                )
                place = jnp.maximum(layer - d, 0)
                old = lax.dynamic_index_in_dim(total, place, 0, keepdims=False)
                total = lax.dynamic_update_index_in_dim(
                    total, jnp.where(layer >= d, dkv, old), place, 0
                )
                return dq, total

            dq = jnp.zeros((width, chunk), jnp.float32)
            total = jnp.zeros((layers, chunk, 2 * DH), jnp.bfloat16)
            dq, total = lax.fori_loop(1, layers, two, (dq, total))
            *dq_parts, dkv = grads(
                scal, docs, layers, tile, 0, q, g, [kv], log_total, delta, dq, team, (jnp.float32,)
            )
            terms = [
                lax.psum_scatter(
                    total.reshape(layers * chunk, 2 * DH), "seq", axis_index_groups=rings, tiled=True
                )
            ]

        def sum_kernel(scal, *refs):
            total = refs[0][...]
            starts = [scal[FIRST_DOC + n] for n in range(docs)]
            many = reaches_far(starts, docs, chunk, chunk * layers) > 0
            for i, x in enumerate(refs[1 : 1 + len(terms)]):
                term = x[...].astype(jnp.float32)
                total = total + (term if i == 0 else jnp.where(many, term, 0.0))
            full = refs[-1]
            full[...] = total.astype(jnp.bfloat16)
            for m in range(team):
                refs[1 + len(terms) + m][...] = full[span(scal[2] ^ m, rows), :]

        dkv_parts = pl.pallas_call(
            sum_kernel,
            out_shape=(half(rows, 2 * DH),) * team,
            in_specs=[whole(pltpu.SMEM)] + [whole()] * (1 + len(terms)),
            out_specs=(whole(),) * team,
            scratch_shapes=[pltpu.VMEM((chunk, 2 * DH), jnp.bfloat16)],
            compiler_params=params(),
            name="sum_terms",
        )(scal, dkv, *terms)
        if team > 1:
            dq_parts = swapped(dq_parts)
            dkv_parts = swapped(dkv_parts)
            (query_grad,) = beside(dq_parts, [width], "place_query_grad")
            key_grad, value_grad = beside(dkv_parts, [DH, DH], "place_key_value_grad")
        else:
            query_grad = dq_parts[0]
            key_grad = dkv_parts[0][:, :DH]
            value_grad = dkv_parts[0][:, DH:]
        return (query_grad, key_grad, value_grad)

    return jax.shard_map(
        shards,
        mesh=mesh,
        in_specs=(
            P("seq", "head"),
            P("seq", "head"),
            P("seq", "head"),
            P("seq", "head"),
            P("head", None),
            P(),
        ),
        out_specs=(P("seq", "head"), P("seq", "head"), P("seq", "head")),
        check_vma=False,
    )
```

```python
import functools
import math

import jax
import jax.numpy as jnp
from jax import lax
from jax.experimental import pallas as pl
from jax.experimental.pallas import tpu as pltpu
from jax.sharding import PartitionSpec as P

DH = 128
ONES = 16
LOG2E = 1.4426950408889634
NEG = -1e30
VMEM_LIMIT = 28 * 1024 * 1024
PACK_LIMIT = 63 * 1024 * 1024
PROJECT_LIMIT = 52 * 1024 * 1024

NT = (((1,), (1,)), ((), ()))
NN = (((1,), (0,)), ((), ()))


def dot(a, b, dims):
    return lax.dot_general(a, b, dims, preferred_element_type=jnp.float32)


def params(limit=VMEM_LIMIT):
    return pltpu.CompilerParams(vmem_limit_bytes=limit)


def whole(memory_space=pltpu.VMEM):
    return pl.BlockSpec(memory_space=memory_space)


def ordered_call(kernel, scal, operands, after, **kwargs):
    count = len(after)

    def body(*refs):
        kernel(*refs[: 1 + len(operands)], *refs[1 + len(operands) + count :])

    specs = kwargs.pop("in_specs", [whole()] * len(operands))
    limit = kwargs.pop("limit", VMEM_LIMIT)
    return pl.pallas_call(
        body,
        in_specs=[whole(pltpu.SMEM)] + specs + [whole(pl.ANY)] * count,
        compiler_params=params(limit),
        **kwargs,
    )(scal, *operands, *after)


def cost(flops, nbytes, exps=0):
    return pl.CostEstimate(flops=1024, bytes_accessed=1024, transcendentals=0)


FIRST_DOC = 4


def row_starts(scal, docs, pos):
    low = jnp.zeros_like(pos)
    for n in range(docs):
        low = jnp.where(pos >= scal[FIRST_DOC + n], scal[FIRST_DOC + n], low)
    return low


def reaches_far(starts, docs, chunk, total):
    far = jnp.int32(0)
    for n in range(docs):
        end = (starts[n + 1] if n + 1 < docs else total) - 1
        far = jnp.where(end // chunk - starts[n] // chunk > 2, 1, far)
    return far


def doc_start_at(scal, docs, pos):
    low = jnp.int32(0)
    for n in range(docs):
        low = jnp.where(pos >= scal[FIRST_DOC + n], scal[FIRST_DOC + n], low)
    return low


def allowed(scal, docs, q0, k0, tq, tk):
    qpos = q0 + lax.broadcasted_iota(jnp.int32, (1, tq), 1)
    kpos = k0 + lax.broadcasted_iota(jnp.int32, (tk, 1), 0)
    return (kpos <= qpos) & (kpos >= row_starts(scal, docs, qpos))


def over_tiles(scal, docs, d, chunk, tile, body):
    tiles = chunk // tile

    def one(qo, ko, q0, tk, need):
        k0 = scal[1] - d * chunk + ko
        @pl.when(need)
        def _():
            body(qo, ko, tk, allowed(scal, docs, q0, k0, tile, tk))

    def step(qt, _):
        qo = pl.multiple_of(qt * tile, tile)
        q0 = scal[0] + qo
        low = doc_start_at(scal, docs, q0)
        k0 = scal[1] - d * chunk
        if tiles == 1:
            one(qo, 0, q0, tile, (k0 <= q0 + tile - 1) & (k0 + tile - 1 >= low))
            return 0
        all_of = (k0 + chunk - tile <= q0 + tile - 1) & (k0 + tile - 1 >= low)
        one(qo, 0, q0, chunk, all_of)

        @pl.when(jnp.logical_not(all_of))
        def _():
            def inner(kt, _):
                ko = pl.multiple_of(kt * tile, tile)
                need = (k0 + ko <= q0 + tile - 1) & (k0 + ko + tile - 1 >= low)
                one(qo, ko, q0, tile, need)
                return 0

            lax.fori_loop(0, tiles, inner, 0)

        return 0

    lax.fori_loop(0, tiles, step, 0)


def each_chunk(total, kv_refs, now_ref, d, down, use):
    count = len(kv_refs)
    if count == 1:
        now_ref[...] = kv_refs[0][...]
        use(0, d)
        return

    def one(i, _):
        for j, ref in enumerate(kv_refs):

            @pl.when(i == j)
            def _():
                now_ref[...] = ref[...]

        use(i, d + i)
        return 0

    if down:
        lax.fori_loop(0, total, lambda i, c: one(total - 1 - i, c), 0)
    else:
        lax.fori_loop(0, total, one, 0)


def chunk_count(scal, docs, chunk, layers, d, count):
    always = min(count, max(1, 3 - d))
    if always == count:
        return count
    far = reaches_far([scal[FIRST_DOC + n] for n in range(docs)], docs, chunk, chunk * layers)
    return always + (count - always) * far


def stats_kernel(docs, layers, tile, heads, d, first, count, scal, q_ref, *refs):
    kv_refs, refs = refs[:count], refs[count:]
    if first:
        m_ref, o_ref, kv_ref, vt_ref = refs
        m_ref[...] = jnp.full_like(m_ref, NEG)
        o_ref[...] = jnp.zeros_like(o_ref)
    else:
        m_in, o_in, m_ref, o_ref, kv_ref, vt_ref = refs
        m_ref[...] = m_in[...]
        o_ref[...] = o_in[...]
    chunk = q_ref.shape[0]
    factor = LOG2E / math.sqrt(DH)
    ext = DH + ONES
    vt_ref[DH:] = jnp.ones((vt_ref.shape[0] - DH, chunk), jnp.bfloat16)

    def body(qo, ko, tk, mask):
        k = kv_ref[pl.ds(ko, tk), :DH]
        vt = vt_ref[:ext, pl.ds(ko, tk)]
        rows = pl.ds(qo, tile)
        scores = [dot(k, q_ref[rows, h * DH : (h + 1) * DH], NT) for h in range(heads)]
        scores = [jnp.where(mask, s, NEG) for s in scores]
        m_old = [m_ref[h : h + 1, rows] for h in range(heads)]
        m_new = [
            jnp.maximum(m, factor * jnp.max(s, axis=0, keepdims=True))
            for m, s in zip(m_old, scores)
        ]
        alpha = [jnp.exp2(a - b) for a, b in zip(m_old, m_new)]
        probs = [jnp.exp2(s * factor - m).astype(jnp.bfloat16) for s, m in zip(scores, m_new)]
        news = [dot(vt, p, NN) for p in probs]
        for h in range(heads):
            part = slice(h * ext, (h + 1) * ext)
            m_ref[h : h + 1, rows] = m_new[h]
            o_ref[part, rows] = alpha[h] * o_ref[part, rows] + news[h]

    def use(i, dist):
        vt_ref[:DH] = kv_ref[:, DH:].T
        over_tiles(scal, docs, dist, chunk, tile, body)

    each_chunk(chunk_count(scal, docs, chunk, layers, d, count), kv_refs, kv_ref, d, False, use)


def stats(scal, docs, layers, tile, d, q, kvs, state, after=()):
    chunk, width = q.shape
    heads = width // DH
    shapes = (
        jax.ShapeDtypeStruct((heads, chunk), jnp.float32),
        jax.ShapeDtypeStruct((heads * (DH + ONES), chunk), jnp.float32),
    )
    first = state is None
    extra = () if first else state
    return ordered_call(
        functools.partial(stats_kernel, docs, layers, tile, heads, d, first, len(kvs)),
        scal,
        (q, *kvs, *extra),
        after,
        out_shape=shapes,
        out_specs=(whole(),) * 2,
        scratch_shapes=[
            pltpu.VMEM((chunk, 2 * DH), jnp.bfloat16),
            pltpu.VMEM((DH + ONES, chunk), jnp.bfloat16),
        ],
        cost_estimate=cost(4 * chunk * chunk * width, 12 * chunk * width, chunk * chunk * heads),
        name="row_stats",
    )


def finish_kernel(heads, g_ref, m_ref, o_ref, log_ref, delta_ref):
    ext = DH + ONES
    for h in range(heads):
        total = o_ref[h * ext + DH : h * ext + DH + 1, :]
        gt = g_ref[:, h * DH : (h + 1) * DH].T.astype(jnp.float32)
        part = jnp.sum(gt * o_ref[h * ext : h * ext + DH, :], axis=0, keepdims=True)
        log_ref[h : h + 1, :] = m_ref[h : h + 1, :] + jnp.log2(total)
        delta_ref[h : h + 1, :] = part / total


def finish(g, m, o):
    heads, chunk = m.shape
    shape = jax.ShapeDtypeStruct((heads, chunk), jnp.float32)
    return pl.pallas_call(
        functools.partial(finish_kernel, heads),
        out_shape=(shape, shape),
        in_specs=[whole()] * 3,
        out_specs=(whole(),) * 2,
        compiler_params=params(),
        cost_estimate=cost(2 * chunk * heads * DH, 6 * chunk * heads * DH),
        name="row_delta",
    )(g, m, o)


def grads_kernel(docs, layers, tile, heads, d, first, team, count, scal, q_ref, g_ref, *refs):
    kv_refs, refs = refs[:count], refs[count:]
    log_ref, delta_ref, refs = refs[0], refs[1], refs[2:]
    if not first:
        dq_in, refs = refs[0], refs[1:]
    if team is None:
        dq_ref, *dkv_refs, kv_ref, kt_ref, acc_ref = refs
    else:
        outs, refs = refs[:team], refs[team:]
        *dkv_refs, kv_ref, kt_ref, acc_ref, dq_ref, full_ref = refs
    chunk = q_ref.shape[0]
    scaling = 1.0 / math.sqrt(DH)
    factor = LOG2E * scaling
    if first:
        dq_ref[...] = jnp.zeros_like(dq_ref)
    else:
        dq_ref[...] = dq_in[...]

    def body(qo, ko, tk, mask):
        rows = pl.ds(qo, tile)
        keys = pl.ds(ko, tk)
        k = kv_ref[keys, :DH]
        v = kv_ref[keys, DH:]
        qs = [q_ref[rows, h * DH : (h + 1) * DH] for h in range(heads)]
        gs = [g_ref[rows, h * DH : (h + 1) * DH] for h in range(heads)]
        scores = [dot(k, q, NT) for q in qs]
        dots = [dot(v, g, NT) for g in gs]
        scores = [jnp.where(mask, s, NEG) for s in scores]
        probs = [
            jnp.exp2(scores[h] * factor - log_ref[h : h + 1, rows]) for h in range(heads)
        ]
        ds = [
            (probs[h] * (dots[h] - delta_ref[h : h + 1, rows])).astype(jnp.bfloat16)
            for h in range(heads)
        ]
        probs = [p.astype(jnp.bfloat16) for p in probs]
        dv = dot(jnp.concatenate(probs, 1), jnp.concatenate(gs, 0), NN)
        dk = dot(jnp.concatenate(ds, 1), jnp.concatenate(qs, 0), NN)
        kt = kt_ref[:, keys]
        news = [dot(kt, x, NN) for x in ds]
        for h in range(heads):
            dq_ref[h * DH : (h + 1) * DH, rows] += news[h]
        acc_ref[keys, :DH] += dk
        acc_ref[keys, DH:] += dv

    def use(i, dist):
        acc_ref[...] = jnp.zeros_like(acc_ref)
        kt_ref[...] = kv_ref[:, :DH].T
        over_tiles(scal, docs, dist, chunk, tile, body)
        for j, ref in enumerate(dkv_refs):

            @pl.when(i == j)
            def _():
                ref[:, :DH] = (acc_ref[:, :DH] * scaling).astype(ref.dtype)
                ref[:, DH:] = acc_ref[:, DH:].astype(ref.dtype)

    each_chunk(chunk_count(scal, docs, chunk, layers, d, count), kv_refs, kv_ref, d, True, use)
    if team is not None:
        for h in range(heads):
            full_ref[:, h * DH : (h + 1) * DH] = (
                (dq_ref[h * DH : (h + 1) * DH, :] * scaling).T.astype(jnp.bfloat16)
            )
        size = chunk // team
        for m in range(team):
            outs[m][...] = full_ref[span(scal[2] ^ m, size), :]


def grads(
    scal, docs, layers, tile, d, q, g, kvs, log_total, delta, dq, team=None, dtypes=()
):
    chunk, width = q.shape
    heads = width // DH
    first = dq is None
    extra = () if first else (dq,)
    dtypes = dtypes or (jnp.bfloat16,) * len(kvs)
    dkv_shapes = tuple(jax.ShapeDtypeStruct((chunk, 2 * DH), dtype) for dtype in dtypes)
    scratch = [
        pltpu.VMEM((chunk, 2 * DH), jnp.bfloat16),
        pltpu.VMEM((DH, chunk), jnp.bfloat16),
        pltpu.VMEM((chunk, 2 * DH), jnp.float32),
    ]
    if team is None:
        shapes = (jax.ShapeDtypeStruct((width, chunk), jnp.float32),)
    else:
        shapes = (jax.ShapeDtypeStruct((chunk // team, width), jnp.bfloat16),) * team
        scratch += [
            pltpu.VMEM((width, chunk), jnp.float32),
            pltpu.VMEM((chunk, width), jnp.bfloat16),
        ]
    return ordered_call(
        functools.partial(grads_kernel, docs, layers, tile, heads, d, first, team, len(kvs)),
        scal,
        (q, g, *kvs, log_total, delta, *extra),
        (),
        out_shape=shapes + dkv_shapes,
        out_specs=(whole(),) * (len(shapes) + len(kvs)),
        scratch_shapes=scratch,
        cost_estimate=cost(10 * chunk * chunk * width, 12 * chunk * width, chunk * chunk * heads),
        name="pair_grads",
    )


def project(scal, d, w, parts, far, blocks, begin, count, after=()):
    rows, depth = d.shape
    wide = w.shape[0] // blocks
    split = w.shape[1] // depth
    each = 0 if not parts else parts[0].shape[1] // wide

    def kernel(*refs):
        scal, d_ref, w_ref = refs[:3]
        total = dot(d_ref[...], w_ref[...], NT)
        if not parts:
            refs[-2][...] = total
            refs[-1][...] = jnp.zeros_like(refs[-1])
            return
        outs = refs[3 + len(parts) + len(after) :]
        for m in range(count):

            @pl.when(pl.program_id(0) == m)
            def _():
                outs[m][...] = (total + refs[3 + m // each][...]).astype(outs[m].dtype)

    def column(s):
        if split == 1:
            return 0
        return 1 - s[3] if far else s[3]

    def part_spec(p):
        return pl.BlockSpec((rows, wide), lambda i, s: (0, jnp.clip(i - p * each, 0, each - 1)))

    w_spec = pl.BlockSpec((wide, depth), lambda i, s: (s[2] ^ (i + begin), column(s)))
    if parts:
        out_shape = (jax.ShapeDtypeStruct((rows, wide), jnp.bfloat16),) * count
        out_specs = (pl.BlockSpec((rows, wide), lambda i, s: (0, 0)),) * count
    else:
        out_shape = (
            jax.ShapeDtypeStruct((rows, wide * count), jnp.float32),
            jax.ShapeDtypeStruct((8, 128), jnp.float32),
        )
        out_specs = (
            pl.BlockSpec((rows, wide), lambda i, s: (0, i)),
            pl.BlockSpec((8, 128), lambda i, s: (0, 0)),
        )
    grid_spec = pltpu.PrefetchScalarGridSpec(
        num_scalar_prefetch=1,
        grid=(count,),
        in_specs=[pl.BlockSpec((rows, depth), lambda i, s: (0, 0)), w_spec]
        + [part_spec(p) for p in range(len(parts))]
        + [whole(pl.ANY)] * len(after),
        out_specs=out_specs,
    )
    return pl.pallas_call(
        kernel,
        out_shape=out_shape,
        grid_spec=grid_spec,
        compiler_params=params(PROJECT_LIMIT),
        cost_estimate=cost(2 * rows * depth * wide * count, 2 * depth * wide * count),
        name="project",
    )(scal, d, w, *parts, *after)


def copies(scal, inputs, out_shapes, plan, name, after=(), limit=VMEM_LIMIT):
    n_in = len(inputs)

    def kernel(scal, *refs):
        ins, outs, sems = refs[:n_in], refs[n_in:-1], refs[-1]
        started = []
        for i, (a, src, b, dst) in enumerate(plan(scal[2])):
            copy = pltpu.make_async_copy(ins[a].at[src], outs[b].at[dst], sems.at[i])
            copy.start()
            started.append(copy)
        for copy in started:
            copy.wait()

    count = len(plan(0))
    size = sum(math.prod(s.shape) * 2 for s in out_shapes)
    return ordered_call(
        kernel,
        scal,
        inputs,
        after,
        out_shape=tuple(out_shapes),
        in_specs=[whole(pl.ANY)] * n_in,
        out_specs=(whole(pl.ANY),) * len(out_shapes),
        scratch_shapes=[pltpu.SemaphoreType.DMA((count,))],
        limit=limit,
        cost_estimate=cost(0, 2 * size),
        name=name,
    )


def add(scal, a, b, after):
    def kernel(scal, a_ref, b_ref, out_ref):
        total = a_ref[...].astype(jnp.float32) + b_ref[...].astype(jnp.float32)
        out_ref[...] = total.astype(out_ref.dtype)

    return ordered_call(
        kernel,
        scal,
        (a, b),
        after,
        out_shape=jax.ShapeDtypeStruct(a.shape, a.dtype),
        out_specs=whole(),
        cost_estimate=cost(a.size, 6 * a.size),
        name="add_terms",
    )


def span(start, size):
    if isinstance(start, int):
        return pl.ds(start, size)
    return pl.ds(pl.multiple_of(start * size, size), size)


ALL = slice(None)


def solution(mesh):
    n_seq = mesh.shape["seq"]
    n_head = mesh.shape["head"]

    def shards(queries, keys, values, d_out, w_out, doc_starts):
        rows = queries.shape[0]
        groups = keys.shape[1] // DH
        heads = queries.shape[1] // keys.shape[1]
        width = heads * DH
        docs = doc_starts.shape[0]
        team = groups
        layers = n_seq // team
        chunk = team * rows
        tile = 256 if chunk % 256 == 0 else rows
        me = lax.axis_index("seq")
        layer = me // team
        head = lax.axis_index("head")
        base = layer * chunk
        scal = jnp.concatenate([jnp.stack([base, base, me % team, head]), doc_starts])
        ends = jnp.concatenate([doc_starts[1:], jnp.full((1,), chunk * layers, jnp.int32)])
        far = jnp.any((ends - 1) // chunk - doc_starts // chunk > 2)

        def half(*shape):
            return jax.ShapeDtypeStruct(shape, jnp.bfloat16)

        def swap(m, x):
            return lax.ppermute(x, "seq", [(i, i ^ m) for i in range(n_seq)])

        def swapped(parts):
            got = list(parts)
            for m in reversed(range(1, team)):
                got[m] = swap(m, parts[m])
            return got

        def shift(d, x, first=0):
            pairs = [
                (i, i + d * team)
                for i in range(first * team, n_seq)
                if 0 <= i + d * team < n_seq
            ]
            return lax.ppermute(x, "seq", pairs)

        def pack(groups_of):
            arrays = [x for group in groups_of for x, _ in group]

            def plan(place):
                out = []
                a = b = 0
                for group in groups_of:
                    for m in range(team):
                        at = 0
                        for i, (_, size) in enumerate(group):
                            dst = (ALL, pl.ds(at, size))
                            out.append((a + i, (ALL, span(place ^ m, size)), b, dst))
                            at += size
                        b += 1
                    a += len(group)
                return out

            shapes = [half(rows, sum(n for _, n in group)) for group in groups_of for _ in range(team)]
            outs = copies(scal, arrays, shapes, plan, "pack_columns", (), PACK_LIMIT)
            return [outs[i : i + team] for i in range(0, len(outs), team)]

        def stack(parts, sizes, name, after=()):
            def plan(place):
                out = []
                for m in range(team):
                    at = 0
                    for b, size in enumerate(sizes):
                        out.append((m, (ALL, pl.ds(at, size)), b, (span(place ^ m, rows), ALL)))
                        at += size
                return out

            return copies(scal, parts, [half(chunk, size) for size in sizes], plan, name, after)

        def beside(parts, sizes, name):
            def plan(place):
                out = []
                for m in range(team):
                    at = 0
                    for b, size in enumerate(sizes):
                        out.append((m, (ALL, pl.ds(at, size)), b, (ALL, span(place ^ m, size))))
                        at += size
                return out

            shapes = [half(rows, team * size) for size in sizes]
            return copies(scal, parts, shapes, plan, name)

        if n_head == 2:
            d_far = lax.ppermute(d_out, "head", [(0, 1), (1, 0)])
        if team > 1:
            kv_sent, q_sent = pack([[(keys, DH), (values, DH)], [(queries, width)]])
            kv_got = swapped(kv_sent)
            q_got = swapped(q_sent)
            near = []
            marks = []
            if n_head == 2:
                part, end = project(scal, d_out, w_out, (), False, team, 0, team, kv_sent[:1])
                near.append(part)
                marks.append(end)
            (kv,) = stack(kv_got, [2 * DH], "stack_keys_values", marks)
            order = (kv,)
        else:
            kv = jnp.concatenate([keys, values], axis=1)
            near = [project(scal, d_out, w_out, (), False, 1, 0, 1)[0]] if n_head == 2 else []
            q = queries
            order = ()
        if n_head == 2:
            g_parts = project(scal, d_far, w_out, near, True, team, 0, team, order)
        else:
            d_all = lax.all_gather(d_out, "head", axis=1, tiled=True)
            zero = jnp.zeros((rows, width * team), jnp.float32)
            g_parts = project(scal, d_all, w_out, [zero], False, team, 0, team, order)
        if team > 1:
            g_got = swapped(g_parts)
            (q,) = stack(q_got, [width], "stack_queries", g_parts[:1])
        def stack_g(after):
            if team > 1:
                return stack(g_got, [width], "stack_attn_grad", after)[0]
            return g_parts[0]

        if layers <= 4:
            steps = [kv] + [shift(1, kv) for d in range(1, min(layers, 2))]
            if layers > 2:
                shapes = [half(chunk, 2 * DH)]
                (again,) = copies(
                    scal, [steps[1]], shapes, lambda _: [(0, ALL, 0, ALL)], "copy_chunk", g_parts[:1]
                )
                steps.append(shift(1, again, 1))
            if layers == 4:
                steps.append(lax.cond(far, lambda x: shift(3, x), lambda x: x, kv))
            state = stats(scal, docs, layers, tile, 0, q, steps[:2], None, g_parts[:1])
            g = stack_g(state[:1])
            if layers > 2:
                state = stats(scal, docs, layers, tile, 2, q, steps[2:], state, (g,))
            log_total, delta = finish(g, *state)
            dq = None
            terms = []
            far_sum = None
            if layers > 2:
                dq, far_sum, *late = grads(
                    scal, docs, layers, tile, 2, q, g, steps[2:], log_total, delta, dq
                )
                far_sum = shift(-1, far_sum, 2)
                if late:
                    terms = [lax.cond(far, lambda x: shift(-3, x), lambda x: x, late[0])]
            dtypes = (jnp.float32, jnp.bfloat16)[: min(layers, 2)]
            *dq_parts, dkv, near_sum = grads(
                scal, docs, layers, tile, 0, q, g, steps[:2], log_total, delta, dq, team, dtypes
            )
            if far_sum is not None:
                near_sum = add(scal, near_sum, far_sum, ())
            terms = [shift(-1, near_sum, 1)] + terms
        else:
            rings = [[z * team + a for z in range(layers)] for a in range(team)]
            every = lax.all_gather(kv, "seq", axis_index_groups=rings)

            def chunk_at(d):
                return lax.dynamic_index_in_dim(every, jnp.maximum(layer - d, 0), 0, keepdims=False)

            def scalars(d):
                return scal - jnp.where(jnp.arange(scal.shape[0]) == 1, d * chunk, 0)

            def one(d, state):
                return tuple(stats(scalars(d), docs, layers, tile, 0, q, [chunk_at(d)], state))

            state = stats(scal, docs, layers, tile, 0, q, [kv], None)
            state = lax.fori_loop(1, layers, one, tuple(state))
            g = stack_g(())
            log_total, delta = finish(g, *state)

            def two(d, carry):
                dq, total = carry
                dq, dkv = grads(
                    scalars(d), docs, layers, tile, 0, q, g, [chunk_at(d)], log_total, delta, dq
                )
                place = jnp.maximum(layer - d, 0)
                old = lax.dynamic_index_in_dim(total, place, 0, keepdims=False)
                total = lax.dynamic_update_index_in_dim(
                    total, jnp.where(layer >= d, dkv, old), place, 0
                )
                return dq, total

            dq = jnp.zeros((width, chunk), jnp.float32)
            total = jnp.zeros((layers, chunk, 2 * DH), jnp.bfloat16)
            dq, total = lax.fori_loop(1, layers, two, (dq, total))
            *dq_parts, dkv = grads(
                scal, docs, layers, tile, 0, q, g, [kv], log_total, delta, dq, team, (jnp.float32,)
            )
            terms = [
                lax.psum_scatter(
                    total.reshape(layers * chunk, 2 * DH), "seq", axis_index_groups=rings, tiled=True
                )
            ]

        def sum_kernel(scal, *refs):
            total = refs[0][...]
            starts = [scal[FIRST_DOC + n] for n in range(docs)]
            many = reaches_far(starts, docs, chunk, chunk * layers) > 0
            for i, x in enumerate(refs[1 : 1 + len(terms)]):
                term = x[...].astype(jnp.float32)
                total = total + (term if i == 0 else jnp.where(many, term, 0.0))
            full = refs[-1]
            full[...] = total.astype(jnp.bfloat16)
            for m in range(team):
                refs[1 + len(terms) + m][...] = full[span(scal[2] ^ m, rows), :]

        dkv_parts = pl.pallas_call(
            sum_kernel,
            out_shape=(half(rows, 2 * DH),) * team,
            in_specs=[whole(pltpu.SMEM)] + [whole()] * (1 + len(terms)),
            out_specs=(whole(),) * team,
            scratch_shapes=[pltpu.VMEM((chunk, 2 * DH), jnp.bfloat16)],
            compiler_params=params(),
            name="sum_terms",
        )(scal, dkv, *terms)
        if team > 1:
            dq_parts = swapped(dq_parts)
            dkv_parts = swapped(dkv_parts)
            (query_grad,) = beside(dq_parts, [width], "place_query_grad")
            key_grad, value_grad = beside(dkv_parts, [DH, DH], "place_key_value_grad")
        else:
            query_grad = dq_parts[0]
            key_grad = dkv_parts[0][:, :DH]
            value_grad = dkv_parts[0][:, DH:]
        return (query_grad, key_grad, value_grad)

    return jax.shard_map(
        shards,
        mesh=mesh,
        in_specs=(
            P("seq", "head"),
            P("seq", "head"),
            P("seq", "head"),
            P("seq", "head"),
            P("head", None),
            P(),
        ),
        out_specs=(P("seq", "head"), P("seq", "head"), P("seq", "head")),
        check_vma=False,
    )
```

```python
import functools
import math

import jax
import jax.numpy as jnp
from jax import lax
from jax.experimental import pallas as pl
from jax.experimental.pallas import tpu as pltpu
from jax.sharding import PartitionSpec as P

DH = 128
ONES = 16
LOG2E = 1.4426950408889634
NEG = -1e30
VMEM_LIMIT = 28 * 1024 * 1024
PACK_LIMIT = 54016 * 1024
PROJECT_LIMIT = 52 * 1024 * 1024

NT = (((1,), (1,)), ((), ()))
NN = (((1,), (0,)), ((), ()))


def dot(a, b, dims):
    return lax.dot_general(a, b, dims, preferred_element_type=jnp.float32)


def params(limit=VMEM_LIMIT):
    return pltpu.CompilerParams(vmem_limit_bytes=limit)


def whole(memory_space=pltpu.VMEM):
    return pl.BlockSpec(memory_space=memory_space)


def ordered_call(kernel, scal, operands, after, **kwargs):
    count = len(after)

    def body(*refs):
        kernel(*refs[: 1 + len(operands)], *refs[1 + len(operands) + count :])

    specs = kwargs.pop("in_specs", [whole()] * len(operands))
    limit = kwargs.pop("limit", VMEM_LIMIT)
    return pl.pallas_call(
        body,
        in_specs=[whole(pltpu.SMEM)] + specs + [whole(pl.ANY)] * count,
        compiler_params=params(limit),
        **kwargs,
    )(scal, *operands, *after)


def cost(flops, nbytes, exps=0):
    return pl.CostEstimate(flops=1024, bytes_accessed=1024, transcendentals=0)


FIRST_DOC = 4


def row_starts(scal, docs, pos):
    low = jnp.zeros_like(pos)
    for n in range(docs):
        low = jnp.where(pos >= scal[FIRST_DOC + n], scal[FIRST_DOC + n], low)
    return low


def reaches_far(starts, docs, chunk, total):
    far = jnp.int32(0)
    for n in range(docs):
        end = (starts[n + 1] if n + 1 < docs else total) - 1
        far = jnp.where(end // chunk - starts[n] // chunk > 2, 1, far)
    return far


def doc_start_at(scal, docs, pos):
    low = jnp.int32(0)
    for n in range(docs):
        low = jnp.where(pos >= scal[FIRST_DOC + n], scal[FIRST_DOC + n], low)
    return low


def allowed(scal, docs, q0, k0, tq, tk):
    qpos = q0 + lax.broadcasted_iota(jnp.int32, (1, tq), 1)
    kpos = k0 + lax.broadcasted_iota(jnp.int32, (tk, 1), 0)
    return (kpos <= qpos) & (kpos >= row_starts(scal, docs, qpos))


def over_tiles(scal, docs, d, chunk, tile, body):
    tiles = chunk // tile

    def one(qo, ko, q0, tk, need):
        k0 = scal[1] - d * chunk + ko
        @pl.when(need)
        def _():
            body(qo, ko, tk, allowed(scal, docs, q0, k0, tile, tk))

    def step(qt, _):
        qo = pl.multiple_of(qt * tile, tile)
        q0 = scal[0] + qo
        low = doc_start_at(scal, docs, q0)
        k0 = scal[1] - d * chunk
        if tiles == 1:
            one(qo, 0, q0, tile, (k0 <= q0 + tile - 1) & (k0 + tile - 1 >= low))
            return 0
        all_of = (k0 + chunk - tile <= q0 + tile - 1) & (k0 + tile - 1 >= low)
        one(qo, 0, q0, chunk, all_of)

        @pl.when(jnp.logical_not(all_of))
        def _():
            def inner(kt, _):
                ko = pl.multiple_of(kt * tile, tile)
                need = (k0 + ko <= q0 + tile - 1) & (k0 + ko + tile - 1 >= low)
                one(qo, ko, q0, tile, need)
                return 0

            lax.fori_loop(0, tiles, inner, 0)

        return 0

    lax.fori_loop(0, tiles, step, 0)


def each_chunk(total, kv_refs, now_ref, d, down, use):
    count = len(kv_refs)
    if count == 1:
        now_ref[...] = kv_refs[0][...]
        use(0, d)
        return

    def one(i, _):
        for j, ref in enumerate(kv_refs):

            @pl.when(i == j)
            def _():
                now_ref[...] = ref[...]

        use(i, d + i)
        return 0

    if down:
        lax.fori_loop(0, total, lambda i, c: one(total - 1 - i, c), 0)
    else:
        lax.fori_loop(0, total, one, 0)


def chunk_count(scal, docs, chunk, layers, d, count):
    always = min(count, max(1, 3 - d))
    if always == count:
        return count
    far = reaches_far([scal[FIRST_DOC + n] for n in range(docs)], docs, chunk, chunk * layers)
    return always + (count - always) * far


def stats_kernel(docs, layers, tile, heads, d, first, count, scal, q_ref, *refs):
    kv_refs, refs = refs[:count], refs[count:]
    if first:
        m_ref, o_ref, kv_ref, vt_ref = refs
        m_ref[...] = jnp.full_like(m_ref, NEG)
        o_ref[...] = jnp.zeros_like(o_ref)
    else:
        m_in, o_in, m_ref, o_ref, kv_ref, vt_ref = refs
        m_ref[...] = m_in[...]
        o_ref[...] = o_in[...]
    chunk = q_ref.shape[0]
    factor = LOG2E / math.sqrt(DH)
    ext = DH + ONES
    vt_ref[DH:] = jnp.ones((vt_ref.shape[0] - DH, chunk), jnp.bfloat16)

    def body(qo, ko, tk, mask):
        k = kv_ref[pl.ds(ko, tk), :DH]
        vt = vt_ref[:ext, pl.ds(ko, tk)]
        rows = pl.ds(qo, tile)
        scores = [dot(k, q_ref[rows, h * DH : (h + 1) * DH], NT) for h in range(heads)]
        scores = [jnp.where(mask, s, NEG) for s in scores]
        m_old = [m_ref[h : h + 1, rows] for h in range(heads)]
        m_new = [
            jnp.maximum(m, factor * jnp.max(s, axis=0, keepdims=True))
            for m, s in zip(m_old, scores)
        ]
        alpha = [jnp.exp2(a - b) for a, b in zip(m_old, m_new)]
        probs = [jnp.exp2(s * factor - m).astype(jnp.bfloat16) for s, m in zip(scores, m_new)]
        news = [dot(vt, p, NN) for p in probs]
        for h in range(heads):
            part = slice(h * ext, (h + 1) * ext)
            m_ref[h : h + 1, rows] = m_new[h]
            o_ref[part, rows] = alpha[h] * o_ref[part, rows] + news[h]

    def use(i, dist):
        vt_ref[:DH] = kv_ref[:, DH:].T
        over_tiles(scal, docs, dist, chunk, tile, body)

    each_chunk(chunk_count(scal, docs, chunk, layers, d, count), kv_refs, kv_ref, d, False, use)


def stats(scal, docs, layers, tile, d, q, kvs, state, after=()):
    chunk, width = q.shape
    heads = width // DH
    shapes = (
        jax.ShapeDtypeStruct((heads, chunk), jnp.float32),
        jax.ShapeDtypeStruct((heads * (DH + ONES), chunk), jnp.float32),
    )
    first = state is None
    extra = () if first else state
    return ordered_call(
        functools.partial(stats_kernel, docs, layers, tile, heads, d, first, len(kvs)),
        scal,
        (q, *kvs, *extra),
        after,
        out_shape=shapes,
        out_specs=(whole(),) * 2,
        scratch_shapes=[
            pltpu.VMEM((chunk, 2 * DH), jnp.bfloat16),
            pltpu.VMEM((DH + ONES, chunk), jnp.bfloat16),
        ],
        cost_estimate=cost(4 * chunk * chunk * width, 12 * chunk * width, chunk * chunk * heads),
        name="row_stats",
    )


def finish_kernel(heads, g_ref, m_ref, o_ref, log_ref, delta_ref):
    ext = DH + ONES
    for h in range(heads):
        total = o_ref[h * ext + DH : h * ext + DH + 1, :]
        gt = g_ref[:, h * DH : (h + 1) * DH].T.astype(jnp.float32)
        part = jnp.sum(gt * o_ref[h * ext : h * ext + DH, :], axis=0, keepdims=True)
        log_ref[h : h + 1, :] = m_ref[h : h + 1, :] + jnp.log2(total)
        delta_ref[h : h + 1, :] = part / total


def finish(g, m, o):
    heads, chunk = m.shape
    shape = jax.ShapeDtypeStruct((heads, chunk), jnp.float32)
    return pl.pallas_call(
        functools.partial(finish_kernel, heads),
        out_shape=(shape, shape),
        in_specs=[whole()] * 3,
        out_specs=(whole(),) * 2,
        compiler_params=params(),
        cost_estimate=cost(2 * chunk * heads * DH, 6 * chunk * heads * DH),
        name="row_delta",
    )(g, m, o)


def grads_kernel(docs, layers, tile, heads, d, first, team, count, scal, q_ref, g_ref, *refs):
    kv_refs, refs = refs[:count], refs[count:]
    log_ref, delta_ref, refs = refs[0], refs[1], refs[2:]
    if not first:
        dq_in, refs = refs[0], refs[1:]
    if team is None:
        dq_ref, *dkv_refs, kv_ref, kt_ref, acc_ref = refs
    else:
        outs, refs = refs[:team], refs[team:]
        *dkv_refs, kv_ref, kt_ref, acc_ref, dq_ref, full_ref = refs
    chunk = q_ref.shape[0]
    scaling = 1.0 / math.sqrt(DH)
    factor = LOG2E * scaling
    if first:
        dq_ref[...] = jnp.zeros_like(dq_ref)
    else:
        dq_ref[...] = dq_in[...]

    def body(qo, ko, tk, mask):
        rows = pl.ds(qo, tile)
        keys = pl.ds(ko, tk)
        k = kv_ref[keys, :DH]
        v = kv_ref[keys, DH:]
        qs = [q_ref[rows, h * DH : (h + 1) * DH] for h in range(heads)]
        gs = [g_ref[rows, h * DH : (h + 1) * DH] for h in range(heads)]
        scores = [dot(k, q, NT) for q in qs]
        dots = [dot(v, g, NT) for g in gs]
        scores = [jnp.where(mask, s, NEG) for s in scores]
        probs = [
            jnp.exp2(scores[h] * factor - log_ref[h : h + 1, rows]) for h in range(heads)
        ]
        ds = [
            (probs[h] * (dots[h] - delta_ref[h : h + 1, rows])).astype(jnp.bfloat16)
            for h in range(heads)
        ]
        probs = [p.astype(jnp.bfloat16) for p in probs]
        dv = dot(jnp.concatenate(probs, 1), jnp.concatenate(gs, 0), NN)
        dk = dot(jnp.concatenate(ds, 1), jnp.concatenate(qs, 0), NN)
        kt = kt_ref[:, keys]
        news = [dot(kt, x, NN) for x in ds]
        for h in range(heads):
            dq_ref[h * DH : (h + 1) * DH, rows] += news[h]
        acc_ref[keys, :DH] += dk
        acc_ref[keys, DH:] += dv

    def use(i, dist):
        acc_ref[...] = jnp.zeros_like(acc_ref)
        kt_ref[...] = kv_ref[:, :DH].T
        over_tiles(scal, docs, dist, chunk, tile, body)
        for j, ref in enumerate(dkv_refs):

            @pl.when(i == j)
            def _():
                ref[:, :DH] = (acc_ref[:, :DH] * scaling).astype(ref.dtype)
                ref[:, DH:] = acc_ref[:, DH:].astype(ref.dtype)

    each_chunk(chunk_count(scal, docs, chunk, layers, d, count), kv_refs, kv_ref, d, True, use)
    if team is not None:
        for h in range(heads):
            full_ref[:, h * DH : (h + 1) * DH] = (
                (dq_ref[h * DH : (h + 1) * DH, :] * scaling).T.astype(jnp.bfloat16)
            )
        size = chunk // team
        for m in range(team):
            outs[m][...] = full_ref[span(scal[2] ^ m, size), :]


def grads(
    scal, docs, layers, tile, d, q, g, kvs, log_total, delta, dq, team=None, dtypes=()
):
    chunk, width = q.shape
    heads = width // DH
    first = dq is None
    extra = () if first else (dq,)
    dtypes = dtypes or (jnp.bfloat16,) * len(kvs)
    dkv_shapes = tuple(jax.ShapeDtypeStruct((chunk, 2 * DH), dtype) for dtype in dtypes)
    scratch = [
        pltpu.VMEM((chunk, 2 * DH), jnp.bfloat16),
        pltpu.VMEM((DH, chunk), jnp.bfloat16),
        pltpu.VMEM((chunk, 2 * DH), jnp.float32),
    ]
    if team is None:
        shapes = (jax.ShapeDtypeStruct((width, chunk), jnp.float32),)
    else:
        shapes = (jax.ShapeDtypeStruct((chunk // team, width), jnp.bfloat16),) * team
        scratch += [
            pltpu.VMEM((width, chunk), jnp.float32),
            pltpu.VMEM((chunk, width), jnp.bfloat16),
        ]
    return ordered_call(
        functools.partial(grads_kernel, docs, layers, tile, heads, d, first, team, len(kvs)),
        scal,
        (q, g, *kvs, log_total, delta, *extra),
        (),
        out_shape=shapes + dkv_shapes,
        out_specs=(whole(),) * (len(shapes) + len(kvs)),
        scratch_shapes=scratch,
        cost_estimate=cost(10 * chunk * chunk * width, 12 * chunk * width, chunk * chunk * heads),
        name="pair_grads",
    )


def project(scal, d, w, parts, far, blocks, begin, count, after=()):
    rows, depth = d.shape
    wide = w.shape[0] // blocks
    split = w.shape[1] // depth
    each = 0 if not parts else parts[0].shape[1] // wide

    def kernel(*refs):
        scal, d_ref, w_ref = refs[:3]
        total = dot(d_ref[...], w_ref[...], NT)
        if not parts:
            refs[-2][...] = total
            refs[-1][...] = jnp.zeros_like(refs[-1])
            return
        outs = refs[3 + len(parts) + len(after) :]
        for m in range(count):

            @pl.when(pl.program_id(0) == m)
            def _():
                outs[m][...] = (total + refs[3 + m // each][...]).astype(outs[m].dtype)

    def column(s):
        if split == 1:
            return 0
        return 1 - s[3] if far else s[3]

    def part_spec(p):
        return pl.BlockSpec((rows, wide), lambda i, s: (0, jnp.clip(i - p * each, 0, each - 1)))

    w_spec = pl.BlockSpec((wide, depth), lambda i, s: (s[2] ^ (i + begin), column(s)))
    if parts:
        out_shape = (jax.ShapeDtypeStruct((rows, wide), jnp.bfloat16),) * count
        out_specs = (pl.BlockSpec((rows, wide), lambda i, s: (0, 0)),) * count
    else:
        out_shape = (
            jax.ShapeDtypeStruct((rows, wide * count), jnp.float32),
            jax.ShapeDtypeStruct((8, 128), jnp.float32),
        )
        out_specs = (
            pl.BlockSpec((rows, wide), lambda i, s: (0, i)),
            pl.BlockSpec((8, 128), lambda i, s: (0, 0)),
        )
    grid_spec = pltpu.PrefetchScalarGridSpec(
        num_scalar_prefetch=1,
        grid=(count,),
        in_specs=[pl.BlockSpec((rows, depth), lambda i, s: (0, 0)), w_spec]
        + [part_spec(p) for p in range(len(parts))]
        + [whole(pl.ANY)] * len(after),
        out_specs=out_specs,
    )
    return pl.pallas_call(
        kernel,
        out_shape=out_shape,
        grid_spec=grid_spec,
        compiler_params=params(PROJECT_LIMIT),
        cost_estimate=cost(2 * rows * depth * wide * count, 2 * depth * wide * count),
        name="project",
    )(scal, d, w, *parts, *after)


def copies(scal, inputs, out_shapes, plan, name, after=(), limit=VMEM_LIMIT, space=pl.ANY):
    n_in = len(inputs)

    def kernel(scal, *refs):
        ins, outs, sems = refs[:n_in], refs[n_in:-1], refs[-1]
        started = []
        for i, (a, src, b, dst) in enumerate(plan(scal[2])):
            copy = pltpu.make_async_copy(ins[a].at[src], outs[b].at[dst], sems.at[i])
            copy.start()
            started.append(copy)
        for copy in started:
            copy.wait()

    count = len(plan(0))
    size = sum(math.prod(s.shape) * 2 for s in out_shapes)
    return ordered_call(
        kernel,
        scal,
        inputs,
        after,
        out_shape=tuple(out_shapes),
        in_specs=[whole(pl.ANY)] * n_in,
        out_specs=(whole(space),) * len(out_shapes),
        scratch_shapes=[pltpu.SemaphoreType.DMA((count,))],
        limit=limit,
        cost_estimate=cost(0, 2 * size),
        name=name,
    )


def add(scal, a, b, after):
    def kernel(scal, a_ref, b_ref, out_ref):
        total = a_ref[...].astype(jnp.float32) + b_ref[...].astype(jnp.float32)
        out_ref[...] = total.astype(out_ref.dtype)

    return ordered_call(
        kernel,
        scal,
        (a, b),
        after,
        out_shape=jax.ShapeDtypeStruct(a.shape, a.dtype),
        out_specs=whole(),
        cost_estimate=cost(a.size, 6 * a.size),
        name="add_terms",
    )


def span(start, size):
    if isinstance(start, int):
        return pl.ds(start, size)
    return pl.ds(pl.multiple_of(start * size, size), size)


ALL = slice(None)


def solution(mesh):
    n_seq = mesh.shape["seq"]
    n_head = mesh.shape["head"]

    def shards(queries, keys, values, d_out, w_out, doc_starts):
        rows = queries.shape[0]
        groups = keys.shape[1] // DH
        heads = queries.shape[1] // keys.shape[1]
        width = heads * DH
        docs = doc_starts.shape[0]
        team = groups
        layers = n_seq // team
        chunk = team * rows
        tile = 256 if chunk % 256 == 0 else rows
        me = lax.axis_index("seq")
        layer = me // team
        head = lax.axis_index("head")
        base = layer * chunk
        scal = jnp.concatenate([jnp.stack([base, base, me % team, head]), doc_starts])
        ends = jnp.concatenate([doc_starts[1:], jnp.full((1,), chunk * layers, jnp.int32)])
        far = jnp.any((ends - 1) // chunk - doc_starts // chunk > 2)

        def half(*shape):
            return jax.ShapeDtypeStruct(shape, jnp.bfloat16)

        def swap(m, x):
            return lax.ppermute(x, "seq", [(i, i ^ m) for i in range(n_seq)])

        def swapped(parts):
            got = list(parts)
            for m in reversed(range(1, team)):
                got[m] = swap(m, parts[m])
            return got

        def shift(d, x, first=0):
            pairs = [
                (i, i + d * team)
                for i in range(first * team, n_seq)
                if 0 <= i + d * team < n_seq
            ]
            return lax.ppermute(x, "seq", pairs)

        def pack(groups_of):
            arrays = [x for group in groups_of for x, _ in group]

            def plan(place):
                out = []
                a = b = 0
                for group in groups_of:
                    for m in range(team):
                        at = 0
                        for i, (_, size) in enumerate(group):
                            dst = (ALL, pl.ds(at, size))
                            out.append((a + i, (ALL, span(place ^ m, size)), b, dst))
                            at += size
                        b += 1
                    a += len(group)
                return out

            shapes = [half(rows, sum(n for _, n in group)) for group in groups_of for _ in range(team)]
            outs = copies(scal, arrays, shapes, plan, "pack_columns", (), PACK_LIMIT, pltpu.VMEM)
            return [outs[i : i + team] for i in range(0, len(outs), team)]

        def stack(parts, sizes, name, after=(), also=()):
            def plan(place):
                out = []
                for m in range(team):
                    at = 0
                    for b, size in enumerate(sizes):
                        out.append((m, (ALL, pl.ds(at, size)), b, (span(place ^ m, rows), ALL)))
                        at += size
                for i in range(len(also)):
                    out.append((team + i, (ALL, ALL), len(sizes) + i, (ALL, ALL)))
                return out

            shapes = [half(chunk, size) for size in sizes] + [half(*x.shape) for x in also]
            return copies(scal, list(parts) + list(also), shapes, plan, name, after)

        def beside(parts, sizes, name):
            def plan(place):
                out = []
                for m in range(team):
                    at = 0
                    for b, size in enumerate(sizes):
                        out.append((m, (ALL, pl.ds(at, size)), b, (ALL, span(place ^ m, size))))
                        at += size
                return out

            shapes = [half(rows, team * size) for size in sizes]
            return copies(scal, parts, shapes, plan, name)

        if n_head == 2:
            d_far = lax.ppermute(d_out, "head", [(0, 1), (1, 0)])
        if team > 1:
            kv_sent, q_sent = pack([[(keys, DH), (values, DH)], [(queries, width)]])
            kv_got = swapped(kv_sent)
            q_got = swapped(q_sent)
            near = []
            marks = []
            if n_head == 2:
                part, end = project(scal, d_out, w_out, (), False, team, 0, team, kv_sent[:1])
                near.append(part)
                marks.append(end)
            (kv,) = stack(kv_got, [2 * DH], "stack_keys_values", marks)
            order = (kv,)
        else:
            kv = jnp.concatenate([keys, values], axis=1)
            near = [project(scal, d_out, w_out, (), False, 1, 0, 1)[0]] if n_head == 2 else []
            q = queries
            order = ()
        if n_head == 2:
            g_parts = project(scal, d_far, w_out, near, True, team, 0, team, order)
        else:
            d_all = lax.all_gather(d_out, "head", axis=1, tiled=True)
            zero = jnp.zeros((rows, width * team), jnp.float32)
            g_parts = project(scal, d_all, w_out, [zero], False, team, 0, team, order)
        if team > 1:
            g_got = swapped(g_parts)
            q, kv_again = stack(q_got, [width], "stack_queries", g_parts[:1], (kv,))
        def stack_g(after):
            if team > 1:
                return stack(g_got, [width], "stack_attn_grad", after)[0]
            return g_parts[0]

        if layers <= 4:
            steps = [kv] + [shift(d, kv) for d in range(1, min(layers, 3))]
            if layers == 4:
                steps.append(lax.cond(far, lambda x: shift(3, x), lambda x: x, kv_again))
            state = stats(scal, docs, layers, tile, 0, q, steps[:2], None, g_parts[:1])
            g = stack_g(state[:1])
            if layers > 2:
                state = stats(scal, docs, layers, tile, 2, q, steps[2:], state, (g,))
            log_total, delta = finish(g, *state)
            dq = None
            terms = []
            far_sum = None
            if layers > 2:
                dq, far_sum, *late = grads(
                    scal, docs, layers, tile, 2, q, g, steps[2:], log_total, delta, dq
                )
                far_sum = shift(-1, far_sum, 2)
                if late:
                    terms = [lax.cond(far, lambda x: shift(-3, x), lambda x: x, late[0])]
            dtypes = (jnp.float32, jnp.bfloat16)[: min(layers, 2)]
            *dq_parts, dkv, near_sum = grads(
                scal, docs, layers, tile, 0, q, g, steps[:2], log_total, delta, dq, team, dtypes
            )
            if far_sum is not None:
                near_sum = add(scal, near_sum, far_sum, ())
            terms = [shift(-1, near_sum, 1)] + terms
        else:
            rings = [[z * team + a for z in range(layers)] for a in range(team)]
            every = lax.all_gather(kv, "seq", axis_index_groups=rings)

            def chunk_at(d):
                return lax.dynamic_index_in_dim(every, jnp.maximum(layer - d, 0), 0, keepdims=False)

            def scalars(d):
                return scal - jnp.where(jnp.arange(scal.shape[0]) == 1, d * chunk, 0)

            def one(d, state):
                return tuple(stats(scalars(d), docs, layers, tile, 0, q, [chunk_at(d)], state))

            state = stats(scal, docs, layers, tile, 0, q, [kv], None)
            state = lax.fori_loop(1, layers, one, tuple(state))
            g = stack_g(())
            log_total, delta = finish(g, *state)

            def two(d, carry):
                dq, total = carry
                dq, dkv = grads(
                    scalars(d), docs, layers, tile, 0, q, g, [chunk_at(d)], log_total, delta, dq
                )
                place = jnp.maximum(layer - d, 0)
                old = lax.dynamic_index_in_dim(total, place, 0, keepdims=False)
                total = lax.dynamic_update_index_in_dim(
                    total, jnp.where(layer >= d, dkv, old), place, 0
                )
                return dq, total

            dq = jnp.zeros((width, chunk), jnp.float32)
            total = jnp.zeros((layers, chunk, 2 * DH), jnp.bfloat16)
            dq, total = lax.fori_loop(1, layers, two, (dq, total))
            *dq_parts, dkv = grads(
                scal, docs, layers, tile, 0, q, g, [kv], log_total, delta, dq, team, (jnp.float32,)
            )
            terms = [
                lax.psum_scatter(
                    total.reshape(layers * chunk, 2 * DH), "seq", axis_index_groups=rings, tiled=True
                )
            ]

        def sum_kernel(scal, *refs):
            total = refs[0][...]
            starts = [scal[FIRST_DOC + n] for n in range(docs)]
            many = reaches_far(starts, docs, chunk, chunk * layers) > 0
            for i, x in enumerate(refs[1 : 1 + len(terms)]):
                term = x[...].astype(jnp.float32)
                total = total + (term if i == 0 else jnp.where(many, term, 0.0))
            full = refs[-1]
            full[...] = total.astype(jnp.bfloat16)
            for m in range(team):
                refs[1 + len(terms) + m][...] = full[span(scal[2] ^ m, rows), :]

        dkv_parts = pl.pallas_call(
            sum_kernel,
            out_shape=(half(rows, 2 * DH),) * team,
            in_specs=[whole(pltpu.SMEM)] + [whole()] * (1 + len(terms)),
            out_specs=(whole(),) * team,
            scratch_shapes=[pltpu.VMEM((chunk, 2 * DH), jnp.bfloat16)],
            compiler_params=params(),
            name="sum_terms",
        )(scal, dkv, *terms)
        if team > 1:
            dq_parts = swapped(dq_parts)
            dkv_parts = swapped(dkv_parts)
            (query_grad,) = beside(dq_parts, [width], "place_query_grad")
            key_grad, value_grad = beside(dkv_parts, [DH, DH], "place_key_value_grad")
        else:
            query_grad = dq_parts[0]
            key_grad = dkv_parts[0][:, :DH]
            value_grad = dkv_parts[0][:, DH:]
        return (query_grad, key_grad, value_grad)

    return jax.shard_map(
        shards,
        mesh=mesh,
        in_specs=(
            P("seq", "head"),
            P("seq", "head"),
            P("seq", "head"),
            P("seq", "head"),
            P("head", None),
            P(),
        ),
        out_specs=(P("seq", "head"), P("seq", "head"), P("seq", "head")),
        check_vma=False,
    )
```

```python
import functools
import math

import jax
import jax.numpy as jnp
from jax import lax
from jax.experimental import pallas as pl
from jax.experimental.pallas import tpu as pltpu
from jax.sharding import PartitionSpec as P

DH = 128
ONES = 16
LOG2E = 1.4426950408889634
NEG = -1e30
VMEM_LIMIT = 28 * 1024 * 1024
PACK_LIMIT = 54016 * 1024
PROJECT_LIMIT = 52 * 1024 * 1024

NT = (((1,), (1,)), ((), ()))
NN = (((1,), (0,)), ((), ()))


def dot(a, b, dims):
    return lax.dot_general(a, b, dims, preferred_element_type=jnp.float32)


def params(limit=VMEM_LIMIT):
    return pltpu.CompilerParams(vmem_limit_bytes=limit)


def whole(memory_space=pltpu.VMEM):
    return pl.BlockSpec(memory_space=memory_space)


def ordered_call(kernel, scal, operands, after, **kwargs):
    count = len(after)

    def body(*refs):
        kernel(*refs[: 1 + len(operands)], *refs[1 + len(operands) + count :])

    specs = kwargs.pop("in_specs", [whole()] * len(operands))
    limit = kwargs.pop("limit", VMEM_LIMIT)
    return pl.pallas_call(
        body,
        in_specs=[whole(pltpu.SMEM)] + specs + [whole(pl.ANY)] * count,
        compiler_params=params(limit),
        **kwargs,
    )(scal, *operands, *after)


def cost(flops, nbytes, exps=0):
    return pl.CostEstimate(flops=1024, bytes_accessed=1024, transcendentals=0)


FIRST_DOC = 4


def row_starts(scal, docs, pos):
    low = jnp.zeros_like(pos)
    for n in range(docs):
        low = jnp.where(pos >= scal[FIRST_DOC + n], scal[FIRST_DOC + n], low)
    return low


def reaches_far(starts, docs, chunk, total):
    far = jnp.int32(0)
    for n in range(docs):
        end = (starts[n + 1] if n + 1 < docs else total) - 1
        far = jnp.where(end // chunk - starts[n] // chunk > 2, 1, far)
    return far


def doc_start_at(scal, docs, pos):
    low = jnp.int32(0)
    for n in range(docs):
        low = jnp.where(pos >= scal[FIRST_DOC + n], scal[FIRST_DOC + n], low)
    return low


def allowed(scal, docs, q0, k0, tq, tk):
    qpos = q0 + lax.broadcasted_iota(jnp.int32, (1, tq), 1)
    kpos = k0 + lax.broadcasted_iota(jnp.int32, (tk, 1), 0)
    return (kpos <= qpos) & (kpos >= row_starts(scal, docs, qpos))


def over_tiles(scal, docs, d, chunk, tile, body):
    tiles = chunk // tile

    def one(qo, ko, q0, tk, need):
        k0 = scal[1] - d * chunk + ko
        @pl.when(need)
        def _():
            body(qo, ko, tk, allowed(scal, docs, q0, k0, tile, tk))

    def step(qt, _):
        qo = pl.multiple_of(qt * tile, tile)
        q0 = scal[0] + qo
        low = doc_start_at(scal, docs, q0)
        k0 = scal[1] - d * chunk
        if tiles == 1:
            one(qo, 0, q0, tile, (k0 <= q0 + tile - 1) & (k0 + tile - 1 >= low))
            return 0
        all_of = (k0 + chunk - tile <= q0 + tile - 1) & (k0 + tile - 1 >= low)
        one(qo, 0, q0, chunk, all_of)

        @pl.when(jnp.logical_not(all_of))
        def _():
            def inner(kt, _):
                ko = pl.multiple_of(kt * tile, tile)
                need = (k0 + ko <= q0 + tile - 1) & (k0 + ko + tile - 1 >= low)
                one(qo, ko, q0, tile, need)
                return 0

            lax.fori_loop(0, tiles, inner, 0)

        return 0

    lax.fori_loop(0, tiles, step, 0)


def each_chunk(total, kv_refs, now_ref, d, down, use):
    count = len(kv_refs)
    if count == 1:
        now_ref[...] = kv_refs[0][...]
        use(0, d)
        return

    def one(i, _):
        for j, ref in enumerate(kv_refs):

            @pl.when(i == j)
            def _():
                now_ref[...] = ref[...]

        use(i, d + i)
        return 0

    if down:
        lax.fori_loop(0, total, lambda i, c: one(total - 1 - i, c), 0)
    else:
        lax.fori_loop(0, total, one, 0)


def chunk_count(scal, docs, chunk, layers, d, count):
    always = min(count, max(1, 3 - d))
    if always == count:
        return count
    far = reaches_far([scal[FIRST_DOC + n] for n in range(docs)], docs, chunk, chunk * layers)
    return always + (count - always) * far


def stats_kernel(docs, layers, tile, heads, d, first, count, scal, q_ref, *refs):
    kv_refs, refs = refs[:count], refs[count:]
    if first:
        m_ref, o_ref, kv_ref, vt_ref = refs
        m_ref[...] = jnp.full_like(m_ref, NEG)
        o_ref[...] = jnp.zeros_like(o_ref)
    else:
        m_in, o_in, m_ref, o_ref, kv_ref, vt_ref = refs
        m_ref[...] = m_in[...]
        o_ref[...] = o_in[...]
    chunk = q_ref.shape[0]
    factor = LOG2E / math.sqrt(DH)
    ext = DH + ONES
    vt_ref[DH:] = jnp.ones((vt_ref.shape[0] - DH, chunk), jnp.bfloat16)

    def body(qo, ko, tk, mask):
        k = kv_ref[pl.ds(ko, tk), :DH]
        vt = vt_ref[:ext, pl.ds(ko, tk)]
        rows = pl.ds(qo, tile)
        scores = [dot(k, q_ref[rows, h * DH : (h + 1) * DH], NT) for h in range(heads)]
        scores = [jnp.where(mask, s, NEG) for s in scores]
        m_old = [m_ref[h : h + 1, rows] for h in range(heads)]
        m_new = [
            jnp.maximum(m, factor * jnp.max(s, axis=0, keepdims=True))
            for m, s in zip(m_old, scores)
        ]
        alpha = [jnp.exp2(a - b) for a, b in zip(m_old, m_new)]
        probs = [jnp.exp2(s * factor - m).astype(jnp.bfloat16) for s, m in zip(scores, m_new)]
        news = [dot(vt, p, NN) for p in probs]
        for h in range(heads):
            part = slice(h * ext, (h + 1) * ext)
            m_ref[h : h + 1, rows] = m_new[h]
            o_ref[part, rows] = alpha[h] * o_ref[part, rows] + news[h]

    def use(i, dist):
        vt_ref[:DH] = kv_ref[:, DH:].T
        over_tiles(scal, docs, dist, chunk, tile, body)

    each_chunk(chunk_count(scal, docs, chunk, layers, d, count), kv_refs, kv_ref, d, False, use)


def stats(scal, docs, layers, tile, d, q, kvs, state, after=()):
    chunk, width = q.shape
    heads = width // DH
    shapes = (
        jax.ShapeDtypeStruct((heads, chunk), jnp.float32),
        jax.ShapeDtypeStruct((heads * (DH + ONES), chunk), jnp.float32),
    )
    first = state is None
    extra = () if first else state
    return ordered_call(
        functools.partial(stats_kernel, docs, layers, tile, heads, d, first, len(kvs)),
        scal,
        (q, *kvs, *extra),
        after,
        out_shape=shapes,
        out_specs=(whole(),) * 2,
        scratch_shapes=[
            pltpu.VMEM((chunk, 2 * DH), jnp.bfloat16),
            pltpu.VMEM((DH + ONES, chunk), jnp.bfloat16),
        ],
        cost_estimate=cost(4 * chunk * chunk * width, 12 * chunk * width, chunk * chunk * heads),
        name="row_stats",
    )


def finish_kernel(heads, g_ref, m_ref, o_ref, log_ref, delta_ref):
    ext = DH + ONES
    for h in range(heads):
        total = o_ref[h * ext + DH : h * ext + DH + 1, :]
        gt = g_ref[:, h * DH : (h + 1) * DH].T.astype(jnp.float32)
        part = jnp.sum(gt * o_ref[h * ext : h * ext + DH, :], axis=0, keepdims=True)
        log_ref[h : h + 1, :] = m_ref[h : h + 1, :] + jnp.log2(total)
        delta_ref[h : h + 1, :] = part / total


def finish(g, m, o):
    heads, chunk = m.shape
    shape = jax.ShapeDtypeStruct((heads, chunk), jnp.float32)
    return pl.pallas_call(
        functools.partial(finish_kernel, heads),
        out_shape=(shape, shape),
        in_specs=[whole()] * 3,
        out_specs=(whole(),) * 2,
        compiler_params=params(),
        cost_estimate=cost(2 * chunk * heads * DH, 6 * chunk * heads * DH),
        name="row_delta",
    )(g, m, o)


def grads_kernel(docs, layers, tile, heads, d, first, team, count, scal, q_ref, g_ref, *refs):
    kv_refs, refs = refs[:count], refs[count:]
    log_ref, delta_ref, refs = refs[0], refs[1], refs[2:]
    if not first:
        dq_in, refs = refs[0], refs[1:]
    if team is None:
        dq_ref, *dkv_refs, kv_ref, kt_ref, acc_ref = refs
    else:
        outs, refs = refs[:team], refs[team:]
        *dkv_refs, kv_ref, kt_ref, acc_ref, dq_ref, full_ref = refs
    chunk = q_ref.shape[0]
    scaling = 1.0 / math.sqrt(DH)
    factor = LOG2E * scaling
    if first:
        dq_ref[...] = jnp.zeros_like(dq_ref)
    else:
        dq_ref[...] = dq_in[...]

    def body(qo, ko, tk, mask):
        rows = pl.ds(qo, tile)
        keys = pl.ds(ko, tk)
        k = kv_ref[keys, :DH]
        v = kv_ref[keys, DH:]
        qs = [q_ref[rows, h * DH : (h + 1) * DH] for h in range(heads)]
        gs = [g_ref[rows, h * DH : (h + 1) * DH] for h in range(heads)]
        scores = [dot(k, q, NT) for q in qs]
        dots = [dot(v, g, NT) for g in gs]
        scores = [jnp.where(mask, s, NEG) for s in scores]
        probs = [
            jnp.exp2(scores[h] * factor - log_ref[h : h + 1, rows]) for h in range(heads)
        ]
        ds = [
            (probs[h] * (dots[h] - delta_ref[h : h + 1, rows])).astype(jnp.bfloat16)
            for h in range(heads)
        ]
        probs = [p.astype(jnp.bfloat16) for p in probs]
        dv = dot(jnp.concatenate(probs, 1), jnp.concatenate(gs, 0), NN)
        dk = dot(jnp.concatenate(ds, 1), jnp.concatenate(qs, 0), NN)
        kt = kt_ref[:, keys]
        news = [dot(kt, x, NN) for x in ds]
        for h in range(heads):
            dq_ref[h * DH : (h + 1) * DH, rows] += news[h]
        acc_ref[keys, :DH] += dk
        acc_ref[keys, DH:] += dv

    def use(i, dist):
        acc_ref[...] = jnp.zeros_like(acc_ref)
        kt_ref[...] = kv_ref[:, :DH].T
        over_tiles(scal, docs, dist, chunk, tile, body)
        for j, ref in enumerate(dkv_refs):

            @pl.when(i == j)
            def _():
                ref[:, :DH] = (acc_ref[:, :DH] * scaling).astype(ref.dtype)
                ref[:, DH:] = acc_ref[:, DH:].astype(ref.dtype)

    each_chunk(chunk_count(scal, docs, chunk, layers, d, count), kv_refs, kv_ref, d, True, use)
    if team is not None:
        for h in range(heads):
            full_ref[:, h * DH : (h + 1) * DH] = (
                (dq_ref[h * DH : (h + 1) * DH, :] * scaling).T.astype(jnp.bfloat16)
            )
        size = chunk // team
        for m in range(team):
            outs[m][...] = full_ref[span(scal[2] ^ m, size), :]


def grads(
    scal, docs, layers, tile, d, q, g, kvs, log_total, delta, dq, team=None, dtypes=(), after=()
):
    chunk, width = q.shape
    heads = width // DH
    first = dq is None
    extra = () if first else (dq,)
    dtypes = dtypes or (jnp.bfloat16,) * len(kvs)
    dkv_shapes = tuple(jax.ShapeDtypeStruct((chunk, 2 * DH), dtype) for dtype in dtypes)
    scratch = [
        pltpu.VMEM((chunk, 2 * DH), jnp.bfloat16),
        pltpu.VMEM((DH, chunk), jnp.bfloat16),
        pltpu.VMEM((chunk, 2 * DH), jnp.float32),
    ]
    if team is None:
        shapes = (jax.ShapeDtypeStruct((width, chunk), jnp.float32),)
    else:
        shapes = (jax.ShapeDtypeStruct((chunk // team, width), jnp.bfloat16),) * team
        scratch += [
            pltpu.VMEM((width, chunk), jnp.float32),
            pltpu.VMEM((chunk, width), jnp.bfloat16),
        ]
    return ordered_call(
        functools.partial(grads_kernel, docs, layers, tile, heads, d, first, team, len(kvs)),
        scal,
        (q, g, *kvs, log_total, delta, *extra),
        after,
        out_shape=shapes + dkv_shapes,
        out_specs=(whole(),) * (len(shapes) + len(kvs)),
        scratch_shapes=scratch,
        cost_estimate=cost(10 * chunk * chunk * width, 12 * chunk * width, chunk * chunk * heads),
        name="pair_grads",
    )


def project(scal, d, w, parts, far, blocks, begin, count, after=()):
    rows, depth = d.shape
    wide = w.shape[0] // blocks
    split = w.shape[1] // depth
    each = 0 if not parts else parts[0].shape[1] // wide

    def kernel(*refs):
        scal, d_ref, w_ref = refs[:3]
        total = dot(d_ref[...], w_ref[...], NT)
        if not parts:
            refs[-2][...] = total
            refs[-1][...] = jnp.zeros_like(refs[-1])
            return
        outs = refs[3 + len(parts) + len(after) :]
        for m in range(count):

            @pl.when(pl.program_id(0) == m)
            def _():
                outs[m][...] = (total + refs[3 + m // each][...]).astype(outs[m].dtype)

    def column(s):
        if split == 1:
            return 0
        return 1 - s[3] if far else s[3]

    def part_spec(p):
        return pl.BlockSpec((rows, wide), lambda i, s: (0, jnp.clip(i - p * each, 0, each - 1)))

    w_spec = pl.BlockSpec((wide, depth), lambda i, s: (s[2] ^ (i + begin), column(s)))
    if parts:
        out_shape = (jax.ShapeDtypeStruct((rows, wide), jnp.bfloat16),) * count
        out_specs = (pl.BlockSpec((rows, wide), lambda i, s: (0, 0)),) * count
    else:
        out_shape = (
            jax.ShapeDtypeStruct((rows, wide * count), jnp.float32),
            jax.ShapeDtypeStruct((8, 128), jnp.float32),
        )
        out_specs = (
            pl.BlockSpec((rows, wide), lambda i, s: (0, i)),
            pl.BlockSpec((8, 128), lambda i, s: (0, 0)),
        )
    grid_spec = pltpu.PrefetchScalarGridSpec(
        num_scalar_prefetch=1,
        grid=(count,),
        in_specs=[pl.BlockSpec((rows, depth), lambda i, s: (0, 0)), w_spec]
        + [part_spec(p) for p in range(len(parts))]
        + [whole(pl.ANY)] * len(after),
        out_specs=out_specs,
    )
    return pl.pallas_call(
        kernel,
        out_shape=out_shape,
        grid_spec=grid_spec,
        compiler_params=params(PROJECT_LIMIT),
        cost_estimate=cost(2 * rows * depth * wide * count, 2 * depth * wide * count),
        name="project",
    )(scal, d, w, *parts, *after)


def copies(scal, inputs, out_shapes, plan, name, after=(), limit=VMEM_LIMIT, space=pl.ANY):
    n_in = len(inputs)

    def kernel(scal, *refs):
        ins, outs, sems = refs[:n_in], refs[n_in:-1], refs[-1]
        started = []
        for i, (a, src, b, dst) in enumerate(plan(scal[2])):
            copy = pltpu.make_async_copy(ins[a].at[src], outs[b].at[dst], sems.at[i])
            copy.start()
            started.append(copy)
        for copy in started:
            copy.wait()

    count = len(plan(0))
    size = sum(math.prod(s.shape) * 2 for s in out_shapes)
    return ordered_call(
        kernel,
        scal,
        inputs,
        after,
        out_shape=tuple(out_shapes),
        in_specs=[whole(pl.ANY)] * n_in,
        out_specs=(whole(space),) * len(out_shapes),
        scratch_shapes=[pltpu.SemaphoreType.DMA((count,))],
        limit=limit,
        cost_estimate=cost(0, 2 * size),
        name=name,
    )


def add(scal, a, b, after):
    def kernel(scal, a_ref, b_ref, out_ref):
        total = a_ref[...].astype(jnp.float32) + b_ref[...].astype(jnp.float32)
        out_ref[...] = total.astype(out_ref.dtype)

    return ordered_call(
        kernel,
        scal,
        (a, b),
        after,
        out_shape=jax.ShapeDtypeStruct(a.shape, a.dtype),
        out_specs=whole(),
        cost_estimate=cost(a.size, 6 * a.size),
        name="add_terms",
    )


def span(start, size):
    if isinstance(start, int):
        return pl.ds(start, size)
    return pl.ds(pl.multiple_of(start * size, size), size)


ALL = slice(None)


def solution(mesh):
    n_seq = mesh.shape["seq"]
    n_head = mesh.shape["head"]

    def shards(queries, keys, values, d_out, w_out, doc_starts):
        rows = queries.shape[0]
        groups = keys.shape[1] // DH
        heads = queries.shape[1] // keys.shape[1]
        width = heads * DH
        docs = doc_starts.shape[0]
        team = groups
        layers = n_seq // team
        chunk = team * rows
        tile = 256 if chunk % 256 == 0 else rows
        me = lax.axis_index("seq")
        layer = me // team
        head = lax.axis_index("head")
        base = layer * chunk
        scal = jnp.concatenate([jnp.stack([base, base, me % team, head]), doc_starts])
        ends = jnp.concatenate([doc_starts[1:], jnp.full((1,), chunk * layers, jnp.int32)])
        far = jnp.any((ends - 1) // chunk - doc_starts // chunk > 2)

        def half(*shape):
            return jax.ShapeDtypeStruct(shape, jnp.bfloat16)

        def swap(m, x):
            return lax.ppermute(x, "seq", [(i, i ^ m) for i in range(n_seq)])

        def swapped(parts):
            got = list(parts)
            for m in reversed(range(1, team)):
                got[m] = swap(m, parts[m])
            return got

        def shift(d, x, first=0):
            pairs = [
                (i, i + d * team)
                for i in range(first * team, n_seq)
                if 0 <= i + d * team < n_seq
            ]
            return lax.ppermute(x, "seq", pairs)

        def pack(groups_of):
            arrays = [x for group in groups_of for x, _ in group]

            def plan(place):
                out = []
                a = b = 0
                for group in groups_of:
                    for m in range(team):
                        at = 0
                        for i, (_, size) in enumerate(group):
                            dst = (ALL, pl.ds(at, size))
                            out.append((a + i, (ALL, span(place ^ m, size)), b, dst))
                            at += size
                        b += 1
                    a += len(group)
                return out

            shapes = [half(rows, sum(n for _, n in group)) for group in groups_of for _ in range(team)]
            outs = copies(scal, arrays, shapes, plan, "pack_columns", (), PACK_LIMIT, pltpu.VMEM)
            return [outs[i : i + team] for i in range(0, len(outs), team)]

        def stack(parts, sizes, name, after=(), also=()):
            def plan(place):
                out = []
                for m in range(team):
                    at = 0
                    for b, size in enumerate(sizes):
                        out.append((m, (ALL, pl.ds(at, size)), b, (span(place ^ m, rows), ALL)))
                        at += size
                for i in range(len(also)):
                    out.append((team + i, (ALL, ALL), len(sizes) + i, (ALL, ALL)))
                return out

            shapes = [half(chunk, size) for size in sizes] + [half(*x.shape) for x in also]
            return copies(scal, list(parts) + list(also), shapes, plan, name, after)

        def beside(parts, sizes, name):
            def plan(place):
                out = []
                for m in range(team):
                    at = 0
                    for b, size in enumerate(sizes):
                        out.append((m, (ALL, pl.ds(at, size)), b, (ALL, span(place ^ m, size))))
                        at += size
                return out

            shapes = [half(rows, team * size) for size in sizes]
            return copies(scal, parts, shapes, plan, name)

        if n_head == 2:
            d_far = lax.ppermute(d_out, "head", [(0, 1), (1, 0)])
        if team > 1:
            kv_sent, q_sent = pack([[(keys, DH), (values, DH)], [(queries, width)]])
            kv_got = swapped(kv_sent)
            q_got = swapped(q_sent)
            near = []
            marks = []
            if n_head == 2:
                part, end = project(scal, d_out, w_out, (), False, team, 0, team, kv_sent[:1])
                near.append(part)
                marks.append(end)
            (kv,) = stack(kv_got, [2 * DH], "stack_keys_values", marks)
            order = (kv,)
        else:
            kv = jnp.concatenate([keys, values], axis=1)
            near = [project(scal, d_out, w_out, (), False, 1, 0, 1)[0]] if n_head == 2 else []
            q = queries
            order = ()
        if n_head == 2:
            g_parts = project(scal, d_far, w_out, near, True, team, 0, team, order)
        else:
            d_all = lax.all_gather(d_out, "head", axis=1, tiled=True)
            zero = jnp.zeros((rows, width * team), jnp.float32)
            g_parts = project(scal, d_all, w_out, [zero], False, team, 0, team, order)
        if team > 1:
            g_got = swapped(g_parts)
            q, kv_again = stack(q_got, [width], "stack_queries", g_parts[:1], (kv,))
        def stack_g(after):
            if team > 1:
                return stack(g_got, [width], "stack_attn_grad", after)[0]
            return g_parts[0]

        if layers <= 4:
            steps = [kv] + [shift(d, kv) for d in range(1, min(layers, 3))]
            if layers == 4:
                steps.append(lax.cond(far, lambda x: shift(3, x), lambda x: x, kv_again))
            state = stats(scal, docs, layers, tile, 0, q, steps[:2], None, g_parts[:1])
            g = stack_g(state[:1])
            if layers > 2:
                state = stats(scal, docs, layers, tile, 2, q, steps[2:], state, (g,))
            log_total, delta = finish(g, *state)
            dq = None
            terms = []
            far_sum = None
            if layers > 2:
                dq, far_sum, *late = grads(
                    scal, docs, layers, tile, 2, q, g, steps[2:], log_total, delta, dq
                )
                far_sum = shift(-1, far_sum, 2)
                if late:
                    terms = [lax.cond(far, lambda x: shift(-3, x), lambda x: x, late[0])]
            dq, near_sum = grads(
                scal, docs, layers, tile, 1, q, g, steps[1:2], log_total, delta, dq
            )
            if far_sum is not None:
                near_sum = add(scal, near_sum, far_sum, ())
            terms = [shift(-1, near_sum, 1)] + terms
            *dq_parts, dkv = grads(
                scal,
                docs,
                layers,
                tile,
                0,
                q,
                g,
                [kv],
                log_total,
                delta,
                dq,
                team,
                (jnp.float32,),
                (near_sum,),
            )
        else:
            rings = [[z * team + a for z in range(layers)] for a in range(team)]
            every = lax.all_gather(kv, "seq", axis_index_groups=rings)

            def chunk_at(d):
                return lax.dynamic_index_in_dim(every, jnp.maximum(layer - d, 0), 0, keepdims=False)

            def scalars(d):
                return scal - jnp.where(jnp.arange(scal.shape[0]) == 1, d * chunk, 0)

            def one(d, state):
                return tuple(stats(scalars(d), docs, layers, tile, 0, q, [chunk_at(d)], state))

            state = stats(scal, docs, layers, tile, 0, q, [kv], None)
            state = lax.fori_loop(1, layers, one, tuple(state))
            g = stack_g(())
            log_total, delta = finish(g, *state)

            def two(d, carry):
                dq, total = carry
                dq, dkv = grads(
                    scalars(d), docs, layers, tile, 0, q, g, [chunk_at(d)], log_total, delta, dq
                )
                place = jnp.maximum(layer - d, 0)
                old = lax.dynamic_index_in_dim(total, place, 0, keepdims=False)
                total = lax.dynamic_update_index_in_dim(
                    total, jnp.where(layer >= d, dkv, old), place, 0
                )
                return dq, total

            dq = jnp.zeros((width, chunk), jnp.float32)
            total = jnp.zeros((layers, chunk, 2 * DH), jnp.bfloat16)
            dq, total = lax.fori_loop(1, layers, two, (dq, total))
            *dq_parts, dkv = grads(
                scal, docs, layers, tile, 0, q, g, [kv], log_total, delta, dq, team, (jnp.float32,)
            )
            terms = [
                lax.psum_scatter(
                    total.reshape(layers * chunk, 2 * DH), "seq", axis_index_groups=rings, tiled=True
                )
            ]

        def sum_kernel(scal, *refs):
            total = refs[0][...]
            starts = [scal[FIRST_DOC + n] for n in range(docs)]
            many = reaches_far(starts, docs, chunk, chunk * layers) > 0
            for i, x in enumerate(refs[1 : 1 + len(terms)]):
                term = x[...].astype(jnp.float32)
                total = total + (term if i == 0 else jnp.where(many, term, 0.0))
            full = refs[-1]
            full[...] = total.astype(jnp.bfloat16)
            for m in range(team):
                refs[1 + len(terms) + m][...] = full[span(scal[2] ^ m, rows), :]

        dkv_parts = pl.pallas_call(
            sum_kernel,
            out_shape=(half(rows, 2 * DH),) * team,
            in_specs=[whole(pltpu.SMEM)] + [whole()] * (1 + len(terms)),
            out_specs=(whole(),) * team,
            scratch_shapes=[pltpu.VMEM((chunk, 2 * DH), jnp.bfloat16)],
            compiler_params=params(),
            name="sum_terms",
        )(scal, dkv, *terms)
        if team > 1:
            dq_parts = swapped(dq_parts)
            dkv_parts = swapped(dkv_parts)
            (query_grad,) = beside(dq_parts, [width], "place_query_grad")
            key_grad, value_grad = beside(dkv_parts, [DH, DH], "place_key_value_grad")
        else:
            query_grad = dq_parts[0]
            key_grad = dkv_parts[0][:, :DH]
            value_grad = dkv_parts[0][:, DH:]
        return (query_grad, key_grad, value_grad)

    return jax.shard_map(
        shards,
        mesh=mesh,
        in_specs=(
            P("seq", "head"),
            P("seq", "head"),
            P("seq", "head"),
            P("seq", "head"),
            P("head", None),
            P(),
        ),
        out_specs=(P("seq", "head"), P("seq", "head"), P("seq", "head")),
        check_vma=False,
    )
```

```python
import functools
import math

import jax
import jax.numpy as jnp
from jax import lax
from jax.experimental import pallas as pl
from jax.experimental.pallas import tpu as pltpu
from jax.sharding import PartitionSpec as P

DH = 128
ONES = 16
LOG2E = 1.4426950408889634
NEG = -1e30
VMEM_LIMIT = 28 * 1024 * 1024
PACK_LIMIT = 54016 * 1024
PROJECT_LIMIT = 53760 * 1024

NT = (((1,), (1,)), ((), ()))
NN = (((1,), (0,)), ((), ()))


def dot(a, b, dims):
    return lax.dot_general(a, b, dims, preferred_element_type=jnp.float32)


def params(limit=VMEM_LIMIT):
    return pltpu.CompilerParams(vmem_limit_bytes=limit)


def whole(memory_space=pltpu.VMEM):
    return pl.BlockSpec(memory_space=memory_space)


def ordered_call(kernel, scal, operands, after, **kwargs):
    count = len(after)

    def body(*refs):
        kernel(*refs[: 1 + len(operands)], *refs[1 + len(operands) + count :])

    specs = kwargs.pop("in_specs", [whole()] * len(operands))
    limit = kwargs.pop("limit", VMEM_LIMIT)
    return pl.pallas_call(
        body,
        in_specs=[whole(pltpu.SMEM)] + specs + [whole(pl.ANY)] * count,
        compiler_params=params(limit),
        **kwargs,
    )(scal, *operands, *after)


def cost(flops, nbytes, exps=0):
    return pl.CostEstimate(flops=1024, bytes_accessed=1024, transcendentals=0)


FIRST_DOC = 4


def row_starts(scal, docs, pos):
    low = jnp.zeros_like(pos)
    for n in range(docs):
        low = jnp.where(pos >= scal[FIRST_DOC + n], scal[FIRST_DOC + n], low)
    return low


def reaches_far(starts, docs, chunk, total):
    far = jnp.int32(0)
    for n in range(docs):
        end = (starts[n + 1] if n + 1 < docs else total) - 1
        far = jnp.where(end // chunk - starts[n] // chunk > 2, 1, far)
    return far


def doc_start_at(scal, docs, pos):
    low = jnp.int32(0)
    for n in range(docs):
        low = jnp.where(pos >= scal[FIRST_DOC + n], scal[FIRST_DOC + n], low)
    return low


def allowed(scal, docs, q0, k0, tq, tk):
    qpos = q0 + lax.broadcasted_iota(jnp.int32, (1, tq), 1)
    kpos = k0 + lax.broadcasted_iota(jnp.int32, (tk, 1), 0)
    return (kpos <= qpos) & (kpos >= row_starts(scal, docs, qpos))


def over_tiles(scal, docs, d, chunk, tile, body):
    tiles = chunk // tile

    def one(qo, ko, q0, tk, need):
        k0 = scal[1] - d * chunk + ko
        @pl.when(need)
        def _():
            body(qo, ko, tk, allowed(scal, docs, q0, k0, tile, tk))

    def step(qt, _):
        qo = pl.multiple_of(qt * tile, tile)
        q0 = scal[0] + qo
        low = doc_start_at(scal, docs, q0)
        k0 = scal[1] - d * chunk
        if tiles == 1:
            one(qo, 0, q0, tile, (k0 <= q0 + tile - 1) & (k0 + tile - 1 >= low))
            return 0
        all_of = (k0 + chunk - tile <= q0 + tile - 1) & (k0 + tile - 1 >= low)
        one(qo, 0, q0, chunk, all_of)

        @pl.when(jnp.logical_not(all_of))
        def _():
            def inner(kt, _):
                ko = pl.multiple_of(kt * tile, tile)
                need = (k0 + ko <= q0 + tile - 1) & (k0 + ko + tile - 1 >= low)
                one(qo, ko, q0, tile, need)
                return 0

            lax.fori_loop(0, tiles, inner, 0)

        return 0

    lax.fori_loop(0, tiles, step, 0)


def each_chunk(total, kv_refs, now_ref, d, down, use):
    count = len(kv_refs)
    if count == 1:
        now_ref[...] = kv_refs[0][...]
        use(0, d)
        return

    def one(i, _):
        for j, ref in enumerate(kv_refs):

            @pl.when(i == j)
            def _():
                now_ref[...] = ref[...]

        use(i, d + i)
        return 0

    if down:
        lax.fori_loop(0, total, lambda i, c: one(total - 1 - i, c), 0)
    else:
        lax.fori_loop(0, total, one, 0)


def chunk_count(scal, docs, chunk, layers, d, count):
    always = min(count, max(1, 3 - d))
    if always == count:
        return count
    far = reaches_far([scal[FIRST_DOC + n] for n in range(docs)], docs, chunk, chunk * layers)
    return always + (count - always) * far


def stats_kernel(docs, layers, tile, heads, d, first, count, scal, q_ref, *refs):
    kv_refs, refs = refs[:count], refs[count:]
    if first:
        m_ref, o_ref, kv_ref, vt_ref = refs
        m_ref[...] = jnp.full_like(m_ref, NEG)
        o_ref[...] = jnp.zeros_like(o_ref)
    else:
        m_in, o_in, m_ref, o_ref, kv_ref, vt_ref = refs
        m_ref[...] = m_in[...]
        o_ref[...] = o_in[...]
    chunk = q_ref.shape[0]
    factor = LOG2E / math.sqrt(DH)
    ext = DH + ONES
    vt_ref[DH:] = jnp.ones((vt_ref.shape[0] - DH, chunk), jnp.bfloat16)

    def body(qo, ko, tk, mask):
        k = kv_ref[pl.ds(ko, tk), :DH]
        vt = vt_ref[:ext, pl.ds(ko, tk)]
        rows = pl.ds(qo, tile)
        scores = [dot(k, q_ref[rows, h * DH : (h + 1) * DH], NT) for h in range(heads)]
        scores = [jnp.where(mask, s, NEG) for s in scores]
        m_old = [m_ref[h : h + 1, rows] for h in range(heads)]
        m_new = [
            jnp.maximum(m, factor * jnp.max(s, axis=0, keepdims=True))
            for m, s in zip(m_old, scores)
        ]
        alpha = [jnp.exp2(a - b) for a, b in zip(m_old, m_new)]
        probs = [jnp.exp2(s * factor - m).astype(jnp.bfloat16) for s, m in zip(scores, m_new)]
        news = [dot(vt, p, NN) for p in probs]
        for h in range(heads):
            part = slice(h * ext, (h + 1) * ext)
            m_ref[h : h + 1, rows] = m_new[h]
            o_ref[part, rows] = alpha[h] * o_ref[part, rows] + news[h]

    def use(i, dist):
        vt_ref[:DH] = kv_ref[:, DH:].T
        over_tiles(scal, docs, dist, chunk, tile, body)

    each_chunk(chunk_count(scal, docs, chunk, layers, d, count), kv_refs, kv_ref, d, False, use)


def stats(scal, docs, layers, tile, d, q, kvs, state, after=()):
    chunk, width = q.shape
    heads = width // DH
    shapes = (
        jax.ShapeDtypeStruct((heads, chunk), jnp.float32),
        jax.ShapeDtypeStruct((heads * (DH + ONES), chunk), jnp.float32),
    )
    first = state is None
    extra = () if first else state
    return ordered_call(
        functools.partial(stats_kernel, docs, layers, tile, heads, d, first, len(kvs)),
        scal,
        (q, *kvs, *extra),
        after,
        out_shape=shapes,
        out_specs=(whole(),) * 2,
        scratch_shapes=[
            pltpu.VMEM((chunk, 2 * DH), jnp.bfloat16),
            pltpu.VMEM((DH + ONES, chunk), jnp.bfloat16),
        ],
        cost_estimate=cost(4 * chunk * chunk * width, 12 * chunk * width, chunk * chunk * heads),
        name="row_stats",
    )


def finish_kernel(heads, g_ref, m_ref, o_ref, log_ref, delta_ref):
    ext = DH + ONES
    for h in range(heads):
        total = o_ref[h * ext + DH : h * ext + DH + 1, :]
        gt = g_ref[:, h * DH : (h + 1) * DH].T.astype(jnp.float32)
        part = jnp.sum(gt * o_ref[h * ext : h * ext + DH, :], axis=0, keepdims=True)
        log_ref[h : h + 1, :] = m_ref[h : h + 1, :] + jnp.log2(total)
        delta_ref[h : h + 1, :] = part / total


def finish(g, m, o):
    heads, chunk = m.shape
    shape = jax.ShapeDtypeStruct((heads, chunk), jnp.float32)
    return pl.pallas_call(
        functools.partial(finish_kernel, heads),
        out_shape=(shape, shape),
        in_specs=[whole()] * 3,
        out_specs=(whole(),) * 2,
        compiler_params=params(),
        cost_estimate=cost(2 * chunk * heads * DH, 6 * chunk * heads * DH),
        name="row_delta",
    )(g, m, o)


def grads_kernel(docs, layers, tile, heads, d, first, team, count, scal, q_ref, g_ref, *refs):
    kv_refs, refs = refs[:count], refs[count:]
    log_ref, delta_ref, refs = refs[0], refs[1], refs[2:]
    if not first:
        dq_in, refs = refs[0], refs[1:]
    if team is None:
        dq_ref, *dkv_refs, kv_ref, kt_ref, acc_ref = refs
    else:
        outs, refs = refs[:team], refs[team:]
        *dkv_refs, kv_ref, kt_ref, acc_ref, dq_ref, full_ref = refs
    chunk = q_ref.shape[0]
    scaling = 1.0 / math.sqrt(DH)
    factor = LOG2E * scaling
    if first:
        dq_ref[...] = jnp.zeros_like(dq_ref)
    else:
        dq_ref[...] = dq_in[...]

    def body(qo, ko, tk, mask):
        rows = pl.ds(qo, tile)
        keys = pl.ds(ko, tk)
        k = kv_ref[keys, :DH]
        v = kv_ref[keys, DH:]
        qs = [q_ref[rows, h * DH : (h + 1) * DH] for h in range(heads)]
        gs = [g_ref[rows, h * DH : (h + 1) * DH] for h in range(heads)]
        scores = [dot(k, q, NT) for q in qs]
        dots = [dot(v, g, NT) for g in gs]
        scores = [jnp.where(mask, s, NEG) for s in scores]
        probs = [
            jnp.exp2(scores[h] * factor - log_ref[h : h + 1, rows]) for h in range(heads)
        ]
        ds = [
            (probs[h] * (dots[h] - delta_ref[h : h + 1, rows])).astype(jnp.bfloat16)
            for h in range(heads)
        ]
        probs = [p.astype(jnp.bfloat16) for p in probs]
        dv = dot(jnp.concatenate(probs, 1), jnp.concatenate(gs, 0), NN)
        dk = dot(jnp.concatenate(ds, 1), jnp.concatenate(qs, 0), NN)
        kt = kt_ref[:, keys]
        news = [dot(kt, x, NN) for x in ds]
        for h in range(heads):
            dq_ref[h * DH : (h + 1) * DH, rows] += news[h]
        acc_ref[keys, :DH] += dk
        acc_ref[keys, DH:] += dv

    def use(i, dist):
        acc_ref[...] = jnp.zeros_like(acc_ref)
        kt_ref[...] = kv_ref[:, :DH].T
        over_tiles(scal, docs, dist, chunk, tile, body)
        for j, ref in enumerate(dkv_refs):

            @pl.when(i == j)
            def _():
                ref[:, :DH] = (acc_ref[:, :DH] * scaling).astype(ref.dtype)
                ref[:, DH:] = acc_ref[:, DH:].astype(ref.dtype)

    each_chunk(chunk_count(scal, docs, chunk, layers, d, count), kv_refs, kv_ref, d, True, use)
    if team is not None:
        for h in range(heads):
            full_ref[:, h * DH : (h + 1) * DH] = (
                (dq_ref[h * DH : (h + 1) * DH, :] * scaling).T.astype(jnp.bfloat16)
            )
        size = chunk // team
        for m in range(team):
            outs[m][...] = full_ref[span(scal[2] ^ m, size), :]


def grads(
    scal, docs, layers, tile, d, q, g, kvs, log_total, delta, dq, team=None, dtypes=(), after=()
):
    chunk, width = q.shape
    heads = width // DH
    first = dq is None
    extra = () if first else (dq,)
    dtypes = dtypes or (jnp.bfloat16,) * len(kvs)
    dkv_shapes = tuple(jax.ShapeDtypeStruct((chunk, 2 * DH), dtype) for dtype in dtypes)
    scratch = [
        pltpu.VMEM((chunk, 2 * DH), jnp.bfloat16),
        pltpu.VMEM((DH, chunk), jnp.bfloat16),
        pltpu.VMEM((chunk, 2 * DH), jnp.float32),
    ]
    if team is None:
        shapes = (jax.ShapeDtypeStruct((width, chunk), jnp.float32),)
    else:
        shapes = (jax.ShapeDtypeStruct((chunk // team, width), jnp.bfloat16),) * team
        scratch += [
            pltpu.VMEM((width, chunk), jnp.float32),
            pltpu.VMEM((chunk, width), jnp.bfloat16),
        ]
    return ordered_call(
        functools.partial(grads_kernel, docs, layers, tile, heads, d, first, team, len(kvs)),
        scal,
        (q, g, *kvs, log_total, delta, *extra),
        after,
        out_shape=shapes + dkv_shapes,
        out_specs=(whole(),) * (len(shapes) + len(kvs)),
        scratch_shapes=scratch,
        cost_estimate=cost(10 * chunk * chunk * width, 12 * chunk * width, chunk * chunk * heads),
        name="pair_grads",
    )


def project(scal, d, w, parts, far, blocks, begin, count, after=()):
    rows, depth = d.shape
    wide = w.shape[0] // blocks
    split = w.shape[1] // depth
    each = 0 if not parts else parts[0].shape[1] // wide

    def kernel(*refs):
        scal, d_ref, w_ref = refs[:3]
        total = dot(d_ref[...], w_ref[...], NT)
        if not parts:
            refs[-2][...] = total
            refs[-1][...] = jnp.zeros_like(refs[-1])
            return
        outs = refs[3 + len(parts) + len(after) :]
        for m in range(count):

            @pl.when(pl.program_id(0) == m)
            def _():
                outs[m][...] = (total + refs[3 + m // each][...]).astype(outs[m].dtype)

    def column(s):
        if split == 1:
            return 0
        return 1 - s[3] if far else s[3]

    def part_spec(p):
        return pl.BlockSpec((rows, wide), lambda i, s: (0, jnp.clip(i - p * each, 0, each - 1)))

    w_spec = pl.BlockSpec((wide, depth), lambda i, s: (s[2] ^ (i + begin), column(s)))
    if parts:
        out_shape = (jax.ShapeDtypeStruct((rows, wide), jnp.bfloat16),) * count
        out_specs = (pl.BlockSpec((rows, wide), lambda i, s: (0, 0)),) * count
    else:
        out_shape = (
            jax.ShapeDtypeStruct((rows, wide * count), jnp.float32),
            jax.ShapeDtypeStruct((8, 128), jnp.float32),
        )
        out_specs = (
            pl.BlockSpec((rows, wide), lambda i, s: (0, i)),
            pl.BlockSpec((8, 128), lambda i, s: (0, 0)),
        )
    grid_spec = pltpu.PrefetchScalarGridSpec(
        num_scalar_prefetch=1,
        grid=(count,),
        in_specs=[pl.BlockSpec((rows, depth), lambda i, s: (0, 0)), w_spec]
        + [part_spec(p) for p in range(len(parts))]
        + [whole(pl.ANY)] * len(after),
        out_specs=out_specs,
    )
    return pl.pallas_call(
        kernel,
        out_shape=out_shape,
        grid_spec=grid_spec,
        compiler_params=params(PROJECT_LIMIT),
        cost_estimate=cost(2 * rows * depth * wide * count, 2 * depth * wide * count),
        name="project",
    )(scal, d, w, *parts, *after)


def copies(scal, inputs, out_shapes, plan, name, after=(), limit=VMEM_LIMIT, space=pl.ANY):
    n_in = len(inputs)

    def kernel(scal, *refs):
        ins, outs, sems = refs[:n_in], refs[n_in:-1], refs[-1]
        started = []
        for i, (a, src, b, dst) in enumerate(plan(scal[2])):
            copy = pltpu.make_async_copy(ins[a].at[src], outs[b].at[dst], sems.at[i])
            copy.start()
            started.append(copy)
        for copy in started:
            copy.wait()

    count = len(plan(0))
    size = sum(math.prod(s.shape) * 2 for s in out_shapes)
    return ordered_call(
        kernel,
        scal,
        inputs,
        after,
        out_shape=tuple(out_shapes),
        in_specs=[whole(pl.ANY)] * n_in,
        out_specs=(whole(space),) * len(out_shapes),
        scratch_shapes=[pltpu.SemaphoreType.DMA((count,))],
        limit=limit,
        cost_estimate=cost(0, 2 * size),
        name=name,
    )


def add(scal, a, b, after):
    def kernel(scal, a_ref, b_ref, out_ref):
        total = a_ref[...].astype(jnp.float32) + b_ref[...].astype(jnp.float32)
        out_ref[...] = total.astype(out_ref.dtype)

    return ordered_call(
        kernel,
        scal,
        (a, b),
        after,
        out_shape=jax.ShapeDtypeStruct(a.shape, a.dtype),
        out_specs=whole(),
        cost_estimate=cost(a.size, 6 * a.size),
        name="add_terms",
    )


def span(start, size):
    if isinstance(start, int):
        return pl.ds(start, size)
    return pl.ds(pl.multiple_of(start * size, size), size)


ALL = slice(None)


def solution(mesh):
    n_seq = mesh.shape["seq"]
    n_head = mesh.shape["head"]

    def shards(queries, keys, values, d_out, w_out, doc_starts):
        rows = queries.shape[0]
        groups = keys.shape[1] // DH
        heads = queries.shape[1] // keys.shape[1]
        width = heads * DH
        docs = doc_starts.shape[0]
        team = groups
        layers = n_seq // team
        chunk = team * rows
        tile = 256 if chunk % 256 == 0 else rows
        me = lax.axis_index("seq")
        layer = me // team
        head = lax.axis_index("head")
        base = layer * chunk
        scal = jnp.concatenate([jnp.stack([base, base, me % team, head]), doc_starts])
        ends = jnp.concatenate([doc_starts[1:], jnp.full((1,), chunk * layers, jnp.int32)])
        far = jnp.any((ends - 1) // chunk - doc_starts // chunk > 2)

        def half(*shape):
            return jax.ShapeDtypeStruct(shape, jnp.bfloat16)

        def swap(m, x):
            return lax.ppermute(x, "seq", [(i, i ^ m) for i in range(n_seq)])

        def swapped(parts):
            got = list(parts)
            for m in reversed(range(1, team)):
                got[m] = swap(m, parts[m])
            return got

        def shift(d, x, first=0):
            pairs = [
                (i, i + d * team)
                for i in range(first * team, n_seq)
                if 0 <= i + d * team < n_seq
            ]
            return lax.ppermute(x, "seq", pairs)

        def pack(groups_of):
            arrays = [x for group in groups_of for x, _ in group]

            def plan(place):
                out = []
                a = b = 0
                for group in groups_of:
                    for m in range(team):
                        at = 0
                        for i, (_, size) in enumerate(group):
                            dst = (ALL, pl.ds(at, size))
                            out.append((a + i, (ALL, span(place ^ m, size)), b, dst))
                            at += size
                        b += 1
                    a += len(group)
                return out

            shapes = [half(rows, sum(n for _, n in group)) for group in groups_of for _ in range(team)]
            outs = copies(scal, arrays, shapes, plan, "pack_columns", (), PACK_LIMIT, pltpu.VMEM)
            return [outs[i : i + team] for i in range(0, len(outs), team)]

        def stack(parts, sizes, name, after=(), also=()):
            def plan(place):
                out = []
                for m in range(team):
                    at = 0
                    for b, size in enumerate(sizes):
                        out.append((m, (ALL, pl.ds(at, size)), b, (span(place ^ m, rows), ALL)))
                        at += size
                for i in range(len(also)):
                    out.append((team + i, (ALL, ALL), len(sizes) + i, (ALL, ALL)))
                return out

            shapes = [half(chunk, size) for size in sizes] + [half(*x.shape) for x in also]
            return copies(scal, list(parts) + list(also), shapes, plan, name, after)

        def beside(parts, sizes, name):
            def plan(place):
                out = []
                for m in range(team):
                    at = 0
                    for b, size in enumerate(sizes):
                        out.append((m, (ALL, pl.ds(at, size)), b, (ALL, span(place ^ m, size))))
                        at += size
                return out

            shapes = [half(rows, team * size) for size in sizes]
            return copies(scal, parts, shapes, plan, name)

        if n_head == 2:
            d_far = lax.ppermute(d_out, "head", [(0, 1), (1, 0)])
        if team > 1:
            kv_sent, q_sent = pack([[(keys, DH), (values, DH)], [(queries, width)]])
            kv_got = swapped(kv_sent)
            q_got = swapped(q_sent)
            near = []
            marks = []
            if n_head == 2:
                part, end = project(scal, d_out, w_out, (), False, team, 0, team, kv_sent[:1])
                near.append(part)
                marks.append(end)
            (kv,) = stack(kv_got, [2 * DH], "stack_keys_values", marks)
            order = (kv,)
        else:
            kv = jnp.concatenate([keys, values], axis=1)
            near = [project(scal, d_out, w_out, (), False, 1, 0, 1)[0]] if n_head == 2 else []
            q = queries
            order = ()
        if n_head == 2:
            g_parts = project(scal, d_far, w_out, near, True, team, 0, team, order)
        else:
            d_all = lax.all_gather(d_out, "head", axis=1, tiled=True)
            zero = jnp.zeros((rows, width * team), jnp.float32)
            g_parts = project(scal, d_all, w_out, [zero], False, team, 0, team, order)
        if team > 1:
            g_got = swapped(g_parts)
            q, kv_again = stack(q_got, [width], "stack_queries", g_parts[:1], (kv,))
        def stack_g(after):
            if team > 1:
                return stack(g_got, [width], "stack_attn_grad", after)[0]
            return g_parts[0]

        if layers <= 4:
            steps = [kv] + [shift(d, kv) for d in range(1, min(layers, 3))]
            if layers == 4:
                steps.append(lax.cond(far, lambda x: shift(3, x), lambda x: x, kv_again))
            state = stats(scal, docs, layers, tile, 0, q, steps[:2], None, g_parts[:1])
            g = stack_g(state[:1])
            if layers > 2:
                state = stats(scal, docs, layers, tile, 2, q, steps[2:], state, (g,))
            log_total, delta = finish(g, *state)
            dq = None
            terms = []
            far_sum = None
            if layers > 2:
                dq, far_sum, *late = grads(
                    scal, docs, layers, tile, 2, q, g, steps[2:], log_total, delta, dq
                )
                far_sum = shift(-1, far_sum, 2)
                if late:
                    terms = [lax.cond(far, lambda x: shift(-3, x), lambda x: x, late[0])]
            dq, near_sum = grads(
                scal, docs, layers, tile, 1, q, g, steps[1:2], log_total, delta, dq
            )
            if far_sum is not None:
                near_sum = add(scal, near_sum, far_sum, ())
            terms = [shift(-1, near_sum, 1)] + terms
            *dq_parts, dkv = grads(
                scal,
                docs,
                layers,
                tile,
                0,
                q,
                g,
                [kv],
                log_total,
                delta,
                dq,
                team,
                (jnp.float32,),
                (near_sum,),
            )
        else:
            rings = [[z * team + a for z in range(layers)] for a in range(team)]
            every = lax.all_gather(kv, "seq", axis_index_groups=rings)

            def chunk_at(d):
                return lax.dynamic_index_in_dim(every, jnp.maximum(layer - d, 0), 0, keepdims=False)

            def scalars(d):
                return scal - jnp.where(jnp.arange(scal.shape[0]) == 1, d * chunk, 0)

            def one(d, state):
                return tuple(stats(scalars(d), docs, layers, tile, 0, q, [chunk_at(d)], state))

            state = stats(scal, docs, layers, tile, 0, q, [kv], None)
            state = lax.fori_loop(1, layers, one, tuple(state))
            g = stack_g(())
            log_total, delta = finish(g, *state)

            def two(d, carry):
                dq, total = carry
                dq, dkv = grads(
                    scalars(d), docs, layers, tile, 0, q, g, [chunk_at(d)], log_total, delta, dq
                )
                place = jnp.maximum(layer - d, 0)
                old = lax.dynamic_index_in_dim(total, place, 0, keepdims=False)
                total = lax.dynamic_update_index_in_dim(
                    total, jnp.where(layer >= d, dkv, old), place, 0
                )
                return dq, total

            dq = jnp.zeros((width, chunk), jnp.float32)
            total = jnp.zeros((layers, chunk, 2 * DH), jnp.bfloat16)
            dq, total = lax.fori_loop(1, layers, two, (dq, total))
            *dq_parts, dkv = grads(
                scal, docs, layers, tile, 0, q, g, [kv], log_total, delta, dq, team, (jnp.float32,)
            )
            terms = [
                lax.psum_scatter(
                    total.reshape(layers * chunk, 2 * DH), "seq", axis_index_groups=rings, tiled=True
                )
            ]

        def sum_kernel(scal, *refs):
            total = refs[0][...]
            starts = [scal[FIRST_DOC + n] for n in range(docs)]
            many = reaches_far(starts, docs, chunk, chunk * layers) > 0
            for i, x in enumerate(refs[1 : 1 + len(terms)]):
                term = x[...].astype(jnp.float32)
                total = total + (term if i == 0 else jnp.where(many, term, 0.0))
            full = refs[-1]
            full[...] = total.astype(jnp.bfloat16)
            for m in range(team):
                refs[1 + len(terms) + m][...] = full[span(scal[2] ^ m, rows), :]

        dkv_parts = pl.pallas_call(
            sum_kernel,
            out_shape=(half(rows, 2 * DH),) * team,
            in_specs=[whole(pltpu.SMEM)] + [whole()] * (1 + len(terms)),
            out_specs=(whole(),) * team,
            scratch_shapes=[pltpu.VMEM((chunk, 2 * DH), jnp.bfloat16)],
            compiler_params=params(),
            name="sum_terms",
        )(scal, dkv, *terms)
        if team > 1:
            dq_parts = swapped(dq_parts)
            dkv_parts = swapped(dkv_parts)
            (query_grad,) = beside(dq_parts, [width], "place_query_grad")
            key_grad, value_grad = beside(dkv_parts, [DH, DH], "place_key_value_grad")
        else:
            query_grad = dq_parts[0]
            key_grad = dkv_parts[0][:, :DH]
            value_grad = dkv_parts[0][:, DH:]
        return (query_grad, key_grad, value_grad)

    return jax.shard_map(
        shards,
        mesh=mesh,
        in_specs=(
            P("seq", "head"),
            P("seq", "head"),
            P("seq", "head"),
            P("seq", "head"),
            P("head", None),
            P(),
        ),
        out_specs=(P("seq", "head"), P("seq", "head"), P("seq", "head")),
        check_vma=False,
    )
```

```python
import functools
import math

import jax
import jax.numpy as jnp
from jax import lax
from jax.experimental import pallas as pl
from jax.experimental.pallas import tpu as pltpu
from jax.sharding import PartitionSpec as P

DH = 128
ONES = 16
LOG2E = 1.4426950408889634
NEG = -1e30
VMEM_LIMIT = 28 * 1024 * 1024
PACK_LIMIT = 54016 * 1024
PROJECT_LIMIT = 40 * 1024 * 1024
FAR_LIMIT = 42 * 1024 * 1024

NT = (((1,), (1,)), ((), ()))
NN = (((1,), (0,)), ((), ()))


def dot(a, b, dims):
    return lax.dot_general(a, b, dims, preferred_element_type=jnp.float32)


def params(limit=VMEM_LIMIT):
    return pltpu.CompilerParams(vmem_limit_bytes=limit)


def whole(memory_space=pltpu.VMEM):
    return pl.BlockSpec(memory_space=memory_space)


def ordered_call(kernel, scal, operands, after, **kwargs):
    count = len(after)

    def body(*refs):
        kernel(*refs[: 1 + len(operands)], *refs[1 + len(operands) + count :])

    specs = kwargs.pop("in_specs", [whole()] * len(operands))
    limit = kwargs.pop("limit", VMEM_LIMIT)
    return pl.pallas_call(
        body,
        in_specs=[whole(pltpu.SMEM)] + specs + [whole(pl.ANY)] * count,
        compiler_params=params(limit),
        **kwargs,
    )(scal, *operands, *after)


def cost(flops, nbytes, exps=0):
    return pl.CostEstimate(flops=1024, bytes_accessed=1024, transcendentals=0)


FIRST_DOC = 4


def row_starts(scal, docs, pos):
    low = jnp.zeros_like(pos)
    for n in range(docs):
        low = jnp.where(pos >= scal[FIRST_DOC + n], scal[FIRST_DOC + n], low)
    return low


def reaches_far(starts, docs, chunk, total):
    far = jnp.int32(0)
    for n in range(docs):
        end = (starts[n + 1] if n + 1 < docs else total) - 1
        far = jnp.where(end // chunk - starts[n] // chunk > 2, 1, far)
    return far


def doc_start_at(scal, docs, pos):
    low = jnp.int32(0)
    for n in range(docs):
        low = jnp.where(pos >= scal[FIRST_DOC + n], scal[FIRST_DOC + n], low)
    return low


def allowed(scal, docs, q0, k0, tq, tk):
    qpos = q0 + lax.broadcasted_iota(jnp.int32, (1, tq), 1)
    kpos = k0 + lax.broadcasted_iota(jnp.int32, (tk, 1), 0)
    return (kpos <= qpos) & (kpos >= row_starts(scal, docs, qpos))


def over_tiles(scal, docs, d, chunk, tile, body):
    tiles = chunk // tile

    def one(qo, ko, q0, tk, need):
        k0 = scal[1] - d * chunk + ko
        @pl.when(need)
        def _():
            body(qo, ko, tk, allowed(scal, docs, q0, k0, tile, tk))

    def step(qt, _):
        qo = pl.multiple_of(qt * tile, tile)
        q0 = scal[0] + qo
        low = doc_start_at(scal, docs, q0)
        k0 = scal[1] - d * chunk
        if tiles == 1:
            one(qo, 0, q0, tile, (k0 <= q0 + tile - 1) & (k0 + tile - 1 >= low))
            return 0
        all_of = (k0 + chunk - tile <= q0 + tile - 1) & (k0 + tile - 1 >= low)
        one(qo, 0, q0, chunk, all_of)

        @pl.when(jnp.logical_not(all_of))
        def _():
            def inner(kt, _):
                ko = pl.multiple_of(kt * tile, tile)
                need = (k0 + ko <= q0 + tile - 1) & (k0 + ko + tile - 1 >= low)
                one(qo, ko, q0, tile, need)
                return 0

            lax.fori_loop(0, tiles, inner, 0)

        return 0

    lax.fori_loop(0, tiles, step, 0)


def each_chunk(total, kv_refs, now_ref, d, down, use):
    count = len(kv_refs)
    if count == 1:
        now_ref[...] = kv_refs[0][...]
        use(0, d)
        return

    def one(i, _):
        for j, ref in enumerate(kv_refs):

            @pl.when(i == j)
            def _():
                now_ref[...] = ref[...]

        use(i, d + i)
        return 0

    if down:
        lax.fori_loop(0, total, lambda i, c: one(total - 1 - i, c), 0)
    else:
        lax.fori_loop(0, total, one, 0)


def chunk_count(scal, docs, chunk, layers, d, count):
    always = min(count, max(1, 3 - d))
    if always == count:
        return count
    far = reaches_far([scal[FIRST_DOC + n] for n in range(docs)], docs, chunk, chunk * layers)
    return always + (count - always) * far


def stats_kernel(docs, layers, tile, heads, d, first, count, scal, q_ref, *refs):
    kv_refs, refs = refs[:count], refs[count:]
    if first:
        m_ref, o_ref, kv_ref, vt_ref = refs
        m_ref[...] = jnp.full_like(m_ref, NEG)
        o_ref[...] = jnp.zeros_like(o_ref)
    else:
        m_in, o_in, m_ref, o_ref, kv_ref, vt_ref = refs
        m_ref[...] = m_in[...]
        o_ref[...] = o_in[...]
    chunk = q_ref.shape[0]
    factor = LOG2E / math.sqrt(DH)
    ext = DH + ONES
    vt_ref[DH:] = jnp.ones((vt_ref.shape[0] - DH, chunk), jnp.bfloat16)

    def body(qo, ko, tk, mask):
        k = kv_ref[pl.ds(ko, tk), :DH]
        vt = vt_ref[:ext, pl.ds(ko, tk)]
        rows = pl.ds(qo, tile)
        scores = [dot(k, q_ref[rows, h * DH : (h + 1) * DH], NT) for h in range(heads)]
        scores = [jnp.where(mask, s, NEG) for s in scores]
        m_old = [m_ref[h : h + 1, rows] for h in range(heads)]
        m_new = [
            jnp.maximum(m, factor * jnp.max(s, axis=0, keepdims=True))
            for m, s in zip(m_old, scores)
        ]
        alpha = [jnp.exp2(a - b) for a, b in zip(m_old, m_new)]
        probs = [jnp.exp2(s * factor - m).astype(jnp.bfloat16) for s, m in zip(scores, m_new)]
        news = [dot(vt, p, NN) for p in probs]
        for h in range(heads):
            part = slice(h * ext, (h + 1) * ext)
            m_ref[h : h + 1, rows] = m_new[h]
            o_ref[part, rows] = alpha[h] * o_ref[part, rows] + news[h]

    def use(i, dist):
        vt_ref[:DH] = kv_ref[:, DH:].T
        over_tiles(scal, docs, dist, chunk, tile, body)

    each_chunk(chunk_count(scal, docs, chunk, layers, d, count), kv_refs, kv_ref, d, False, use)


def stats(scal, docs, layers, tile, d, q, kvs, state, after=()):
    chunk, width = q.shape
    heads = width // DH
    shapes = (
        jax.ShapeDtypeStruct((heads, chunk), jnp.float32),
        jax.ShapeDtypeStruct((heads * (DH + ONES), chunk), jnp.float32),
    )
    first = state is None
    extra = () if first else state
    return ordered_call(
        functools.partial(stats_kernel, docs, layers, tile, heads, d, first, len(kvs)),
        scal,
        (q, *kvs, *extra),
        after,
        out_shape=shapes,
        out_specs=(whole(),) * 2,
        scratch_shapes=[
            pltpu.VMEM((chunk, 2 * DH), jnp.bfloat16),
            pltpu.VMEM((DH + ONES, chunk), jnp.bfloat16),
        ],
        cost_estimate=cost(4 * chunk * chunk * width, 12 * chunk * width, chunk * chunk * heads),
        name="row_stats",
    )


def finish_kernel(heads, g_ref, m_ref, o_ref, log_ref, delta_ref):
    ext = DH + ONES
    for h in range(heads):
        total = o_ref[h * ext + DH : h * ext + DH + 1, :]
        gt = g_ref[:, h * DH : (h + 1) * DH].T.astype(jnp.float32)
        part = jnp.sum(gt * o_ref[h * ext : h * ext + DH, :], axis=0, keepdims=True)
        log_ref[h : h + 1, :] = m_ref[h : h + 1, :] + jnp.log2(total)
        delta_ref[h : h + 1, :] = part / total


def finish(g, m, o):
    heads, chunk = m.shape
    shape = jax.ShapeDtypeStruct((heads, chunk), jnp.float32)
    return pl.pallas_call(
        functools.partial(finish_kernel, heads),
        out_shape=(shape, shape),
        in_specs=[whole()] * 3,
        out_specs=(whole(),) * 2,
        compiler_params=params(),
        cost_estimate=cost(2 * chunk * heads * DH, 6 * chunk * heads * DH),
        name="row_delta",
    )(g, m, o)


def grads_kernel(docs, layers, tile, heads, d, first, team, count, scal, q_ref, g_ref, *refs):
    kv_refs, refs = refs[:count], refs[count:]
    log_ref, delta_ref, refs = refs[0], refs[1], refs[2:]
    if not first:
        dq_in, refs = refs[0], refs[1:]
    if team is None:
        dq_ref, *dkv_refs, kv_ref, kt_ref, acc_ref = refs
    else:
        outs, refs = refs[:team], refs[team:]
        *dkv_refs, kv_ref, kt_ref, acc_ref, dq_ref, full_ref = refs
    chunk = q_ref.shape[0]
    scaling = 1.0 / math.sqrt(DH)
    factor = LOG2E * scaling
    if first:
        dq_ref[...] = jnp.zeros_like(dq_ref)
    else:
        dq_ref[...] = dq_in[...]

    def body(qo, ko, tk, mask):
        rows = pl.ds(qo, tile)
        keys = pl.ds(ko, tk)
        k = kv_ref[keys, :DH]
        v = kv_ref[keys, DH:]
        qs = [q_ref[rows, h * DH : (h + 1) * DH] for h in range(heads)]
        gs = [g_ref[rows, h * DH : (h + 1) * DH] for h in range(heads)]
        scores = [dot(k, q, NT) for q in qs]
        dots = [dot(v, g, NT) for g in gs]
        scores = [jnp.where(mask, s, NEG) for s in scores]
        probs = [
            jnp.exp2(scores[h] * factor - log_ref[h : h + 1, rows]) for h in range(heads)
        ]
        ds = [
            (probs[h] * (dots[h] - delta_ref[h : h + 1, rows])).astype(jnp.bfloat16)
            for h in range(heads)
        ]
        probs = [p.astype(jnp.bfloat16) for p in probs]
        dv = dot(jnp.concatenate(probs, 1), jnp.concatenate(gs, 0), NN)
        dk = dot(jnp.concatenate(ds, 1), jnp.concatenate(qs, 0), NN)
        kt = kt_ref[:, keys]
        news = [dot(kt, x, NN) for x in ds]
        for h in range(heads):
            dq_ref[h * DH : (h + 1) * DH, rows] += news[h]
        acc_ref[keys, :DH] += dk
        acc_ref[keys, DH:] += dv

    def use(i, dist):
        acc_ref[...] = jnp.zeros_like(acc_ref)
        kt_ref[...] = kv_ref[:, :DH].T
        over_tiles(scal, docs, dist, chunk, tile, body)
        for j, ref in enumerate(dkv_refs):

            @pl.when(i == j)
            def _():
                ref[:, :DH] = (acc_ref[:, :DH] * scaling).astype(ref.dtype)
                ref[:, DH:] = acc_ref[:, DH:].astype(ref.dtype)

    each_chunk(chunk_count(scal, docs, chunk, layers, d, count), kv_refs, kv_ref, d, True, use)
    if team is not None:
        for h in range(heads):
            full_ref[:, h * DH : (h + 1) * DH] = (
                (dq_ref[h * DH : (h + 1) * DH, :] * scaling).T.astype(jnp.bfloat16)
            )
        size = chunk // team
        for m in range(team):
            outs[m][...] = full_ref[span(scal[2] ^ m, size), :]


def grads(
    scal, docs, layers, tile, d, q, g, kvs, log_total, delta, dq, team=None, dtypes=(), after=()
):
    chunk, width = q.shape
    heads = width // DH
    first = dq is None
    extra = () if first else (dq,)
    dtypes = dtypes or (jnp.bfloat16,) * len(kvs)
    dkv_shapes = tuple(jax.ShapeDtypeStruct((chunk, 2 * DH), dtype) for dtype in dtypes)
    scratch = [
        pltpu.VMEM((chunk, 2 * DH), jnp.bfloat16),
        pltpu.VMEM((DH, chunk), jnp.bfloat16),
        pltpu.VMEM((chunk, 2 * DH), jnp.float32),
    ]
    if team is None:
        shapes = (jax.ShapeDtypeStruct((width, chunk), jnp.float32),)
    else:
        shapes = (jax.ShapeDtypeStruct((chunk // team, width), jnp.bfloat16),) * team
        scratch += [
            pltpu.VMEM((width, chunk), jnp.float32),
            pltpu.VMEM((chunk, width), jnp.bfloat16),
        ]
    return ordered_call(
        functools.partial(grads_kernel, docs, layers, tile, heads, d, first, team, len(kvs)),
        scal,
        (q, g, *kvs, log_total, delta, *extra),
        after,
        out_shape=shapes + dkv_shapes,
        out_specs=(whole(),) * (len(shapes) + len(kvs)),
        scratch_shapes=scratch,
        cost_estimate=cost(10 * chunk * chunk * width, 12 * chunk * width, chunk * chunk * heads),
        name="pair_grads",
    )


def project(scal, d, w, parts, far, blocks, begin, count, after=()):
    rows, depth = d.shape
    wide = w.shape[0] // blocks
    split = w.shape[1] // depth
    each = 0 if not parts else parts[0].shape[1] // wide

    def kernel(*refs):
        scal, d_ref, w_ref = refs[:3]
        total = dot(d_ref[...], w_ref[...], NT)
        if not parts:
            refs[-2][...] = total
            refs[-1][...] = jnp.zeros_like(refs[-1])
            return
        outs = refs[3 + len(parts) + len(after) :]
        for m in range(count):

            @pl.when(pl.program_id(0) == m)
            def _():
                outs[m][...] = (total + refs[3 + m // each][...]).astype(outs[m].dtype)

    def column(s):
        if split == 1:
            return 0
        return 1 - s[3] if far else s[3]

    def part_spec(p):
        return pl.BlockSpec((rows, wide), lambda i, s: (0, jnp.clip(i - p * each, 0, each - 1)))

    w_spec = pl.BlockSpec((wide, depth), lambda i, s: (s[2] ^ (i + begin), column(s)))
    if parts:
        out_shape = (jax.ShapeDtypeStruct((rows, wide), jnp.bfloat16),) * count
        out_specs = (pl.BlockSpec((rows, wide), lambda i, s: (0, 0)),) * count
    else:
        out_shape = (
            jax.ShapeDtypeStruct((rows, wide * count), jnp.float32),
            jax.ShapeDtypeStruct((8, 128), jnp.float32),
        )
        out_specs = (
            pl.BlockSpec((rows, wide), lambda i, s: (0, i)),
            pl.BlockSpec((8, 128), lambda i, s: (0, 0)),
        )
    grid_spec = pltpu.PrefetchScalarGridSpec(
        num_scalar_prefetch=1,
        grid=(count,),
        in_specs=[pl.BlockSpec((rows, depth), lambda i, s: (0, 0)), w_spec]
        + [part_spec(p) for p in range(len(parts))]
        + [whole(pl.ANY)] * len(after),
        out_specs=out_specs,
    )
    return pl.pallas_call(
        kernel,
        out_shape=out_shape,
        grid_spec=grid_spec,
        compiler_params=params(PROJECT_LIMIT),
        cost_estimate=cost(2 * rows * depth * wide * count, 2 * depth * wide * count),
        name="project",
    )(scal, d, w, *parts, *after)


def project_near(scal, d, w, blocks, after):
    rows, depth = d.shape
    wide = w.shape[0] // blocks

    def kernel(*refs):
        scal, d_ref, w_ref, all_ref = refs[:4]
        out_ref, far_ref, sem = refs[4 + len(after) :]
        columns = span(1 - scal[3], depth)
        copy = pltpu.make_async_copy(all_ref.at[:, columns], far_ref, sem)
        pl.when(pl.program_id(0) == 0)(copy.start)
        out_ref[...] = dot(d_ref[...], w_ref[...], NT)
        pl.when(pl.program_id(0) == blocks - 1)(copy.wait)

    grid_spec = pltpu.PrefetchScalarGridSpec(
        num_scalar_prefetch=1,
        grid=(blocks,),
        in_specs=[
            pl.BlockSpec((rows, depth), lambda i, s: (0, 0)),
            pl.BlockSpec((wide, depth), lambda i, s: (s[2] ^ i, s[3])),
            whole(pl.ANY),
        ]
        + [whole(pl.ANY)] * len(after),
        out_specs=(pl.BlockSpec((rows, wide), lambda i, s: (0, i)), whole()),
        scratch_shapes=[pltpu.SemaphoreType.DMA],
    )
    return pl.pallas_call(
        kernel,
        out_shape=(
            jax.ShapeDtypeStruct((rows, wide * blocks), jnp.float32),
            jax.ShapeDtypeStruct((w.shape[0], depth), w.dtype),
        ),
        grid_spec=grid_spec,
        compiler_params=params(PROJECT_LIMIT),
        cost_estimate=cost(2 * rows * depth * wide * blocks, 4 * depth * wide * blocks),
        name="project_near",
    )(scal, d, w, w, *after)


def project_far(scal, d, w_far, part, blocks, after):
    rows = d.shape[0]
    wide = w_far.shape[0] // blocks

    def kernel(scal, d_ref, w_ref, part_ref, *outs):
        for m in range(blocks):
            total = dot(d_ref[...], w_ref[span(scal[2] ^ m, wide), :], NT)
            outs[m][...] = (total + part_ref[:, m * wide : (m + 1) * wide]).astype(jnp.bfloat16)

    return ordered_call(
        kernel,
        scal,
        (d, w_far, part),
        after,
        out_shape=(jax.ShapeDtypeStruct((rows, wide), jnp.bfloat16),) * blocks,
        out_specs=(whole(),) * blocks,
        limit=FAR_LIMIT,
        cost_estimate=cost(2 * rows * w_far.size, 2 * w_far.size),
        name="project_far",
    )


def copies(scal, inputs, out_shapes, plan, name, after=(), limit=VMEM_LIMIT, space=pl.ANY):
    n_in = len(inputs)

    def kernel(scal, *refs):
        ins, outs, sems = refs[:n_in], refs[n_in:-1], refs[-1]
        started = []
        for i, (a, src, b, dst) in enumerate(plan(scal[2])):
            copy = pltpu.make_async_copy(ins[a].at[src], outs[b].at[dst], sems.at[i])
            copy.start()
            started.append(copy)
        for copy in started:
            copy.wait()

    count = len(plan(0))
    size = sum(math.prod(s.shape) * 2 for s in out_shapes)
    return ordered_call(
        kernel,
        scal,
        inputs,
        after,
        out_shape=tuple(out_shapes),
        in_specs=[whole(pl.ANY)] * n_in,
        out_specs=(whole(space),) * len(out_shapes),
        scratch_shapes=[pltpu.SemaphoreType.DMA((count,))],
        limit=limit,
        cost_estimate=cost(0, 2 * size),
        name=name,
    )


def add(scal, a, b, after):
    def kernel(scal, a_ref, b_ref, out_ref):
        total = a_ref[...].astype(jnp.float32) + b_ref[...].astype(jnp.float32)
        out_ref[...] = total.astype(out_ref.dtype)

    return ordered_call(
        kernel,
        scal,
        (a, b),
        after,
        out_shape=jax.ShapeDtypeStruct(a.shape, a.dtype),
        out_specs=whole(),
        cost_estimate=cost(a.size, 6 * a.size),
        name="add_terms",
    )


def span(start, size):
    if isinstance(start, int):
        return pl.ds(start, size)
    return pl.ds(pl.multiple_of(start * size, size), size)


ALL = slice(None)


def solution(mesh):
    n_seq = mesh.shape["seq"]
    n_head = mesh.shape["head"]

    def shards(queries, keys, values, d_out, w_out, doc_starts):
        rows = queries.shape[0]
        groups = keys.shape[1] // DH
        heads = queries.shape[1] // keys.shape[1]
        width = heads * DH
        docs = doc_starts.shape[0]
        team = groups
        layers = n_seq // team
        chunk = team * rows
        tile = 256 if chunk % 256 == 0 else rows
        me = lax.axis_index("seq")
        layer = me // team
        head = lax.axis_index("head")
        base = layer * chunk
        scal = jnp.concatenate([jnp.stack([base, base, me % team, head]), doc_starts])
        ends = jnp.concatenate([doc_starts[1:], jnp.full((1,), chunk * layers, jnp.int32)])
        far = jnp.any((ends - 1) // chunk - doc_starts // chunk > 2)

        def half(*shape):
            return jax.ShapeDtypeStruct(shape, jnp.bfloat16)

        def swap(m, x):
            return lax.ppermute(x, "seq", [(i, i ^ m) for i in range(n_seq)])

        def swapped(parts):
            got = list(parts)
            for m in reversed(range(1, team)):
                got[m] = swap(m, parts[m])
            return got

        def shift(d, x, first=0):
            pairs = [
                (i, i + d * team)
                for i in range(first * team, n_seq)
                if 0 <= i + d * team < n_seq
            ]
            return lax.ppermute(x, "seq", pairs)

        def pack(groups_of):
            arrays = [x for group in groups_of for x, _ in group]

            def plan(place):
                out = []
                a = b = 0
                for group in groups_of:
                    for m in range(team):
                        at = 0
                        for i, (_, size) in enumerate(group):
                            dst = (ALL, pl.ds(at, size))
                            out.append((a + i, (ALL, span(place ^ m, size)), b, dst))
                            at += size
                        b += 1
                    a += len(group)
                return out

            shapes = [half(rows, sum(n for _, n in group)) for group in groups_of for _ in range(team)]
            outs = copies(scal, arrays, shapes, plan, "pack_columns", (), PACK_LIMIT, pltpu.VMEM)
            return [outs[i : i + team] for i in range(0, len(outs), team)]

        def stack(parts, sizes, name, after=(), also=()):
            def plan(place):
                out = []
                for m in range(team):
                    at = 0
                    for b, size in enumerate(sizes):
                        out.append((m, (ALL, pl.ds(at, size)), b, (span(place ^ m, rows), ALL)))
                        at += size
                for i in range(len(also)):
                    out.append((team + i, (ALL, ALL), len(sizes) + i, (ALL, ALL)))
                return out

            shapes = [half(chunk, size) for size in sizes] + [half(*x.shape) for x in also]
            return copies(scal, list(parts) + list(also), shapes, plan, name, after)

        def beside(parts, sizes, name):
            def plan(place):
                out = []
                for m in range(team):
                    at = 0
                    for b, size in enumerate(sizes):
                        out.append((m, (ALL, pl.ds(at, size)), b, (ALL, span(place ^ m, size))))
                        at += size
                return out

            shapes = [half(rows, team * size) for size in sizes]
            return copies(scal, parts, shapes, plan, name)

        if n_head == 2:
            d_far = lax.ppermute(d_out, "head", [(0, 1), (1, 0)])
        if team > 1:
            kv_sent, q_sent = pack([[(keys, DH), (values, DH)], [(queries, width)]])
            kv_got = swapped(kv_sent)
            q_got = swapped(q_sent)
            near = []
            marks = []
            if n_head == 2:
                part, w_far = project_near(scal, d_out, w_out, team, kv_sent[:1])
                marks.append(w_far)
            (kv,) = stack(kv_got, [2 * DH], "stack_keys_values", marks)
            order = (kv,)
        else:
            kv = jnp.concatenate([keys, values], axis=1)
            near = [project(scal, d_out, w_out, (), False, 1, 0, 1)[0]] if n_head == 2 else []
            q = queries
            order = ()
        if n_head == 2 and team > 1:
            g_parts = project_far(scal, d_far, w_far, part, team, order)
        elif n_head == 2:
            g_parts = project(scal, d_far, w_out, near, True, team, 0, team, order)
        else:
            d_all = lax.all_gather(d_out, "head", axis=1, tiled=True)
            zero = jnp.zeros((rows, width * team), jnp.float32)
            g_parts = project(scal, d_all, w_out, [zero], False, team, 0, team, order)
        if team > 1:
            g_got = swapped(g_parts)
            q, kv_again = stack(q_got, [width], "stack_queries", g_parts[:1], (kv,))
        def stack_g(after):
            if team > 1:
                return stack(g_got, [width], "stack_attn_grad", after)[0]
            return g_parts[0]

        if layers <= 4:
            steps = [kv] + [shift(d, kv) for d in range(1, min(layers, 3))]
            if layers == 4:
                steps.append(lax.cond(far, lambda x: shift(3, x), lambda x: x, kv_again))
            state = stats(scal, docs, layers, tile, 0, q, steps[:2], None, g_parts[:1])
            g = stack_g(state[:1])
            if layers > 2:
                state = stats(scal, docs, layers, tile, 2, q, steps[2:], state, (g,))
            log_total, delta = finish(g, *state)
            dq = None
            terms = []
            far_sum = None
            if layers > 2:
                dq, far_sum, *late = grads(
                    scal, docs, layers, tile, 2, q, g, steps[2:], log_total, delta, dq
                )
                far_sum = shift(-1, far_sum, 2)
                if late:
                    terms = [lax.cond(far, lambda x: shift(-3, x), lambda x: x, late[0])]
            dq, near_sum = grads(
                scal, docs, layers, tile, 1, q, g, steps[1:2], log_total, delta, dq
            )
            if far_sum is not None:
                near_sum = add(scal, near_sum, far_sum, ())
            terms = [shift(-1, near_sum, 1)] + terms
            *dq_parts, dkv = grads(
                scal,
                docs,
                layers,
                tile,
                0,
                q,
                g,
                [kv],
                log_total,
                delta,
                dq,
                team,
                (jnp.float32,),
                (near_sum,),
            )
        else:
            rings = [[z * team + a for z in range(layers)] for a in range(team)]
            every = lax.all_gather(kv, "seq", axis_index_groups=rings)

            def chunk_at(d):
                return lax.dynamic_index_in_dim(every, jnp.maximum(layer - d, 0), 0, keepdims=False)

            def scalars(d):
                return scal - jnp.where(jnp.arange(scal.shape[0]) == 1, d * chunk, 0)

            def one(d, state):
                return tuple(stats(scalars(d), docs, layers, tile, 0, q, [chunk_at(d)], state))

            state = stats(scal, docs, layers, tile, 0, q, [kv], None)
            state = lax.fori_loop(1, layers, one, tuple(state))
            g = stack_g(())
            log_total, delta = finish(g, *state)

            def two(d, carry):
                dq, total = carry
                dq, dkv = grads(
                    scalars(d), docs, layers, tile, 0, q, g, [chunk_at(d)], log_total, delta, dq
                )
                place = jnp.maximum(layer - d, 0)
                old = lax.dynamic_index_in_dim(total, place, 0, keepdims=False)
                total = lax.dynamic_update_index_in_dim(
                    total, jnp.where(layer >= d, dkv, old), place, 0
                )
                return dq, total

            dq = jnp.zeros((width, chunk), jnp.float32)
            total = jnp.zeros((layers, chunk, 2 * DH), jnp.bfloat16)
            dq, total = lax.fori_loop(1, layers, two, (dq, total))
            *dq_parts, dkv = grads(
                scal, docs, layers, tile, 0, q, g, [kv], log_total, delta, dq, team, (jnp.float32,)
            )
            terms = [
                lax.psum_scatter(
                    total.reshape(layers * chunk, 2 * DH), "seq", axis_index_groups=rings, tiled=True
                )
            ]

        def sum_kernel(scal, *refs):
            total = refs[0][...]
            starts = [scal[FIRST_DOC + n] for n in range(docs)]
            many = reaches_far(starts, docs, chunk, chunk * layers) > 0
            for i, x in enumerate(refs[1 : 1 + len(terms)]):
                term = x[...].astype(jnp.float32)
                total = total + (term if i == 0 else jnp.where(many, term, 0.0))
            full = refs[-1]
            full[...] = total.astype(jnp.bfloat16)
            for m in range(team):
                refs[1 + len(terms) + m][...] = full[span(scal[2] ^ m, rows), :]

        dkv_parts = pl.pallas_call(
            sum_kernel,
            out_shape=(half(rows, 2 * DH),) * team,
            in_specs=[whole(pltpu.SMEM)] + [whole()] * (1 + len(terms)),
            out_specs=(whole(),) * team,
            scratch_shapes=[pltpu.VMEM((chunk, 2 * DH), jnp.bfloat16)],
            compiler_params=params(),
            name="sum_terms",
        )(scal, dkv, *terms)
        if team > 1:
            dq_parts = swapped(dq_parts)
            dkv_parts = swapped(dkv_parts)
            (query_grad,) = beside(dq_parts, [width], "place_query_grad")
            key_grad, value_grad = beside(dkv_parts, [DH, DH], "place_key_value_grad")
        else:
            query_grad = dq_parts[0]
            key_grad = dkv_parts[0][:, :DH]
            value_grad = dkv_parts[0][:, DH:]
        return (query_grad, key_grad, value_grad)

    return jax.shard_map(
        shards,
        mesh=mesh,
        in_specs=(
            P("seq", "head"),
            P("seq", "head"),
            P("seq", "head"),
            P("seq", "head"),
            P("head", None),
            P(),
        ),
        out_specs=(P("seq", "head"), P("seq", "head"), P("seq", "head")),
        check_vma=False,
    )
```
